256 devices in a mesh: dp: 4 (over z_lo), ctx: 64 (over z_hi, x, y, core).
Axes of the slice: x: 4, y: 4, z: 8 (z_hi: 2, z_lo: 4; z = z_hi * 4 + z_lo), core: 2. Of those that a mesh axis runs over, the one named last changes fastest.
Arguments:
- query_rows: bfloat16 [4, 8192, 2048], P('dp', 'ctx'), may hold values from -6 to 6
- key_rows: bfloat16 [4, 8192, 512], P('dp', 'ctx'), may hold values from -6 to 6
- value_head_rows: bfloat16 [4, 8192, 512], P('dp', 'ctx'), may hold values from -6 to 6
- grad_output: bfloat16 [4, 8192, 2048], P('dp', 'ctx'), may hold values from -6 to 6
- layer_inputs: bfloat16 [4, 8192, 4096], P('dp', 'ctx'), may hold values from -16 to 16
- stretch_order: int32 [4, 64, 2], P('dp'), may hold values from 0 to 1, each once within a row
- session_starts: int32 [4, 64], P('dp'), may hold values from 0 to 8192, as said below
Outputs:
- grad_query: bfloat16 [4, 8192, 2048], P('dp', 'ctx')
- grad_key: bfloat16 [4, 8192, 512], P('dp', 'ctx')
- grad_value: bfloat16 [4, 8192, 512], P('dp', 'ctx')
- grad_value_weight: float32 [4096, 512], P(('dp', 'ctx'))
The draws below stay inside these ranges and needn't reach their ends.
Inputs may be any that keep to these rules, and one draw needn't show every extreme that they name: `session_starts`: in each pack the first start is 0 and starts rise; of the starts below 8192, consecutive ones differ by at least 128 and at most 384; one session that begins inside the pack has exactly 384 positions, and none has more; the last entry, and any entry that would lie past the pack's end, equals 8192 and marks an unused start.
All inputs are finite; a program needn't handle non-finite values.
Results may differ from the reference program's by a relative error of at most 0.013.
Values may be sent and summed in bfloat16 or wider, within the bound.
No kernel may reach another device: no remote copies, remote signals or barrier semaphores. Data moves between devices by JAX's collectives and lax.ppermute only.
A program may use at most 128 MiB of HBM per device.

```python
import jax
import jax.numpy as jnp
from jax import lax

MODEL_WIDTH = 4096
QUERY_HEADS = 16
KEY_VALUE_HEADS = 4
HEAD_SIZE = 128
TOK_DEV = 128
STRETCH = 64
SPAN = 4
QUERY_PER_KEY = 4
STRETCHES_DEV = 2
SESS_MOST = 384
NSTART = 64
PACK_TOKENS = 8192
PACK_COUNT = 4
N_CTX = 64


def draw_query_rows(key, part):
    key = jax.random.fold_in(key, 11)
    return jnp.clip(jax.random.normal(key, (PACK_COUNT, PACK_TOKENS, QUERY_HEADS * HEAD_SIZE), jnp.float32), -6.0, 6.0).astype(jnp.bfloat16)


def draw_key_rows(key, part):
    key = jax.random.fold_in(key, 13)
    return jnp.clip(jax.random.normal(key, (PACK_COUNT, PACK_TOKENS, KEY_VALUE_HEADS * HEAD_SIZE), jnp.float32), -6.0, 6.0).astype(jnp.bfloat16)


def draw_session_starts(key, part):
    key = jax.random.fold_in(key, 5)
    gap_key, pick_key = jax.random.split(key)
    gap_sizes = jax.random.randint(gap_key, (PACK_COUNT, NSTART - 1), TOK_DEV, SESS_MOST + 1, jnp.int32)
    longest = jax.random.randint(pick_key, (PACK_COUNT, 1), 0, NSTART // 4, jnp.int32)
    gap_sizes = jnp.where(jnp.arange(NSTART - 1, dtype=jnp.int32)[None, :] == longest, SESS_MOST, gap_sizes)
    first_col = jnp.zeros((PACK_COUNT, 1), jnp.int32)
    starts = jnp.concatenate([first_col, jnp.cumsum(gap_sizes, axis=1).astype(jnp.int32)], axis=1)
    starts = jnp.minimum(starts, PACK_TOKENS)
    last_col = jnp.arange(NSTART, dtype=jnp.int32)[None, :] == NSTART - 1
    return jnp.where(last_col, PACK_TOKENS, starts).astype(jnp.int32)


def spiked(entries, key, source, target, parts, factor):
    def block_of(position):
        return (jnp.arange(entries.shape[position]) // (entries.shape[position] // parts)).reshape((-1,) + (1,) * (entries.ndim - 1 - position))

    near = jax.random.permutation(key, parts)[block_of(target)]
    second = (block_of(target) + parts // 2) % parts
    return jnp.where((block_of(source) == near) | (block_of(source) == second), factor * entries, entries)


def block_scale(stream_key, shape, pieces, low, largest):
    def one(position, shards_of):
        steps = jax.random.uniform(jax.random.fold_in(jax.random.fold_in(stream_key, 6), position), (shards_of,), jnp.float32, low / len(pieces), largest / len(pieces))
        return jnp.repeat(jnp.exp(steps), shape[position] // shards_of).reshape((-1,) + (1,) * (len(shape) - position - 1))

    factor_of = one(*pieces[0])
    for cut in pieces[1:]:
        factor_of = factor_of * one(*cut)
    return factor_of


def bell_draw(rng, shape, scale, limit, cuts=(), held_as=jnp.bfloat16):
    values = jax.random.normal(rng, shape, jnp.float32) * scale
    if len(cuts) > 0:
        values = block_scale(rng, shape, cuts, -0.22, 0.18) * values
    return jnp.clip(values, min=-limit, max=limit).astype(held_as)


def noise_with(own_key, extent, spread, bound, pieces, heavy, held_as=jnp.bfloat16):
    values = spread * jax.random.normal(own_key, extent, jnp.float32)
    if pieces:
        values = values * block_scale(own_key, extent, pieces, -0.22, 0.18)
    return jnp.clip(spiked(values, jax.random.fold_in(own_key, 3), *heavy), -bound, bound).astype(held_as)


def setup_inputs(seed: int = 0) -> dict:
    streams_of = jax.random.split(jax.random.key(seed), 8)
    return {
        "query_rows": draw_query_rows(jax.random.fold_in(streams_of[7], 71), 0),
        "key_rows": draw_key_rows(jax.random.fold_in(streams_of[7], 71), 0),
        "value_head_rows": bell_draw(streams_of[2], (PACK_COUNT, PACK_TOKENS, KEY_VALUE_HEADS * HEAD_SIZE), 1.0, 6.0, ((0, 4), (1, 64))),
        "grad_output": bell_draw(streams_of[3], (PACK_COUNT, PACK_TOKENS, QUERY_HEADS * HEAD_SIZE), 1.0, 6.0, ((0, 4), (1, 64))),
        "layer_inputs": noise_with(streams_of[4], (PACK_COUNT, PACK_TOKENS, MODEL_WIDTH), 1.0, 16.0, ((0, 4), (1, 64)), (1, 2, 64, 4.0)),
        "stretch_order": jax.vmap(lambda own: jax.random.permutation(own, STRETCHES_DEV))(jax.random.split(streams_of[5], PACK_COUNT * N_CTX)).reshape((PACK_COUNT, N_CTX, STRETCHES_DEV)).astype(jnp.int32),
        "session_starts": draw_session_starts(jax.random.fold_in(streams_of[7], 71), 0),
    }


def session_ids(positions, starts_row):
    return jnp.sum((starts_row[None, :] <= positions[:, None]).astype(jnp.int32), axis=1)


def group_grads(query_group, key_window, value_window, grad_group, allowed):
    score_scale = HEAD_SIZE ** -0.5
    query_f = query_group.astype(jnp.float32)
    key_f = key_window.astype(jnp.float32)
    value_f = value_window.astype(jnp.float32)
    grad_f = grad_group.astype(jnp.float32)
    scores = jnp.einsum('tjd,kd->jtk', query_f, key_f) * score_scale
    scores = jnp.where(allowed[None], scores, jnp.float32(-1.0e30))
    row_max = jnp.max(scores, axis=2, keepdims=True)
    row_sum = jnp.sum(jnp.exp(scores - row_max), axis=2, keepdims=True)
    log_total = row_max + jnp.log(row_sum)
    probability = jnp.exp(scores - log_total)
    prob_half = lax.optimization_barrier(probability.astype(jnp.bfloat16))
    attended = jnp.einsum('jtk,kd->tjd', prob_half.astype(jnp.float32), value_f).astype(jnp.bfloat16)
    attended = lax.optimization_barrier(attended)
    row_delta = jnp.sum(grad_f * attended.astype(jnp.float32), axis=2).T
    grad_prob = jnp.einsum('tjd,kd->jtk', grad_f, value_f)
    grad_score = (probability * (grad_prob - row_delta[:, :, None])).astype(jnp.bfloat16)
    grad_score = lax.optimization_barrier(grad_score).astype(jnp.float32)
    grad_q = jnp.einsum('jtk,kd->tjd', grad_score, key_f) * score_scale
    grad_k = jnp.einsum('jtk,tjd->kd', grad_score, query_f) * score_scale
    grad_v = jnp.einsum('jtk,tjd->kd', prob_half.astype(jnp.float32), grad_f)
    return grad_q, grad_k, grad_v


def pack_grads(query_pack, packed_keys, packed_values, grad_pack, order_pack, starts_row):
    offsets = jnp.arange(STRETCH, dtype=jnp.int32)
    shard_base = jnp.arange(N_CTX, dtype=jnp.int32) * TOK_DEV
    positions = (shard_base[:, None, None] + order_pack[:, :, None] * STRETCH + offsets[None, None, :]).reshape(PACK_TOKENS).astype(jnp.int32)
    sessions = session_ids(positions, starts_row)
    padding_rows = (SPAN - 1) * TOK_DEV
    window_rows = SPAN * TOK_DEV
    padded_keys = jnp.concatenate([jnp.zeros((padding_rows, KEY_VALUE_HEADS * HEAD_SIZE), packed_keys.dtype), packed_keys], axis=0)
    padded_values = jnp.concatenate([jnp.zeros((padding_rows, KEY_VALUE_HEADS * HEAD_SIZE), packed_values.dtype), packed_values], axis=0)
    pos_pad = jnp.concatenate([jnp.full((padding_rows,), -1, jnp.int32), positions], axis=0)
    sess_pad = jnp.concatenate([jnp.zeros((padding_rows,), jnp.int32), sessions], axis=0)

    def shard_step(carry, shard_index):
        key_acc, value_acc = carry
        first_row = (shard_index * TOK_DEV).astype(jnp.int32)
        query_block = lax.dynamic_slice_in_dim(query_pack, first_row, TOK_DEV, 0).reshape(TOK_DEV, QUERY_HEADS, HEAD_SIZE)
        grad_block = lax.dynamic_slice_in_dim(grad_pack, first_row, TOK_DEV, 0).reshape(TOK_DEV, QUERY_HEADS, HEAD_SIZE)
        query_pos = lax.dynamic_slice_in_dim(positions, first_row, TOK_DEV, 0)
        query_sess = lax.dynamic_slice_in_dim(sessions, first_row, TOK_DEV, 0)
        key_window = lax.dynamic_slice_in_dim(padded_keys, first_row, window_rows, 0)
        value_window = lax.dynamic_slice_in_dim(padded_values, first_row, window_rows, 0)
        key_pos = lax.dynamic_slice_in_dim(pos_pad, first_row, window_rows, 0)
        key_sess = lax.dynamic_slice_in_dim(sess_pad, first_row, window_rows, 0)
        allowed = (key_sess[None, :] == query_sess[:, None]) & (key_pos[None, :] <= query_pos[:, None]) & (key_pos[None, :] >= 0)
        query_parts, key_parts, value_parts = [], [], []
        for head_group in range(KEY_VALUE_HEADS):
            grad_q, grad_k, grad_v = group_grads(
                query_block[:, head_group * QUERY_PER_KEY:(head_group + 1) * QUERY_PER_KEY],
                key_window[:, head_group * HEAD_SIZE:(head_group + 1) * HEAD_SIZE],
                value_window[:, head_group * HEAD_SIZE:(head_group + 1) * HEAD_SIZE],
                grad_block[:, head_group * QUERY_PER_KEY:(head_group + 1) * QUERY_PER_KEY],
                allowed)
            query_parts.append(grad_q)
            key_parts.append(grad_k)
            value_parts.append(grad_v)
        grad_q_all = jnp.concatenate(query_parts, axis=1).reshape(TOK_DEV, QUERY_HEADS * HEAD_SIZE).astype(jnp.bfloat16)
        key_terms = jnp.concatenate(key_parts, axis=1)
        value_terms = jnp.concatenate(value_parts, axis=1)
        key_acc = lax.dynamic_update_slice_in_dim(key_acc, lax.dynamic_slice_in_dim(key_acc, first_row, window_rows, 0) + key_terms, first_row, 0)
        value_acc = lax.dynamic_update_slice_in_dim(value_acc, lax.dynamic_slice_in_dim(value_acc, first_row, window_rows, 0) + value_terms, first_row, 0)
        return (key_acc, value_acc), grad_q_all

    zeroed_accumulator = jnp.zeros((padding_rows + PACK_TOKENS, KEY_VALUE_HEADS * HEAD_SIZE), jnp.float32)
    (key_acc, value_acc), grad_q_blocks = lax.scan(shard_step, (zeroed_accumulator, zeroed_accumulator), jnp.arange(N_CTX, dtype=jnp.int32))
    grad_q_pack = grad_q_blocks.reshape(PACK_TOKENS, QUERY_HEADS * HEAD_SIZE)
    return grad_q_pack, key_acc[padding_rows:].astype(jnp.bfloat16), value_acc[padding_rows:].astype(jnp.bfloat16)


def reference(query_rows, key_rows, value_head_rows, grad_output, layer_inputs, stretch_order, session_starts):
    query_list, key_list, value_list = [], [], []
    summed_weight_gradient = jnp.zeros((MODEL_WIDTH, KEY_VALUE_HEADS * HEAD_SIZE), jnp.float32)
    for pack_index in range(PACK_COUNT):
        grad_q_pack, grad_k_pack, grad_v_pack = pack_grads(
            query_rows[pack_index], key_rows[pack_index], value_head_rows[pack_index],
            grad_output[pack_index], stretch_order[pack_index], session_starts[pack_index])
        query_list.append(grad_q_pack)
        key_list.append(grad_k_pack)
        value_list.append(grad_v_pack)
        summed_weight_gradient = summed_weight_gradient + jnp.dot(layer_inputs[pack_index].T, grad_v_pack, preferred_element_type=jnp.float32)
    return jnp.stack(query_list), jnp.stack(key_list), jnp.stack(value_list), summed_weight_gradient
```

```python
import math

import jax
import jax.numpy as jnp
from jax import lax
from jax.experimental import pallas as pl
from jax.experimental.pallas import tpu as pltpu
from jax.sharding import Mesh, PartitionSpec as P

HEAD = 128
STRETCH = 64
SPAN = 4
GROUPS = 4
PER_GROUP = 4
ROWS = 128
KEYS = SPAN * ROWS
WIDE = PER_GROUP * ROWS
MASKED = -1e30
SCALE = HEAD**-0.5
LOG2E = math.log2(math.e)
BF16 = jnp.bfloat16
F32 = jnp.float32
AXES = ("zl", "zh", "x", "y", "c")
CTX = ("zh", "x", "y", "c")
N_CTX = 64
NSTART = 64
MIB = 1024 * 1024


def nt(a, b):
    return lax.dot_general(a, b, (((1,), (1,)), ((), ())), preferred_element_type=F32)


def tn(a, b):
    return lax.dot_general(a, b, (((0,), (0,)), ((), ())), preferred_element_type=F32)


def nn(a, b):
    return lax.dot_general(a, b, (((1,), (0,)), ((), ())), preferred_element_type=F32)


def stack_heads(block):
    return jnp.concatenate([block[:, h * HEAD : (h + 1) * HEAD] for h in range(PER_GROUP)], axis=0)


def forward_kernel(
    ids, order, starts, q_ref, g_ref, k0, k1, k2, k3, prob_ref, own_ref, v1, v2, v3, bias_ref
):
    shard = ids[0]

    @pl.when(pl.program_id(0) == 0)
    def _():
        lane = lax.broadcasted_iota(jnp.int32, (1, ROWS), 1)
        first, second = order[2 * shard], order[2 * shard + 1]
        stretch = jnp.where(lane < STRETCH, first, second)
        query_pos = shard * ROWS + stretch * STRETCH + (lane & (STRETCH - 1))
        begin = jnp.zeros((1, ROWS), jnp.int32)
        for i in range(NSTART):
            begin = jnp.where(starts[i] <= query_pos, starts[i], begin)
        row = lax.broadcasted_iota(jnp.int32, (STRETCH, ROWS), 0)
        for d in range(SPAN):
            source = shard - d
            known = jnp.maximum(source, 0)
            for j in range(2):
                key_pos = source * ROWS + order[2 * known + j] * STRETCH + row
                allowed = (key_pos <= query_pos) & (key_pos >= begin)
                bias_ref[pl.ds((2 * d + j) * STRETCH, STRETCH), :] = jnp.where(
                    allowed, 0.0, MASKED
                )

    keys = jnp.concatenate([k0[...], k1[...], k2[...], k3[...]], axis=0)
    bias = bias_ref[...]
    for h in range(PER_GROUP):
        cols = pl.ds(h * HEAD, HEAD)
        score = nt(keys, q_ref[:, cols]) * (SCALE * LOG2E) + bias
        weight = jnp.exp2(score - jnp.max(score, axis=0, keepdims=True))
        total = jnp.sum(weight, axis=0, keepdims=True)
        prob_ref[0, :, cols] = (weight * (1.0 / total)).astype(BF16)
    value_grad = nn(prob_ref[0], stack_heads(g_ref[...]))
    own_ref[...] = value_grad[:ROWS]
    for d, ref in ((1, v1), (2, v2), (3, v3)):
        ref[...] = value_grad[d * ROWS : (d + 1) * ROWS].astype(BF16)


def backward_kernel(
    prob_ref, q_ref, g_ref, k0, k1, k2, k3, v0, v1, v2, v3, gq_ref, own_ref, d1, d2, d3
):
    keys = jnp.concatenate([k0[...], k1[...], k2[...], k3[...]], axis=0)
    values = jnp.concatenate([v0[...], v1[...], v2[...], v3[...]], axis=0)
    prob = prob_ref[0].astype(F32)
    grad_prob = nt(values, stack_heads(g_ref[...]))
    weighted = prob * grad_prob
    delta = jnp.sum(weighted, axis=0, keepdims=True)
    grad_score = (weighted - prob * delta).astype(BF16)
    key_grad = nn(grad_score, stack_heads(q_ref[...])) * SCALE
    own_ref[...] = key_grad[:ROWS]
    for d, ref in ((1, d1), (2, d2), (3, d3)):
        ref[...] = key_grad[d * ROWS : (d + 1) * ROWS].astype(BF16)
    query_grad = tn(grad_score, keys) * SCALE
    for h in range(PER_GROUP):
        gq_ref[:, h * HEAD : (h + 1) * HEAD] = query_grad[h * ROWS : (h + 1) * ROWS].astype(BF16)


def group_spec(width):
    return pl.BlockSpec((ROWS, width), lambda g, *_: (0, g))


def prob_spec():
    return pl.BlockSpec((1, KEYS, WIDE), lambda g, *_: (g, 0, 0))


def forward_call(ids, order, starts, query, grad, keys):
    narrow = jax.ShapeDtypeStruct((ROWS, GROUPS * HEAD), BF16)
    return pl.pallas_call(
        forward_kernel,
        grid_spec=pltpu.PrefetchScalarGridSpec(
            num_scalar_prefetch=3,
            grid=(GROUPS,),
            in_specs=[group_spec(PER_GROUP * HEAD)] * 2 + [group_spec(HEAD)] * SPAN,
            out_specs=[prob_spec()] + [group_spec(HEAD)] * SPAN,
            scratch_shapes=[pltpu.VMEM((KEYS, ROWS), F32)],
        ),
        out_shape=[
            jax.ShapeDtypeStruct((GROUPS, KEYS, WIDE), BF16),
            jax.ShapeDtypeStruct((ROWS, GROUPS * HEAD), F32),
            narrow,
            narrow,
            narrow,
        ],
        cost_estimate=pl.CostEstimate(
            flops=4 * 16 * ROWS * KEYS * HEAD, bytes_accessed=6 * MIB, transcendentals=MIB
        ),
        compiler_params=pltpu.CompilerParams(vmem_limit_bytes=24 * MIB),
        name="forward_and_value_gradient",
    )(ids, order, starts, query, grad, *keys)


def backward_call(prob, query, grad, keys, values):
    narrow = jax.ShapeDtypeStruct((ROWS, GROUPS * HEAD), BF16)
    return pl.pallas_call(
        backward_kernel,
        grid=(GROUPS,),
        in_specs=[prob_spec()] + [group_spec(PER_GROUP * HEAD)] * 2 + [group_spec(HEAD)] * 8,
        out_specs=[group_spec(PER_GROUP * HEAD)] + [group_spec(HEAD)] * SPAN,
        out_shape=[
            jax.ShapeDtypeStruct((ROWS, GROUPS * WIDE), BF16),
            jax.ShapeDtypeStruct((ROWS, GROUPS * HEAD), F32),
            narrow,
            narrow,
            narrow,
        ],
        cost_estimate=pl.CostEstimate(
            flops=6 * 16 * ROWS * KEYS * HEAD, bytes_accessed=6 * MIB, transcendentals=0
        ),
        compiler_params=pltpu.CompilerParams(vmem_limit_bytes=24 * MIB),
        name="query_and_key_gradient",
    )(prob, query, grad, *keys, *values)


def pack_kernel(ids, a0, a1, a2, a3, o0, o1, o2, o3):
    for a, o in ((a0, o0), (a1, o1), (a2, o2), (a3, o3)):
        o[...] = a[...]


def pack_call(ids, inputs):
    def taken(d):
        return pl.BlockSpec((ROWS, HEAD), lambda i, ids: (0, 4 * i + ((ids[1] + d) & 3)))

    return pl.pallas_call(
        pack_kernel,
        grid_spec=pltpu.PrefetchScalarGridSpec(
            num_scalar_prefetch=1,
            grid=(8,),
            in_specs=[taken(d) for d in range(4)],
            out_specs=[pl.BlockSpec((ROWS, HEAD), lambda i, ids: (0, i))] * 4,
        ),
        out_shape=[jax.ShapeDtypeStruct((ROWS, 8 * HEAD), BF16)] * 4,
        cost_estimate=pl.CostEstimate(flops=0, bytes_accessed=2 * MIB, transcendentals=0),
        name="pack_inputs",
    )(ids, inputs, inputs, inputs, inputs)


def weight_kernel(ids, grads, a0, a1, a2, a3, b0, b1, b2, b3, out_ref):
    x, core = ids[1], ids[2]
    total = jnp.zeros((8 * HEAD, 256), F32)
    for side, blocks in ((core, (a0, a1, a2, a3)), (1 - core, (b0, b1, b2, b3))):
        for d, block in enumerate(blocks):
            total += tn(block[...], grads[((x + 4 - d) & 3) * 2 + side])
    half = total.astype(BF16)
    for z in range(8):
        for y in range(4):
            out_ref[y, z * 32 : (z + 1) * 32, :] = half[z * 128 + y * 32 : z * 128 + y * 32 + 32]


def weight_call(ids, grads, own, other):
    whole = pl.BlockSpec(memory_space=pltpu.VMEM)
    return pl.pallas_call(
        weight_kernel,
        grid_spec=pltpu.PrefetchScalarGridSpec(
            num_scalar_prefetch=1,
            grid=(1,),
            in_specs=[whole] * 9,
            out_specs=whole,
        ),
        out_shape=jax.ShapeDtypeStruct((4, 256, 256), BF16),
        cost_estimate=pl.CostEstimate(
            flops=2 * 1024 * 1024 * 256, bytes_accessed=3 * MIB, transcendentals=0
        ),
        compiler_params=pltpu.CompilerParams(vmem_limit_bytes=32 * MIB),
        name="weight_gradient",
    )(ids, grads, *own, *other)


def shift_shards(block, distance):
    route = [(i - distance, i) for i in range(N_CTX) if 0 <= i - distance < N_CTX]
    return lax.ppermute(block, CTX, route)


def shift_x(block, distance):
    return lax.ppermute(block, "x", [(i, (i + distance) % 4) for i in range(4)])


def swap_core(block):
    return lax.ppermute(block, "c", [(0, 1), (1, 0)])


def shards(query, key, value, grad, inputs, stretch_order, session_starts):
    query, key, value, grad, inputs = query[0], key[0], value[0], grad[0], inputs[0]
    x, core = lax.axis_index("x"), lax.axis_index("c")
    ids = jnp.stack([lax.axis_index(CTX), x, core]).astype(jnp.int32)
    order = stretch_order.reshape(-1)
    starts = session_starts.reshape(-1)

    keys = [key] + [shift_shards(key, d) for d in range(1, SPAN)]
    values = [value] + [shift_shards(value, d) for d in range(1, SPAN)]
    packed = pack_call(ids, inputs)
    own = [packed[0]] + [shift_x(packed[d], d) for d in range(1, 4)]
    other = [swap_core(block) for block in own]

    prob, value_own, *value_terms = forward_call(ids, order, starts, query, grad, keys)
    grad_value = value_own
    for d in range(1, SPAN):
        grad_value = grad_value + shift_shards(value_terms[d - 1], -d).astype(F32)
    grad_value = grad_value.astype(BF16)

    grad_query, key_own, *key_terms = backward_call(prob, query, grad, keys, values)
    grad_key = key_own
    for d in range(1, SPAN):
        grad_key = grad_key + shift_shards(key_terms[d - 1], -d).astype(F32)
    grad_key = grad_key.astype(BF16)

    halves = jnp.stack([grad_value[:, :256], grad_value[:, 256:]])
    sent = jnp.broadcast_to(halves[None], (4, 2, ROWS, 256)).reshape(8, ROWS, 256)
    gathered = lax.all_to_all(sent, ("x", "c"), 0, 0, tiled=True)
    partial = weight_call(ids, gathered, own, other)
    partial = lax.all_to_all(partial, "y", 0, 0, tiled=True)
    partial = jnp.sum(partial.astype(F32), axis=0).astype(BF16).reshape(16, 16, 256)
    partial = lax.all_to_all(partial, ("zl", "zh", "c"), 0, 0, tiled=True)
    summed = jnp.sum(partial.reshape(8, 2, 16, 256).astype(F32), axis=0)
    weight_grad = jnp.concatenate([summed[0], summed[1]], axis=1)
    return grad_query[None], grad_key[None], grad_value[None], weight_grad


def solution(mesh):
    fine = Mesh(mesh.devices.reshape(4, 2, 4, 4, 2), AXES)
    rows = P("zl", CTX, None)
    return jax.shard_map(
        shards,
        mesh=fine,
        in_specs=(rows, rows, rows, rows, rows, P("zl", None, None), P("zl", None)),
        out_specs=(rows, rows, rows, P(AXES, None)),
        check_vma=False,
    )
```

```python
import math

import jax
import jax.numpy as jnp
from jax import lax
from jax.experimental import pallas as pl
from jax.experimental.pallas import tpu as pltpu
from jax.sharding import Mesh, PartitionSpec as P

HEAD = 128
STRETCH = 64
SPAN = 4
GROUPS = 4
PER_GROUP = 4
ROWS = 128
KEYS = SPAN * ROWS
WIDE = PER_GROUP * ROWS
MASKED = -1e30
SCALE = HEAD**-0.5
LOG2E = math.log2(math.e)
BF16 = jnp.bfloat16
F32 = jnp.float32
AXES = ("zl", "zh", "x", "y", "c")
CTX = ("zh", "x", "y", "c")
N_CTX = 64
NSTART = 64
MIB = 1024 * 1024
VMEM = 24 * MIB
VMEM_F = 59 * MIB


def nt(a, b):
    return lax.dot_general(a, b, (((1,), (1,)), ((), ())), preferred_element_type=F32)


def tn(a, b):
    return lax.dot_general(a, b, (((0,), (0,)), ((), ())), preferred_element_type=F32)


def nn(a, b):
    return lax.dot_general(a, b, (((1,), (0,)), ((), ())), preferred_element_type=F32)


def stack_heads(block):
    return jnp.concatenate([block[:, h * HEAD : (h + 1) * HEAD] for h in range(PER_GROUP)], axis=0)


def forward_kernel(
    ids,
    order_in,
    starts_in,
    q_in,
    g_in,
    k_in,
    k1,
    k2,
    k3,
    prob_ref,
    own_ref,
    v1,
    v2,
    v3,
    bias_ref,
    q_ref,
    g_ref,
    k0,
    order,
    starts,
    sems,
):
    group = pl.program_id(0)
    shard = ids[0]
    copies = [
        pltpu.make_async_copy(q_in, q_ref, sems.at[0]),
        pltpu.make_async_copy(g_in, g_ref, sems.at[1]),
        pltpu.make_async_copy(k_in, k0, sems.at[2]),
        pltpu.make_async_copy(order_in, order, sems.at[3]),
        pltpu.make_async_copy(starts_in, starts, sems.at[4]),
    ]

    @pl.when(group == 0)
    def _():
        for copy in copies:
            copy.start()
        copies[3].wait()
        copies[4].wait()
        lane = lax.broadcasted_iota(jnp.int32, (1, ROWS), 1)
        stretch = jnp.where(lane < STRETCH, order[0, shard, 0], order[0, shard, 1])
        query_pos = shard * ROWS + stretch * STRETCH + (lane & (STRETCH - 1))
        begin = jnp.zeros((1, ROWS), jnp.int32)
        for i in range(NSTART):
            begin = jnp.where(starts[0, i] <= query_pos, starts[0, i], begin)
        row = lax.broadcasted_iota(jnp.int32, (STRETCH, ROWS), 0)
        for d in range(SPAN):
            source = shard - d
            known = jnp.maximum(source, 0)
            for j in range(2):
                key_pos = source * ROWS + order[0, known, j] * STRETCH + row
                allowed = (key_pos <= query_pos) & (key_pos >= begin)
                bias_ref[pl.ds((2 * d + j) * STRETCH, STRETCH), :] = jnp.where(
                    allowed, 0.0, MASKED
                )
        for copy in copies[:3]:
            copy.wait()

    wide = pl.ds(pl.multiple_of(group * PER_GROUP * HEAD, PER_GROUP * HEAD), PER_GROUP * HEAD)
    narrow = pl.ds(pl.multiple_of(group * HEAD, HEAD), HEAD)
    keys = jnp.concatenate([k0[:, narrow], k1[...], k2[...], k3[...]], axis=0)
    bias = bias_ref[...]
    queries = q_ref[:, wide]
    for h in range(PER_GROUP):
        cols = slice(h * HEAD, (h + 1) * HEAD)
        score = nt(keys, queries[:, cols]) * (SCALE * LOG2E) + bias
        weight = jnp.exp2(score - jnp.max(score, axis=0, keepdims=True))
        total = jnp.sum(weight, axis=0, keepdims=True)
        prob_ref[0, :, cols] = (weight * (1.0 / total)).astype(BF16)
    value_grad = nn(prob_ref[0], stack_heads(g_ref[:, wide]))
    own_ref[...] = value_grad[:ROWS]
    for d, ref in ((1, v1), (2, v2), (3, v3)):
        ref[...] = value_grad[d * ROWS : (d + 1) * ROWS].astype(BF16)


def backward_kernel(
    prob_ref,
    q_in,
    g_in,
    k_in,
    v_in,
    k1,
    k2,
    k3,
    v1,
    v2,
    v3,
    gq_ref,
    own_ref,
    d1,
    d2,
    d3,
    q_ref,
    g_ref,
    k0,
    v0,
    sems,
):
    group = pl.program_id(0)

    @pl.when(group == 0)
    def _():
        copies = [
            pltpu.make_async_copy(source, target, sems.at[i])
            for i, (source, target) in enumerate(
                ((q_in, q_ref), (g_in, g_ref), (k_in, k0), (v_in, v0))
            )
        ]
        for copy in copies:
            copy.start()
        for copy in copies:
            copy.wait()

    wide = pl.ds(pl.multiple_of(group * PER_GROUP * HEAD, PER_GROUP * HEAD), PER_GROUP * HEAD)
    narrow = pl.ds(pl.multiple_of(group * HEAD, HEAD), HEAD)
    keys = jnp.concatenate([k0[:, narrow], k1[...], k2[...], k3[...]], axis=0)
    values = jnp.concatenate([v0[:, narrow], v1[...], v2[...], v3[...]], axis=0)
    prob = prob_ref[0].astype(F32)
    grad_prob = nt(values, stack_heads(g_ref[:, wide]))
    weighted = prob * grad_prob
    delta = jnp.sum(weighted, axis=0, keepdims=True)
    grad_score = (weighted - prob * delta).astype(BF16)
    key_grad = nn(grad_score, stack_heads(q_ref[:, wide])) * SCALE
    own_ref[...] = key_grad[:ROWS]
    for d, ref in ((1, d1), (2, d2), (3, d3)):
        ref[...] = key_grad[d * ROWS : (d + 1) * ROWS].astype(BF16)
    query_grad = tn(grad_score, keys) * SCALE
    for h in range(PER_GROUP):
        gq_ref[:, h * HEAD : (h + 1) * HEAD] = query_grad[h * ROWS : (h + 1) * ROWS].astype(BF16)


HBM_SPEC = pl.BlockSpec(memory_space=pltpu.HBM)


def group_spec(width):
    return pl.BlockSpec((ROWS, width), lambda g, *_: (0, g))


def prob_spec():
    return pl.BlockSpec((1, KEYS, WIDE), lambda g, *_: (g, 0, 0))


def forward_call(ids, order, starts, query, grad, keys):
    narrow = jax.ShapeDtypeStruct((ROWS, GROUPS * HEAD), BF16)
    return pl.pallas_call(
        forward_kernel,
        grid_spec=pltpu.PrefetchScalarGridSpec(
            num_scalar_prefetch=1,
            grid=(GROUPS,),
            in_specs=[HBM_SPEC] * 5 + [group_spec(HEAD)] * 3,
            out_specs=[prob_spec()] + [group_spec(HEAD)] * SPAN,
            scratch_shapes=[
                pltpu.VMEM((KEYS, ROWS), F32),
                pltpu.VMEM((ROWS, GROUPS * WIDE), BF16),
                pltpu.VMEM((ROWS, GROUPS * WIDE), BF16),
                pltpu.VMEM((ROWS, GROUPS * HEAD), BF16),
                pltpu.SMEM((1, N_CTX, 2), jnp.int32),
                pltpu.SMEM((1, NSTART), jnp.int32),
                pltpu.SemaphoreType.DMA((5,)),
            ],
        ),
        out_shape=[
            jax.ShapeDtypeStruct((GROUPS, KEYS, WIDE), BF16),
            jax.ShapeDtypeStruct((ROWS, GROUPS * HEAD), F32),
            narrow,
            narrow,
            narrow,
        ],
        cost_estimate=pl.CostEstimate(
            flops=4 * 16 * ROWS * KEYS * HEAD, bytes_accessed=6 * MIB, transcendentals=MIB
        ),
        compiler_params=pltpu.CompilerParams(vmem_limit_bytes=VMEM_F),
        name="forward_and_value_gradient",
    )(ids, order, starts, query, grad, *keys)


def backward_call(prob, query, grad, keys, values):
    narrow = jax.ShapeDtypeStruct((ROWS, GROUPS * HEAD), BF16)
    return pl.pallas_call(
        backward_kernel,
        grid=(GROUPS,),
        in_specs=[prob_spec()] + [HBM_SPEC] * 4 + [group_spec(HEAD)] * 6,
        out_specs=[group_spec(PER_GROUP * HEAD)] + [group_spec(HEAD)] * SPAN,
        scratch_shapes=[
            pltpu.VMEM((ROWS, GROUPS * WIDE), BF16),
            pltpu.VMEM((ROWS, GROUPS * WIDE), BF16),
            pltpu.VMEM((ROWS, GROUPS * HEAD), BF16),
            pltpu.VMEM((ROWS, GROUPS * HEAD), BF16),
            pltpu.SemaphoreType.DMA((4,)),
        ],
        out_shape=[
            jax.ShapeDtypeStruct((ROWS, GROUPS * WIDE), BF16),
            jax.ShapeDtypeStruct((ROWS, GROUPS * HEAD), F32),
            narrow,
            narrow,
            narrow,
        ],
        cost_estimate=pl.CostEstimate(
            flops=6 * 16 * ROWS * KEYS * HEAD, bytes_accessed=6 * MIB, transcendentals=0
        ),
        compiler_params=pltpu.CompilerParams(vmem_limit_bytes=VMEM),
        name="query_and_key_gradient",
    )(prob, query, grad, keys[0], values[0], *keys[1:], *values[1:])


def pack_kernel(ids, source, o0, o1, o2, o3, in_ref, sem):
    copy = pltpu.make_async_copy(source, in_ref, sem)
    copy.start()
    copy.wait()
    for d, out_ref in enumerate((o0, o1, o2, o3)):
        x = (ids[1] + d) & 3
        for z in range(8):
            column = pl.multiple_of((4 * z + x) * HEAD, HEAD)
            out_ref[:, z * HEAD : (z + 1) * HEAD] = in_ref[:, pl.ds(column, HEAD)]


def pack_call(ids, inputs):
    whole = pl.BlockSpec(memory_space=pltpu.VMEM)
    return pl.pallas_call(
        pack_kernel,
        grid_spec=pltpu.PrefetchScalarGridSpec(
            num_scalar_prefetch=1,
            grid=(1,),
            in_specs=[HBM_SPEC],
            out_specs=[whole] * 4,
            scratch_shapes=[pltpu.VMEM((ROWS, 32 * HEAD), BF16), pltpu.SemaphoreType.DMA],
        ),
        out_shape=[jax.ShapeDtypeStruct((ROWS, 8 * HEAD), BF16)] * 4,
        cost_estimate=pl.CostEstimate(flops=0, bytes_accessed=2 * MIB, transcendentals=0),
        compiler_params=pltpu.CompilerParams(vmem_limit_bytes=VMEM),
        name="pack_inputs",
    )(ids, inputs)


def total_kernel(own, r1, r2, r3, out_ref, sent_ref):
    total = own[...] + r1[...].astype(F32) + r2[...].astype(F32) + r3[...].astype(F32)
    total = total.astype(BF16)
    out_ref[...] = total
    for x in range(4):
        for c in range(2):
            sent_ref[2 * x + c] = total[:, c * 256 : (c + 1) * 256]


def total_call(own, returned):
    return pl.pallas_call(
        total_kernel,
        out_shape=[
            jax.ShapeDtypeStruct((ROWS, GROUPS * HEAD), BF16),
            jax.ShapeDtypeStruct((8, ROWS, 256), BF16),
        ],
        compiler_params=pltpu.CompilerParams(vmem_limit_bytes=VMEM),
        name="value_gradient_total",
    )(own, *returned)


def weight_kernel(ids, grads, a0, a1, a2, a3, b0, b1, b2, b3, out_ref):
    x, core = ids[1], ids[2]
    left = [ref[...] for ref in (a0, a1, a2, a3, b0, b1, b2, b3)]
    right = [grads[2 * ((x + 4 - d) & 3) + side] for side in (core, 1 - core) for d in range(4)]
    left, right = jnp.concatenate(left, axis=0), jnp.concatenate(right, axis=0)
    out_ref[...] = tn(left, right).astype(BF16)


def weight_call(ids, grads, own, other):
    taken = pl.BlockSpec((ROWS, 256), lambda i, _: (0, i))
    return pl.pallas_call(
        weight_kernel,
        grid_spec=pltpu.PrefetchScalarGridSpec(
            num_scalar_prefetch=1,
            grid=(4,),
            in_specs=[pl.BlockSpec((8, ROWS, 256), lambda i, _: (0, 0, 0))] + [taken] * 8,
            out_specs=pl.BlockSpec((256, 256), lambda i, _: (i, 0)),
        ),
        out_shape=jax.ShapeDtypeStruct((1024, 256), BF16),
        cost_estimate=pl.CostEstimate(
            flops=2 * 1024 * 1024 * 256, bytes_accessed=3 * MIB, transcendentals=0
        ),
        compiler_params=pltpu.CompilerParams(vmem_limit_bytes=VMEM),
        name="weight_gradient",
    )(ids, grads, *own, *other)


def final_kernel(ids, in_ref, keep_ref, send_ref):
    core = ids[2]
    total = in_ref[0].astype(F32)
    for i in range(1, 32):
        total += in_ref[i].astype(F32)
    first, second = total[:16], total[16:]
    keep_ref[...] = jnp.where(core == 0, first, second)
    send_ref[...] = jnp.where(core == 0, second, first)


def final_call(ids, parts):
    whole = pl.BlockSpec(memory_space=pltpu.VMEM)
    return pl.pallas_call(
        final_kernel,
        grid_spec=pltpu.PrefetchScalarGridSpec(
            num_scalar_prefetch=1, grid=(1,), in_specs=[whole], out_specs=[whole] * 2
        ),
        out_shape=[jax.ShapeDtypeStruct((16, 256), F32)] * 2,
        compiler_params=pltpu.CompilerParams(vmem_limit_bytes=VMEM),
        name="weight_rows",
    )(ids, parts)


def shift_shards(block, distance):
    route = [(i - distance, i) for i in range(N_CTX) if 0 <= i - distance < N_CTX]
    return lax.ppermute(block, CTX, route)


def shift_x(block, distance):
    return lax.ppermute(block, "x", [(i, (i + distance) % 4) for i in range(4)])


def swap_core(block):
    return lax.ppermute(block, "c", [(0, 1), (1, 0)])


def shards(query, key, value, grad, inputs, stretch_order, session_starts):
    query, key, value, grad, inputs = query[0], key[0], value[0], grad[0], inputs[0]
    x, core = lax.axis_index("x"), lax.axis_index("c")
    ids = jnp.stack([lax.axis_index(CTX), x, core]).astype(jnp.int32)

    far = [shift_shards(key, d) for d in (3, 2, 1)]
    keys = [key] + far[::-1]
    far = [shift_shards(value, d) for d in (3, 2, 1)]
    values = [value] + far[::-1]

    prob, value_own, *value_terms = forward_call(ids, stretch_order, session_starts, query, grad, keys)
    returned = [shift_shards(value_terms[d - 1], -d) for d in (3, 2, 1)]
    grad_query, key_own, *key_terms = backward_call(prob, query, grad, keys, values)
    packed = pack_call(ids, inputs)
    own = [packed[0]] + [shift_x(packed[d], d) for d in range(1, 4)]
    other = [swap_core(block) for block in own]
    grad_value, sent = total_call(value_own, returned)
    sent, grad_query = lax.optimization_barrier((sent, grad_query))
    gathered = lax.all_to_all(sent, ("x", "c"), 0, 0, tiled=True)
    partial = weight_call(ids, gathered, own, other).reshape(32, 32, 256)
    partial = lax.all_to_all(partial, ("zl", "zh", "y"), 0, 0, tiled=True)

    grad_key = key_own
    for d in (3, 2, 1):
        grad_key = grad_key + shift_shards(key_terms[d - 1], -d).astype(F32)
    grad_key = grad_key.astype(BF16)

    keep, send = final_call(ids, partial)
    swapped = swap_core(send)
    first, second = jnp.where(core == 0, keep, swapped), jnp.where(core == 0, swapped, keep)
    weight_grad = jnp.concatenate([first, second], axis=1)
    return grad_query[None], grad_key[None], grad_value[None], weight_grad


def solution(mesh):
    fine = Mesh(mesh.devices.reshape(4, 2, 4, 4, 2), AXES)
    rows = P("zl", CTX, None)
    return jax.shard_map(
        shards,
        mesh=fine,
        in_specs=(rows, rows, rows, rows, rows, P("zl", None, None), P("zl", None)),
        out_specs=(rows, rows, rows, P(AXES, None)),
        check_vma=False,
    )
```

```python
import math

import jax
import jax.numpy as jnp
from jax import lax
from jax.experimental import pallas as pl
from jax.experimental.pallas import tpu as pltpu
from jax.sharding import Mesh, PartitionSpec as P

HEAD = 128
STRETCH = 64
SPAN = 4
PER_GROUP = 4
GROUPS = 2
ROWS = 128
KEYS = SPAN * ROWS
WIDE = PER_GROUP * HEAD
HALF = GROUPS * HEAD
MASKED = -1e30
SCALE = HEAD**-0.5
LOG2E = math.log2(math.e)
BF16 = jnp.bfloat16
F32 = jnp.float32
AXES = ("zl", "zh", "x", "y", "c")
CTX = ("zh", "x", "y", "c")
CHIP = ("zh", "x", "y")
N_CHIP = 32
NSTART = 64
MIB = 1024 * 1024
PARAMS = pltpu.CompilerParams(vmem_limit_bytes=8 * MIB)
LARGE = pltpu.CompilerParams(vmem_limit_bytes=24 * MIB)
WHOLE = pl.BlockSpec(memory_space=pltpu.VMEM)


def nt(a, b):
    return lax.dot_general(a, b, (((1,), (1,)), ((), ())), preferred_element_type=F32)


def tn(a, b):
    return lax.dot_general(a, b, (((0,), (0,)), ((), ())), preferred_element_type=F32)


def nn(a, b):
    return lax.dot_general(a, b, (((1,), (0,)), ((), ())), preferred_element_type=F32)


def shape(*dims, dtype=BF16):
    return jax.ShapeDtypeStruct(dims, dtype)


def cost(flops, mib):
    return pl.CostEstimate(flops=flops, bytes_accessed=int(mib * MIB), transcendentals=0)


def stack_heads(block):
    return jnp.concatenate([block[:, h * HEAD : (h + 1) * HEAD] for h in range(PER_GROUP)], axis=0)


def put_rows(out_ref, core, own, other):
    out_ref[pl.ds(pl.multiple_of(core * ROWS, ROWS), ROWS), :] = own[...]
    out_ref[pl.ds(pl.multiple_of((1 - core) * ROWS, ROWS), ROWS), :] = other[...]


def pick_kernel(ids, k_own, k_other, v_own, v_other, key_ref, value_ref, last_ref):
    put_rows(key_ref, ids[2], k_own, k_other)
    put_rows(value_ref, ids[2], v_own, v_other)
    last_ref[:, :HALF] = key_ref[ROWS:]
    last_ref[:, HALF:] = value_ref[ROWS:]


def pick_call(ids, *blocks):
    half = pl.BlockSpec((ROWS, HALF), lambda i, ids: (0, ids[2]))
    return pl.pallas_call(
        pick_kernel,
        grid_spec=pltpu.PrefetchScalarGridSpec(
            num_scalar_prefetch=1, grid=(1,), in_specs=[half] * 4, out_specs=[WHOLE] * 3
        ),
        out_shape=[shape(2 * ROWS, HALF)] * 2 + [shape(ROWS, 2 * HALF)],
        compiler_params=PARAMS,
        cost_estimate=cost(0, 0.5),
        name="pick_keys_and_values",
    )(ids, *blocks)


def prepare_kernel(
    ids, order, starts, q_own, q_other, g_own, g_other, bias_ref, queries_ref, grads_ref
):
    put_rows(queries_ref, ids[2], q_own, q_other)
    put_rows(grads_ref, ids[2], g_own, g_other)
    base = ids[0] - ids[2]
    lane = lax.broadcasted_iota(jnp.int32, (1, ROWS), 1)
    row = lax.broadcasted_iota(jnp.int32, (STRETCH, ROWS), 0)
    for s in range(2):
        shard = base + s
        stretch = jnp.where(lane < STRETCH, order[2 * shard], order[2 * shard + 1])
        query_pos = shard * ROWS + stretch * STRETCH + (lane & (STRETCH - 1))
        begin = jnp.zeros((1, ROWS), jnp.int32)
        for i in range(NSTART):
            begin = jnp.where(starts[i] <= query_pos, starts[i], begin)
        for d in range(SPAN):
            source = shard - (SPAN - 1) + d
            known = jnp.maximum(source, 0)
            for j in range(2):
                key_pos = source * ROWS + order[2 * known + j] * STRETCH + row
                allowed = (key_pos <= query_pos) & (key_pos >= begin)
                bias_ref[s, (2 * d + j) * STRETCH : (2 * d + j + 1) * STRETCH, :] = jnp.where(
                    allowed, 0.0, MASKED
                )


def prepare_call(ids, order, starts, *blocks):
    half = pl.BlockSpec((ROWS, GROUPS * WIDE), lambda i, ids, *_: (0, ids[2]))
    return pl.pallas_call(
        prepare_kernel,
        grid_spec=pltpu.PrefetchScalarGridSpec(
            num_scalar_prefetch=3, grid=(1,), in_specs=[half] * 4, out_specs=[WHOLE] * 3
        ),
        out_shape=[shape(2, KEYS, ROWS, dtype=F32)] + [shape(2 * ROWS, GROUPS * WIDE)] * 2,
        compiler_params=PARAMS,
        cost_estimate=cost(0, 2.5),
        name="prepare",
    )(ids, order, starts, *blocks)


def spread(out, far1, far2, s0, s1):
    out[:ROWS] = s0[3 * ROWS :] + s1[2 * ROWS : 3 * ROWS]
    out[ROWS:] = s1[3 * ROWS :]
    far1[:ROWS] = (s0[ROWS : 2 * ROWS] + s1[:ROWS]).astype(BF16)
    far1[ROWS:] = (s0[2 * ROWS : 3 * ROWS] + s1[ROWS : 2 * ROWS]).astype(BF16)
    far2[...] = s0[:ROWS].astype(BF16)


def forward_kernel(bias, q_ref, g_ref, k2, k1, k0, prob_ref, own_ref, far1, far2):
    keys = jnp.concatenate([k2[...], k1[...], k0[...]], axis=0)
    terms = []
    for s in range(2):
        rows = slice(s * ROWS, (s + 1) * ROWS)
        window = keys[s * ROWS : s * ROWS + KEYS]
        for h in range(PER_GROUP):
            cols = slice(h * HEAD, (h + 1) * HEAD)
            score = nt(window, q_ref[rows, cols]) * (SCALE * LOG2E) + bias[s]
            weight = jnp.exp2(score - jnp.max(score, axis=0, keepdims=True))
            total = jnp.sum(weight, axis=0, keepdims=True)
            prob_ref[0, s, :, cols] = (weight * (1.0 / total)).astype(BF16)
        terms.append(nn(prob_ref[0, s], stack_heads(g_ref[rows, :])))
    spread(own_ref, far1, far2, *terms)


def backward_kernel(
    ids,
    prob_ref,
    q_ref,
    g_ref,
    k2,
    k1,
    k0,
    v2,
    v1,
    v0,
    keep_ref,
    send_ref,
    own_ref,
    far1,
    far2,
    gq_ref,
):
    core = ids[2]
    keys = jnp.concatenate([k2[...], k1[...], k0[...]], axis=0)
    values = jnp.concatenate([v2[...], v1[...], v0[...]], axis=0)
    terms = []
    for s in range(2):
        rows = slice(s * ROWS, (s + 1) * ROWS)
        window = slice(s * ROWS, s * ROWS + KEYS)
        prob = prob_ref[0, s].astype(F32)
        weighted = prob * nt(values[window], stack_heads(g_ref[rows, :]))
        delta = jnp.sum(weighted, axis=0, keepdims=True)
        grad_score = (weighted - prob * delta).astype(BF16)
        terms.append(nn(grad_score, stack_heads(q_ref[rows, :])) * SCALE)
        query_grad = tn(grad_score, keys[window]) * SCALE
        for h in range(PER_GROUP):
            gq_ref[s, :, h * HEAD : (h + 1) * HEAD] = query_grad[h * ROWS : (h + 1) * ROWS].astype(
                BF16
            )
    spread(own_ref, far1, far2, *terms)
    keep_ref[...] = gq_ref[core]
    send_ref[...] = gq_ref[1 - core]


def narrow(rows, shift=0):
    return pl.BlockSpec((rows, HEAD), lambda j, *_: (0, j + shift))


def wide(rows):
    return pl.BlockSpec((rows, WIDE), lambda j, *_: (0, j))


WINDOW = [narrow(ROWS), narrow(2 * ROWS), narrow(2 * ROWS)]
VALUE_WINDOW = [narrow(ROWS, GROUPS)] + WINDOW[1:]
TERMS = [narrow(2 * ROWS), narrow(2 * ROWS), narrow(ROWS)]
PROB_SPEC = pl.BlockSpec((1, 2, KEYS, WIDE), lambda j, *_: (j, 0, 0, 0))


def term_shapes():
    return [shape(2 * ROWS, HALF, dtype=F32), shape(2 * ROWS, HALF), shape(ROWS, HALF)]


def forward_call(bias, queries, grads, keys):
    return pl.pallas_call(
        forward_kernel,
        grid=(GROUPS,),
        in_specs=[pl.BlockSpec((2, KEYS, ROWS), lambda j: (0, 0, 0))]
        + [wide(2 * ROWS)] * 2
        + WINDOW,
        out_specs=[PROB_SPEC] + TERMS,
        out_shape=[shape(GROUPS, 2, KEYS, WIDE)] + term_shapes(),
        compiler_params=LARGE,
        cost_estimate=cost(4 * 16 * ROWS * KEYS * HEAD, 6),
        name="forward_and_value_gradient",
    )(bias, queries, grads, *keys)


def backward_call(ids, prob, queries, grads, keys, values):
    return pl.pallas_call(
        backward_kernel,
        grid_spec=pltpu.PrefetchScalarGridSpec(
            num_scalar_prefetch=1,
            grid=(GROUPS,),
            in_specs=[PROB_SPEC] + [wide(2 * ROWS)] * 2 + WINDOW + VALUE_WINDOW,
            out_specs=[wide(ROWS)] * 2 + TERMS,
            scratch_shapes=[pltpu.VMEM((2, ROWS, WIDE), BF16)],
        ),
        out_shape=[shape(ROWS, GROUPS * WIDE)] * 2 + term_shapes(),
        compiler_params=LARGE,
        cost_estimate=cost(6 * 16 * ROWS * KEYS * HEAD, 6),
        name="query_and_key_gradient",
    )(ids, prob, queries, grads, *keys, *values)


def pack_kernel(ids, in_ref, o0, o1, o2, o3):
    for d, out_ref in enumerate((o0, o1, o2, o3)):
        x = (ids[1] + d) & 3
        for z in range(8):
            column = pl.multiple_of((4 * z + x) * HEAD, HEAD)
            out_ref[:, z * HEAD : (z + 1) * HEAD] = in_ref[:, pl.ds(column, HEAD)]


def pack_call(ids, inputs):
    return pl.pallas_call(
        pack_kernel,
        grid_spec=pltpu.PrefetchScalarGridSpec(
            num_scalar_prefetch=1, grid=(1,), in_specs=[WHOLE], out_specs=[WHOLE] * 4
        ),
        out_shape=[shape(ROWS, 8 * HEAD)] * 4,
        compiler_params=PARAMS,
        cost_estimate=cost(0, 2),
        name="pack_inputs",
    )(ids, inputs)


def add_terms(own, r1, r2):
    first = own[:ROWS] + r1[:ROWS].astype(F32)
    second = own[ROWS:] + r1[ROWS:].astype(F32) + r2[...].astype(F32)
    return first.astype(BF16), second.astype(BF16)


def value_total_kernel(ids, own, r1, r2, keep_ref, send_ref, copies_ref):
    core = ids[2]
    first, second = add_terms(own, r1, r2)
    for x in range(4):
        copies_ref[x, :ROWS], copies_ref[x, ROWS:] = first, second
    keep_ref[...] = copies_ref[0, pl.ds(pl.multiple_of(core * ROWS, ROWS), ROWS), :]
    send_ref[...] = copies_ref[0, pl.ds(pl.multiple_of((1 - core) * ROWS, ROWS), ROWS), :]


def key_total_kernel(ids, own, r1, r2, keep_ref, send_ref, both_ref):
    core = ids[2]
    both_ref[:ROWS], both_ref[ROWS:] = add_terms(own, r1, r2)
    keep_ref[...] = both_ref[pl.ds(pl.multiple_of(core * ROWS, ROWS), ROWS), :]
    send_ref[...] = both_ref[pl.ds(pl.multiple_of((1 - core) * ROWS, ROWS), ROWS), :]


def total_call(ids, own, r1, r2, copies):
    return pl.pallas_call(
        value_total_kernel if copies else key_total_kernel,
        grid_spec=pltpu.PrefetchScalarGridSpec(
            num_scalar_prefetch=1,
            grid=(1,),
            in_specs=[WHOLE] * 3,
            out_specs=[WHOLE] * (3 if copies else 2),
            scratch_shapes=[] if copies else [pltpu.VMEM((2 * ROWS, HALF), BF16)],
        ),
        out_shape=[shape(ROWS, HALF)] * 2 + ([shape(4, 2 * ROWS, HALF)] if copies else []),
        compiler_params=PARAMS,
        cost_estimate=cost(0, 1),
        name="value_gradient_total" if copies else "key_gradient_total",
    )(ids, own, r1, r2)


def join_kernel(ids, *refs):
    core = ids[2]
    count = len(refs) // 3
    for keep, other, out in zip(refs[:count], refs[count : 2 * count], refs[2 * count :]):
        width = keep.shape[1]
        out[:, pl.ds(pl.multiple_of(core * width, HEAD), width)] = keep[...]
        out[:, pl.ds(pl.multiple_of((1 - core) * width, HEAD), width)] = other[...]


def join_call(ids, keep, other, name):
    return pl.pallas_call(
        join_kernel,
        grid_spec=pltpu.PrefetchScalarGridSpec(
            num_scalar_prefetch=1,
            grid=(1,),
            in_specs=[WHOLE] * (2 * len(keep)),
            out_specs=[WHOLE] * len(keep),
        ),
        out_shape=[shape(a.shape[0], 2 * a.shape[1], dtype=a.dtype) for a in keep],
        compiler_params=PARAMS,
        cost_estimate=cost(0, 0.5),
        name=name,
    )(ids, *keep, *other)


def weight_kernel(ids, grads, a0, a1, a2, a3, b0, b1, b2, b3, out_ref):
    x, core = ids[1], ids[2]
    left = [ref[...] for ref in (a0, a1, a2, a3, b0, b1, b2, b3)]
    right = []
    for side in (core, 1 - core):
        rows = pl.ds(pl.multiple_of(side * ROWS, ROWS), ROWS)
        right += [grads[(x + 4 - d) & 3, rows, :] for d in range(4)]
    left, right = jnp.concatenate(left, axis=0), jnp.concatenate(right, axis=0)
    out_ref[...] = tn(left, right).astype(BF16)


def weight_call(ids, grads, own, other):
    taken = pl.BlockSpec((ROWS, 256), lambda i, _: (0, i))
    return pl.pallas_call(
        weight_kernel,
        grid_spec=pltpu.PrefetchScalarGridSpec(
            num_scalar_prefetch=1,
            grid=(4,),
            in_specs=[pl.BlockSpec((4, 2 * ROWS, HALF), lambda i, _: (0, 0, 0))] + [taken] * 8,
            out_specs=pl.BlockSpec((256, HALF), lambda i, _: (i, 0)),
        ),
        out_shape=shape(1024, HALF),
        compiler_params=LARGE,
        cost_estimate=cost(2 * 1024 * 1024 * 256, 3),
        name="weight_gradient",
    )(ids, grads, *own, *other)


def final_kernel(ids, in_ref, keep_ref, send_ref, total_ref):
    core = ids[2]
    total = in_ref[0].astype(F32)
    for i in range(1, 32):
        total += in_ref[i].astype(F32)
    total_ref[...] = total
    keep_ref[...] = total_ref[pl.ds(pl.multiple_of(core * 16, 16), 16), :]
    send_ref[...] = total_ref[pl.ds(pl.multiple_of((1 - core) * 16, 16), 16), :]


def final_call(ids, parts):
    return pl.pallas_call(
        final_kernel,
        grid_spec=pltpu.PrefetchScalarGridSpec(
            num_scalar_prefetch=1,
            grid=(1,),
            in_specs=[WHOLE],
            out_specs=[WHOLE] * 2,
            scratch_shapes=[pltpu.VMEM((32, HALF), F32)],
        ),
        out_shape=[shape(16, HALF, dtype=F32)] * 2,
        compiler_params=PARAMS,
        cost_estimate=cost(0, 0.5),
        name="weight_rows",
    )(ids, parts)


def shift_chips(block, distance):
    route = [(i - distance, i) for i in range(N_CHIP) if 0 <= i - distance < N_CHIP]
    return lax.ppermute(block, CHIP, route)


def shift_x(block, distance):
    return lax.ppermute(block, "x", [(i, (i + distance) % 4) for i in range(4)])


def swap_core(block):
    return lax.ppermute(block, "c", [(0, 1), (1, 0)])


def shards(query, key, value, grad, inputs, stretch_order, session_starts):
    query, key, value, grad, inputs = query[0], key[0], value[0], grad[0], inputs[0]
    core = lax.axis_index("c")
    ids = jnp.stack([lax.axis_index(CTX), lax.axis_index("x"), core]).astype(jnp.int32)

    key0, value0, last = pick_call(ids, key, swap_core(key), value, swap_core(value))
    far2 = shift_chips(last, 2)
    keys = [far2, shift_chips(key0, 1), key0]
    bias, queries, grads = prepare_call(
        ids,
        stretch_order.reshape(-1),
        session_starts.reshape(-1),
        query,
        swap_core(query),
        grad,
        swap_core(grad),
    )
    bias, value0 = lax.optimization_barrier((bias, value0))
    value1 = shift_chips(value0, 1)

    prob, value_own, value_t1, value_t2 = forward_call(bias, queries, grads, keys)
    value_r2 = shift_chips(value_t2, -2)
    value_r1 = shift_chips(value_t1, -1)
    values = [far2, value1, value0]
    query_keep, query_send, key_own, key_t1, key_t2 = backward_call(
        ids, prob, queries, grads, keys, values
    )
    inputs, query_send = lax.optimization_barrier((inputs, query_send))
    packed = pack_call(ids, inputs)
    own = [packed[0]] + [shift_x(packed[d], d) for d in range(1, 4)]
    other = [swap_core(block) for block in own]
    value_r1, query_send = lax.optimization_barrier((value_r1, query_send))
    value_keep, value_send, sent = total_call(ids, value_own, value_r1, value_r2, True)
    gathered = lax.all_to_all(sent, "x", 0, 0, tiled=True)
    partial = weight_call(ids, gathered, own, other).reshape(32, 32, HALF)
    partial = lax.all_to_all(partial, ("zl", "zh", "y"), 0, 0, tiled=True)

    key_r2 = shift_chips(key_t2, -2)
    key_r1 = shift_chips(key_t1, -1)
    key_keep, key_send = total_call(ids, key_own, key_r1, key_r2, False)
    grad_query, grad_value = join_call(
        ids,
        [query_keep, value_keep],
        [swap_core(query_send), swap_core(value_send)],
        "join_query_and_value",
    )
    (grad_key,) = join_call(ids, [key_keep], [swap_core(key_send)], "join_key")

    row_keep, row_send = final_call(ids, partial)
    (weight_grad,) = join_call(ids, [row_keep], [swap_core(row_send)], "join_weight")
    return grad_query[None], grad_key[None], grad_value[None], weight_grad


def solution(mesh):
    fine = Mesh(mesh.devices.reshape(4, 2, 4, 4, 2), AXES)
    rows = P("zl", CTX, None)
    return jax.shard_map(
        shards,
        mesh=fine,
        in_specs=(rows, rows, rows, rows, rows, P("zl", None, None), P("zl", None)),
        out_specs=(rows, rows, rows, P(AXES, None)),
        check_vma=False,
    )
```

```python
import math

import jax
import jax.numpy as jnp
from jax import lax
from jax.experimental import pallas as pl
from jax.experimental.pallas import tpu as pltpu
from jax.sharding import Mesh, PartitionSpec as P

HEAD = 128
STRETCH = 64
SPAN = 4
PER_GROUP = 4
GROUPS = 2
ROWS = 128
KEYS = SPAN * ROWS
WIDE = PER_GROUP * HEAD
HALF = GROUPS * HEAD
MASKED = -1e30
SCALE = HEAD**-0.5
LOG2E = math.log2(math.e)
BF16 = jnp.bfloat16
F32 = jnp.float32
AXES = ("zl", "zh", "x", "y", "c")
CTX = ("zh", "x", "y", "c")
CHIP = ("zh", "x", "y")
N_CHIP = 32
NSTART = 64
MIB = 1024 * 1024
PARAMS = pltpu.CompilerParams(vmem_limit_bytes=8 * MIB)
LARGE = pltpu.CompilerParams(vmem_limit_bytes=24 * MIB)
WHOLE = pl.BlockSpec(memory_space=pltpu.VMEM)


def nt(a, b):
    return lax.dot_general(a, b, (((1,), (1,)), ((), ())), preferred_element_type=F32)


def tn(a, b):
    return lax.dot_general(a, b, (((0,), (0,)), ((), ())), preferred_element_type=F32)


def nn(a, b):
    return lax.dot_general(a, b, (((1,), (0,)), ((), ())), preferred_element_type=F32)


def shape(*dims, dtype=BF16):
    return jax.ShapeDtypeStruct(dims, dtype)


def cost(flops, mib):
    return pl.CostEstimate(flops=flops, bytes_accessed=int(mib * MIB), transcendentals=0)


def stack_heads(block):
    return jnp.concatenate([block[:, h * HEAD : (h + 1) * HEAD] for h in range(PER_GROUP)], axis=0)


def put_rows(out_ref, core, own, other):
    out_ref[pl.ds(pl.multiple_of(core * ROWS, ROWS), ROWS), :] = own[...]
    out_ref[pl.ds(pl.multiple_of((1 - core) * ROWS, ROWS), ROWS), :] = other[...]


def pick_keys_kernel(ids, own, other, both_ref):
    put_rows(both_ref, ids[2], own, other)


def pick_values_kernel(ids, own, other, keys, both_ref, last_ref):
    put_rows(both_ref, ids[2], own, other)
    last_ref[:, :HALF] = keys[ROWS:]
    last_ref[:, HALF:] = both_ref[ROWS:]


def pick_call(ids, own, other, keys=None):
    half = pl.BlockSpec((ROWS, HALF), lambda i, ids: (0, ids[2]))
    extra = [] if keys is None else [keys]
    return pl.pallas_call(
        pick_values_kernel if extra else pick_keys_kernel,
        grid_spec=pltpu.PrefetchScalarGridSpec(
            num_scalar_prefetch=1,
            grid=(1,),
            in_specs=[half] * 2 + [WHOLE] * len(extra),
            out_specs=[WHOLE] * (1 + len(extra)),
        ),
        out_shape=[shape(2 * ROWS, HALF)] + [shape(ROWS, 2 * HALF)] * len(extra),
        compiler_params=PARAMS,
        cost_estimate=cost(0, 0.5),
        name="pick_values" if extra else "pick_keys",
    )(ids, own, other, *extra)


def prepare_kernel(
    ids, order, starts, q_own, q_other, g_own, g_other, bias_ref, queries_ref, grads_ref
):
    put_rows(queries_ref, ids[2], q_own, q_other)
    put_rows(grads_ref, ids[2], g_own, g_other)
    base = ids[0] - ids[2]
    lane = lax.broadcasted_iota(jnp.int32, (1, ROWS), 1)
    row = lax.broadcasted_iota(jnp.int32, (STRETCH, ROWS), 0)
    for s in range(2):
        shard = base + s
        stretch = jnp.where(lane < STRETCH, order[2 * shard], order[2 * shard + 1])
        query_pos = shard * ROWS + stretch * STRETCH + (lane & (STRETCH - 1))
        begin = jnp.zeros((1, ROWS), jnp.int32)
        for i in range(NSTART):
            begin = jnp.where(starts[i] <= query_pos, starts[i], begin)
        for d in range(SPAN):
            source = shard - (SPAN - 1) + d
            known = jnp.maximum(source, 0)
            for j in range(2):
                key_pos = source * ROWS + order[2 * known + j] * STRETCH + row
                allowed = (key_pos <= query_pos) & (key_pos >= begin)
                bias_ref[s, (2 * d + j) * STRETCH : (2 * d + j + 1) * STRETCH, :] = jnp.where(
                    allowed, 0.0, MASKED
                )


def prepare_call(ids, order, starts, *blocks):
    half = pl.BlockSpec((ROWS, GROUPS * WIDE), lambda i, ids, *_: (0, ids[2]))
    return pl.pallas_call(
        prepare_kernel,
        grid_spec=pltpu.PrefetchScalarGridSpec(
            num_scalar_prefetch=3, grid=(1,), in_specs=[half] * 4, out_specs=[WHOLE] * 3
        ),
        out_shape=[shape(2, KEYS, ROWS, dtype=F32)] + [shape(2 * ROWS, GROUPS * WIDE)] * 2,
        compiler_params=PARAMS,
        cost_estimate=cost(0, 2.5),
        name="prepare",
    )(ids, order, starts, *blocks)


def spread(out, far1, far2, s0, s1):
    out[:ROWS] = s0[3 * ROWS :] + s1[2 * ROWS : 3 * ROWS]
    out[ROWS:] = s1[3 * ROWS :]
    far1[:ROWS] = (s0[ROWS : 2 * ROWS] + s1[:ROWS]).astype(BF16)
    far1[ROWS:] = (s0[2 * ROWS : 3 * ROWS] + s1[ROWS : 2 * ROWS]).astype(BF16)
    far2[...] = s0[:ROWS].astype(far2.dtype)


def forward_kernel(bias, q_ref, g_ref, k2, k1, k0, prob_ref, own_ref, far1, far2):
    keys = jnp.concatenate([k2[...], k1[...], k0[...]], axis=0)
    terms = []
    for s in range(2):
        rows = slice(s * ROWS, (s + 1) * ROWS)
        window = keys[s * ROWS : s * ROWS + KEYS]
        for h in range(PER_GROUP):
            cols = slice(h * HEAD, (h + 1) * HEAD)
            score = nt(window, q_ref[rows, cols]) * (SCALE * LOG2E) + bias[s]
            weight = jnp.exp2(score - jnp.max(score, axis=0, keepdims=True))
            total = jnp.sum(weight, axis=0, keepdims=True)
            prob_ref[0, s, :, cols] = (weight * (1.0 / total)).astype(BF16)
        terms.append(nn(prob_ref[0, s], stack_heads(g_ref[rows, :])))
    spread(own_ref, far1, far2, *terms)


def backward_kernel(
    ids,
    prob_ref,
    q_ref,
    g_ref,
    k2,
    k1,
    k0,
    v2,
    v1,
    v0,
    keep_ref,
    send_ref,
    own_ref,
    far1,
    far2,
    gq_ref,
):
    core = ids[2]
    keys = jnp.concatenate([k2[...], k1[...], k0[...]], axis=0)
    values = jnp.concatenate([v2[...], v1[...], v0[...]], axis=0)
    terms = []
    for s in range(2):
        rows = slice(s * ROWS, (s + 1) * ROWS)
        window = slice(s * ROWS, s * ROWS + KEYS)
        prob = prob_ref[0, s].astype(F32)
        weighted = prob * nt(values[window], stack_heads(g_ref[rows, :]))
        delta = jnp.sum(weighted, axis=0, keepdims=True)
        grad_score = (weighted - prob * delta).astype(BF16)
        terms.append(nn(grad_score, stack_heads(q_ref[rows, :])) * SCALE)
        query_grad = tn(grad_score, keys[window]) * SCALE
        for h in range(PER_GROUP):
            gq_ref[s, :, h * HEAD : (h + 1) * HEAD] = query_grad[h * ROWS : (h + 1) * ROWS].astype(
                BF16
            )
    spread(own_ref, far1, far2, *terms)
    keep_ref[...] = gq_ref[core]
    send_ref[...] = gq_ref[1 - core]


def narrow(rows, shift=0):
    return pl.BlockSpec((rows, HEAD), lambda j, *_: (0, j + shift))


def wide(rows):
    return pl.BlockSpec((rows, WIDE), lambda j, *_: (0, j))


WINDOW = [narrow(ROWS), narrow(2 * ROWS), narrow(2 * ROWS)]
VALUE_WINDOW = [narrow(ROWS, GROUPS)] + WINDOW[1:]
TERMS = [narrow(2 * ROWS), narrow(2 * ROWS), narrow(ROWS)]
PROB_SPEC = pl.BlockSpec((1, 2, KEYS, WIDE), lambda j, *_: (j, 0, 0, 0))


def term_shapes(last):
    return [shape(2 * ROWS, HALF, dtype=F32), shape(2 * ROWS, HALF), shape(ROWS, HALF, dtype=last)]


def forward_call(bias, queries, grads, keys):
    return pl.pallas_call(
        forward_kernel,
        grid=(GROUPS,),
        in_specs=[pl.BlockSpec((2, KEYS, ROWS), lambda j: (0, 0, 0))]
        + [wide(2 * ROWS)] * 2
        + WINDOW,
        out_specs=[PROB_SPEC] + TERMS,
        out_shape=[shape(GROUPS, 2, KEYS, WIDE)] + term_shapes(F32),
        compiler_params=LARGE,
        cost_estimate=cost(4 * 16 * ROWS * KEYS * HEAD, 6),
        name="forward_and_value_gradient",
    )(bias, queries, grads, *keys)


def backward_call(ids, prob, queries, grads, keys, values):
    return pl.pallas_call(
        backward_kernel,
        grid_spec=pltpu.PrefetchScalarGridSpec(
            num_scalar_prefetch=1,
            grid=(GROUPS,),
            in_specs=[PROB_SPEC] + [wide(2 * ROWS)] * 2 + WINDOW + VALUE_WINDOW,
            out_specs=[wide(ROWS)] * 2 + TERMS,
            scratch_shapes=[pltpu.VMEM((2, ROWS, WIDE), BF16)],
        ),
        out_shape=[shape(ROWS, GROUPS * WIDE)] * 2 + term_shapes(BF16),
        compiler_params=LARGE,
        cost_estimate=cost(6 * 16 * ROWS * KEYS * HEAD, 6),
        name="query_and_key_gradient",
    )(ids, prob, queries, grads, *keys, *values)


def pack_kernel(ids, in_ref, o0, o1, o2, o3):
    for d, out_ref in enumerate((o0, o1, o2, o3)):
        x = (ids[1] + d) & 3
        for z in range(8):
            column = pl.multiple_of((4 * z + x) * HEAD, HEAD)
            out_ref[:, z * HEAD : (z + 1) * HEAD] = in_ref[:, pl.ds(column, HEAD)]


def pack_call(ids, inputs):
    return pl.pallas_call(
        pack_kernel,
        grid_spec=pltpu.PrefetchScalarGridSpec(
            num_scalar_prefetch=1, grid=(1,), in_specs=[WHOLE], out_specs=[WHOLE] * 4
        ),
        out_shape=[shape(ROWS, 8 * HEAD)] * 4,
        compiler_params=PARAMS,
        cost_estimate=cost(0, 2),
        name="pack_inputs",
    )(ids, inputs)


def add_terms(own, r1, r2):
    first = own[:ROWS] + r1[:ROWS].astype(F32)
    second = own[ROWS:] + r1[ROWS:].astype(F32) + r2[...].astype(F32)
    return first.astype(BF16), second.astype(BF16)


def value_total_kernel(ids, own, r1, r2, keep_ref, send_ref, copies_ref):
    core = ids[2]
    first, second = add_terms(own, r1, r2)
    for x in range(4):
        copies_ref[x, :ROWS], copies_ref[x, ROWS:] = first, second
    keep_ref[...] = copies_ref[0, pl.ds(pl.multiple_of(core * ROWS, ROWS), ROWS), :]
    send_ref[...] = copies_ref[0, pl.ds(pl.multiple_of((1 - core) * ROWS, ROWS), ROWS), :]


def key_total_kernel(ids, own, r1, r2, keep_ref, send_ref, both_ref):
    core = ids[2]
    both_ref[:ROWS], both_ref[ROWS:] = add_terms(own, r1, r2)
    keep_ref[...] = both_ref[pl.ds(pl.multiple_of(core * ROWS, ROWS), ROWS), :]
    send_ref[...] = both_ref[pl.ds(pl.multiple_of((1 - core) * ROWS, ROWS), ROWS), :]


def total_call(ids, own, r1, r2, copies):
    return pl.pallas_call(
        value_total_kernel if copies else key_total_kernel,
        grid_spec=pltpu.PrefetchScalarGridSpec(
            num_scalar_prefetch=1,
            grid=(1,),
            in_specs=[WHOLE] * 3,
            out_specs=[WHOLE] * (3 if copies else 2),
            scratch_shapes=[] if copies else [pltpu.VMEM((2 * ROWS, HALF), BF16)],
        ),
        out_shape=[shape(ROWS, HALF)] * 2 + ([shape(4, 2 * ROWS, HALF)] if copies else []),
        compiler_params=PARAMS,
        cost_estimate=cost(0, 1),
        name="value_gradient_total" if copies else "key_gradient_total",
    )(ids, own, r1, r2)


def join_kernel(ids, *refs):
    core = ids[2]
    count = len(refs) // 3
    for keep, other, out in zip(refs[:count], refs[count : 2 * count], refs[2 * count :]):
        width = keep.shape[1]
        out[:, pl.ds(pl.multiple_of(core * width, HEAD), width)] = keep[...]
        out[:, pl.ds(pl.multiple_of((1 - core) * width, HEAD), width)] = other[...]


def join_call(ids, keep, other, name):
    return pl.pallas_call(
        join_kernel,
        grid_spec=pltpu.PrefetchScalarGridSpec(
            num_scalar_prefetch=1,
            grid=(1,),
            in_specs=[WHOLE] * (2 * len(keep)),
            out_specs=[WHOLE] * len(keep),
        ),
        out_shape=[shape(a.shape[0], 2 * a.shape[1], dtype=a.dtype) for a in keep],
        compiler_params=PARAMS,
        cost_estimate=cost(0, 0.5),
        name=name,
    )(ids, *keep, *other)


def weight_kernel(ids, grads, a0, a1, a2, a3, b0, b1, b2, b3, out_ref):
    x, core = ids[1], ids[2]
    left = [ref[...] for ref in (a0, a1, a2, a3, b0, b1, b2, b3)]
    right = []
    for side in (core, 1 - core):
        rows = pl.ds(pl.multiple_of(side * ROWS, ROWS), ROWS)
        right += [grads[(x + 4 - d) & 3, rows, :] for d in range(4)]
    left, right = jnp.concatenate(left, axis=0), jnp.concatenate(right, axis=0)
    out_ref[...] = tn(left, right).astype(BF16)


def weight_call(ids, grads, own, other):
    taken = pl.BlockSpec((ROWS, 256), lambda i, _: (0, i))
    return pl.pallas_call(
        weight_kernel,
        grid_spec=pltpu.PrefetchScalarGridSpec(
            num_scalar_prefetch=1,
            grid=(4,),
            in_specs=[pl.BlockSpec((4, 2 * ROWS, HALF), lambda i, _: (0, 0, 0))] + [taken] * 8,
            out_specs=pl.BlockSpec((256, HALF), lambda i, _: (i, 0)),
        ),
        out_shape=shape(1024, HALF),
        compiler_params=LARGE,
        cost_estimate=cost(2 * 1024 * 1024 * 256, 3),
        name="weight_gradient",
    )(ids, grads, *own, *other)


def final_kernel(ids, in_ref, keep_ref, send_ref, total_ref):
    core = ids[2]
    total = in_ref[0].astype(F32)
    for i in range(1, 32):
        total += in_ref[i].astype(F32)
    total_ref[...] = total
    keep_ref[...] = total_ref[pl.ds(pl.multiple_of(core * 16, 16), 16), :]
    send_ref[...] = total_ref[pl.ds(pl.multiple_of((1 - core) * 16, 16), 16), :]


def final_call(ids, parts):
    return pl.pallas_call(
        final_kernel,
        grid_spec=pltpu.PrefetchScalarGridSpec(
            num_scalar_prefetch=1,
            grid=(1,),
            in_specs=[WHOLE],
            out_specs=[WHOLE] * 2,
            scratch_shapes=[pltpu.VMEM((32, HALF), F32)],
        ),
        out_shape=[shape(16, HALF, dtype=F32)] * 2,
        compiler_params=PARAMS,
        cost_estimate=cost(0, 0.5),
        name="weight_rows",
    )(ids, parts)


def shift_chips(block, distance):
    route = [(i - distance, i) for i in range(N_CHIP) if 0 <= i - distance < N_CHIP]
    return lax.ppermute(block, CHIP, route)


def shift_x(block, distance):
    return lax.ppermute(block, "x", [(i, (i + distance) % 4) for i in range(4)])


def swap_core(block):
    return lax.ppermute(block, "c", [(0, 1), (1, 0)])


def shards(query, key, value, grad, inputs, stretch_order, session_starts):
    query, key, value, grad, inputs = query[0], key[0], value[0], grad[0], inputs[0]
    core = lax.axis_index("c")
    ids = jnp.stack([lax.axis_index(CTX), lax.axis_index("x"), core]).astype(jnp.int32)

    key_other, value = lax.optimization_barrier((swap_core(key), value))
    (key0,) = pick_call(ids, key, key_other)
    key0, query, grad, value = lax.optimization_barrier((key0, query, grad, value))
    key1 = shift_chips(key0, 1)
    value0, last = pick_call(ids, value, swap_core(value), key0)
    far2 = shift_chips(last, 2)
    keys = [far2, key1, key0]
    bias, queries, grads = prepare_call(
        ids,
        stretch_order.reshape(-1),
        session_starts.reshape(-1),
        query,
        swap_core(query),
        grad,
        swap_core(grad),
    )
    bias, value0 = lax.optimization_barrier((bias, value0))
    values = [far2, shift_chips(value0, 1), value0]

    prob, value_own, value_t1, value_t2 = forward_call(bias, queries, grads, keys)
    value_r2 = shift_chips(value_t2, -2)
    value_r1 = shift_chips(value_t1, -1)
    query_keep, query_send, key_own, key_t1, key_t2 = backward_call(
        ids, prob, queries, grads, keys, values
    )
    inputs, query_send = lax.optimization_barrier((inputs, query_send))
    packed = pack_call(ids, inputs)
    own = [packed[0]] + [shift_x(packed[d], d) for d in range(1, 4)]
    other = [swap_core(block) for block in own]
    value_r1, query_send = lax.optimization_barrier((value_r1, query_send))
    value_keep, value_send, sent = total_call(ids, value_own, value_r1, value_r2, True)
    key_r2 = shift_chips(key_t2, -2)
    key_r1 = shift_chips(key_t1, -1)
    gathered = lax.all_to_all(sent, "x", 0, 0, tiled=True)
    partial = weight_call(ids, gathered, own, other)
    partial, key_r1, key_r2 = lax.optimization_barrier((partial, key_r1, key_r2))
    partial = lax.all_to_all(partial.reshape(32, 32, HALF), ("zl", "zh", "y"), 0, 0, tiled=True)

    key_keep, key_send = total_call(ids, key_own, key_r1, key_r2, False)
    grad_query, grad_key, grad_value = join_call(
        ids,
        [query_keep, key_keep, value_keep],
        [swap_core(query_send), swap_core(key_send), swap_core(value_send)],
        "join_outputs",
    )
    partial, grad_query = lax.optimization_barrier((partial, grad_query))
    row_keep, row_send = final_call(ids, partial)
    swapped = swap_core(row_send)
    first, second = jnp.where(core == 0, row_keep, swapped), jnp.where(core == 0, swapped, row_keep)
    weight_grad = jnp.concatenate([first, second], axis=1)
    return grad_query[None], grad_key[None], grad_value[None], weight_grad


def solution(mesh):
    fine = Mesh(mesh.devices.reshape(4, 2, 4, 4, 2), AXES)
    rows = P("zl", CTX, None)
    return jax.shard_map(
        shards,
        mesh=fine,
        in_specs=(rows, rows, rows, rows, rows, P("zl", None, None), P("zl", None)),
        out_specs=(rows, rows, rows, P(AXES, None)),
        check_vma=False,
    )
```

```python
import math

import jax
import jax.numpy as jnp
from jax import lax
from jax.experimental import pallas as pl
from jax.experimental.pallas import tpu as pltpu
from jax.sharding import Mesh, PartitionSpec as P

HEAD = 128
STRETCH = 64
SPAN = 4
PER_GROUP = 4
GROUPS = 2
ROWS = 128
KEYS = SPAN * ROWS
WIDE = PER_GROUP * HEAD
HALF = GROUPS * HEAD
MASKED = -1e30
SCALE = HEAD**-0.5
LOG2E = math.log2(math.e)
BF16 = jnp.bfloat16
F32 = jnp.float32
AXES = ("zl", "zh", "x", "y", "c")
CTX = ("zh", "x", "y", "c")
CHIP = ("zh", "x", "y")
N_CHIP = 32
NSTART = 64
MIB = 1024 * 1024
PARAMS = pltpu.CompilerParams(vmem_limit_bytes=8 * MIB)
LARGE = pltpu.CompilerParams(vmem_limit_bytes=24 * MIB)
WHOLE = pl.BlockSpec(memory_space=pltpu.VMEM)


def nt(a, b):
    return lax.dot_general(a, b, (((1,), (1,)), ((), ())), preferred_element_type=F32)


def tn(a, b):
    return lax.dot_general(a, b, (((0,), (0,)), ((), ())), preferred_element_type=F32)


def nn(a, b):
    return lax.dot_general(a, b, (((1,), (0,)), ((), ())), preferred_element_type=F32)


def shape(*dims, dtype=BF16):
    return jax.ShapeDtypeStruct(dims, dtype)


def cost(flops, mib):
    return pl.CostEstimate(flops=flops, bytes_accessed=int(mib * MIB), transcendentals=0)


def stack_heads(block):
    return jnp.concatenate([block[:, h * HEAD : (h + 1) * HEAD] for h in range(PER_GROUP)], axis=0)


def put_rows(out_ref, core, own, other):
    out_ref[pl.ds(pl.multiple_of(core * ROWS, ROWS), ROWS), :] = own[...]
    out_ref[pl.ds(pl.multiple_of((1 - core) * ROWS, ROWS), ROWS), :] = other[...]


def pick_keys_kernel(ids, own, other, both_ref):
    put_rows(both_ref, ids[2], own, other)


def pick_values_kernel(ids, own, other, keys, both_ref, last_ref):
    put_rows(both_ref, ids[2], own, other)
    last_ref[:, :HALF] = keys[ROWS:]
    last_ref[:, HALF:] = both_ref[ROWS:]


def pick_call(ids, own, other, keys=None):
    half = pl.BlockSpec((ROWS, HALF), lambda i, ids: (0, ids[2]))
    extra = [] if keys is None else [keys]
    return pl.pallas_call(
        pick_values_kernel if extra else pick_keys_kernel,
        grid_spec=pltpu.PrefetchScalarGridSpec(
            num_scalar_prefetch=1,
            grid=(1,),
            in_specs=[half] * 2 + [WHOLE] * len(extra),
            out_specs=[WHOLE] * (1 + len(extra)),
        ),
        out_shape=[shape(2 * ROWS, HALF)] + [shape(ROWS, 2 * HALF)] * len(extra),
        compiler_params=PARAMS,
        cost_estimate=cost(0, 0.5),
        name="pick_values" if extra else "pick_keys",
    )(ids, own, other, *extra)


def prepare_kernel(
    ids, order, starts, q_own, q_other, g_own, g_other, bias_ref, queries_ref, grads_ref
):
    put_rows(queries_ref, ids[2], q_own, q_other)
    put_rows(grads_ref, ids[2], g_own, g_other)
    base = ids[0] - ids[2]
    lane = lax.broadcasted_iota(jnp.int32, (1, ROWS), 1)
    row = lax.broadcasted_iota(jnp.int32, (STRETCH, ROWS), 0)
    for s in range(2):
        shard = base + s
        stretch = jnp.where(lane < STRETCH, order[2 * shard], order[2 * shard + 1])
        query_pos = shard * ROWS + stretch * STRETCH + (lane & (STRETCH - 1))
        begin = jnp.zeros((1, ROWS), jnp.int32)
        for i in range(NSTART):
            begin = jnp.where(starts[i] <= query_pos, starts[i], begin)
        for d in range(SPAN):
            source = shard - (SPAN - 1) + d
            known = jnp.maximum(source, 0)
            for j in range(2):
                key_pos = source * ROWS + order[2 * known + j] * STRETCH + row
                allowed = (key_pos <= query_pos) & (key_pos >= begin)
                bias_ref[s, (2 * d + j) * STRETCH : (2 * d + j + 1) * STRETCH, :] = jnp.where(
                    allowed, 0.0, MASKED
                )


def prepare_call(ids, order, starts, *blocks):
    half = pl.BlockSpec((ROWS, GROUPS * WIDE), lambda i, ids, *_: (0, ids[2]))
    return pl.pallas_call(
        prepare_kernel,
        grid_spec=pltpu.PrefetchScalarGridSpec(
            num_scalar_prefetch=3, grid=(1,), in_specs=[half] * 4, out_specs=[WHOLE] * 3
        ),
        out_shape=[shape(2, KEYS, ROWS, dtype=F32)] + [shape(2 * ROWS, GROUPS * WIDE)] * 2,
        compiler_params=PARAMS,
        cost_estimate=cost(0, 2.5),
        name="prepare",
    )(ids, order, starts, *blocks)


def spread(out, far1, far2, s0, s1):
    out[:ROWS] = s0[3 * ROWS :] + s1[2 * ROWS : 3 * ROWS]
    out[ROWS:] = s1[3 * ROWS :]
    far1[:ROWS] = (s0[ROWS : 2 * ROWS] + s1[:ROWS]).astype(BF16)
    far1[ROWS:] = (s0[2 * ROWS : 3 * ROWS] + s1[ROWS : 2 * ROWS]).astype(BF16)
    far2[...] = s0[:ROWS].astype(far2.dtype)


def forward_kernel(bias, q_ref, g_ref, k2, k1, k0, prob_ref, own_ref, far1, far2):
    keys = jnp.concatenate([k2[...], k1[...], k0[...]], axis=0)
    terms = []
    for s in range(2):
        rows = slice(s * ROWS, (s + 1) * ROWS)
        window = keys[s * ROWS : s * ROWS + KEYS]
        for h in range(PER_GROUP):
            cols = slice(h * HEAD, (h + 1) * HEAD)
            score = nt(window, q_ref[rows, cols]) * (SCALE * LOG2E) + bias[s]
            weight = jnp.exp2(score - jnp.max(score, axis=0, keepdims=True))
            total = jnp.sum(weight, axis=0, keepdims=True)
            prob_ref[0, s, :, cols] = (weight * (1.0 / total)).astype(BF16)
        terms.append(nn(prob_ref[0, s], stack_heads(g_ref[rows, :])))
    spread(own_ref, far1, far2, *terms)


def backward_kernel(
    ids,
    prob_ref,
    q_ref,
    g_ref,
    k2,
    k1,
    k0,
    v2,
    v1,
    v0,
    keep_ref,
    send_ref,
    own_ref,
    far1,
    far2,
    gq_ref,
):
    core = ids[2]
    keys = jnp.concatenate([k2[...], k1[...], k0[...]], axis=0)
    values = jnp.concatenate([v2[...], v1[...], v0[...]], axis=0)
    terms = []
    for s in range(2):
        rows = slice(s * ROWS, (s + 1) * ROWS)
        window = slice(s * ROWS, s * ROWS + KEYS)
        prob = prob_ref[0, s].astype(F32)
        weighted = prob * nt(values[window], stack_heads(g_ref[rows, :]))
        delta = jnp.sum(weighted, axis=0, keepdims=True)
        grad_score = (weighted - prob * delta).astype(BF16)
        terms.append(nn(grad_score, stack_heads(q_ref[rows, :])) * SCALE)
        query_grad = tn(grad_score, keys[window]) * SCALE
        for h in range(PER_GROUP):
            gq_ref[s, :, h * HEAD : (h + 1) * HEAD] = query_grad[h * ROWS : (h + 1) * ROWS].astype(
                BF16
            )
    spread(own_ref, far1, far2, *terms)
    keep_ref[...] = gq_ref[core]
    send_ref[...] = gq_ref[1 - core]


def narrow(rows, shift=0):
    return pl.BlockSpec((rows, HEAD), lambda j, *_: (0, j + shift))


def wide(rows):
    return pl.BlockSpec((rows, WIDE), lambda j, *_: (0, j))


WINDOW = [narrow(ROWS), narrow(2 * ROWS), narrow(2 * ROWS)]
VALUE_WINDOW = [narrow(ROWS, GROUPS)] + WINDOW[1:]
TERMS = [narrow(2 * ROWS), narrow(2 * ROWS), narrow(ROWS)]
PROB_SPEC = pl.BlockSpec((1, 2, KEYS, WIDE), lambda j, *_: (j, 0, 0, 0))


def term_shapes(last):
    return [shape(2 * ROWS, HALF, dtype=F32), shape(2 * ROWS, HALF), shape(ROWS, HALF, dtype=last)]


def forward_call(bias, queries, grads, keys):
    return pl.pallas_call(
        forward_kernel,
        grid=(GROUPS,),
        in_specs=[pl.BlockSpec((2, KEYS, ROWS), lambda j: (0, 0, 0))]
        + [wide(2 * ROWS)] * 2
        + WINDOW,
        out_specs=[PROB_SPEC] + TERMS,
        out_shape=[shape(GROUPS, 2, KEYS, WIDE)] + term_shapes(BF16),
        compiler_params=LARGE,
        cost_estimate=cost(4 * 16 * ROWS * KEYS * HEAD, 6),
        name="forward_and_value_gradient",
    )(bias, queries, grads, *keys)


def backward_call(ids, prob, queries, grads, keys, values):
    return pl.pallas_call(
        backward_kernel,
        grid_spec=pltpu.PrefetchScalarGridSpec(
            num_scalar_prefetch=1,
            grid=(GROUPS,),
            in_specs=[PROB_SPEC] + [wide(2 * ROWS)] * 2 + WINDOW + VALUE_WINDOW,
            out_specs=[wide(ROWS)] * 2 + TERMS,
            scratch_shapes=[pltpu.VMEM((2, ROWS, WIDE), BF16)],
        ),
        out_shape=[shape(ROWS, GROUPS * WIDE)] * 2 + term_shapes(BF16),
        compiler_params=LARGE,
        cost_estimate=cost(6 * 16 * ROWS * KEYS * HEAD, 6),
        name="query_and_key_gradient",
    )(ids, prob, queries, grads, *keys, *values)


def pack_kernel(ids, in_ref, o0, o1, o2, o3):
    for d, out_ref in enumerate((o0, o1, o2, o3)):
        x = (ids[1] + d) & 3
        for z in range(8):
            column = pl.multiple_of((4 * z + x) * HEAD, HEAD)
            out_ref[:, z * HEAD : (z + 1) * HEAD] = in_ref[:, pl.ds(column, HEAD)]


def pack_call(ids, inputs):
    return pl.pallas_call(
        pack_kernel,
        grid_spec=pltpu.PrefetchScalarGridSpec(
            num_scalar_prefetch=1, grid=(1,), in_specs=[WHOLE], out_specs=[WHOLE] * 4
        ),
        out_shape=[shape(ROWS, 8 * HEAD)] * 4,
        compiler_params=PARAMS,
        cost_estimate=cost(0, 2),
        name="pack_inputs",
    )(ids, inputs)


def add_terms(own, r1, r2):
    first = own[:ROWS] + r1[:ROWS].astype(F32)
    second = own[ROWS:] + r1[ROWS:].astype(F32) + r2[...].astype(F32)
    return first.astype(BF16), second.astype(BF16)


def value_total_kernel(ids, own, r1, r2, keep_ref, send_ref, copies_ref):
    core = ids[2]
    first, second = add_terms(own, r1, r2)
    for x in range(4):
        copies_ref[x, :ROWS], copies_ref[x, ROWS:] = first, second
    keep_ref[...] = copies_ref[0, pl.ds(pl.multiple_of(core * ROWS, ROWS), ROWS), :]
    send_ref[...] = copies_ref[0, pl.ds(pl.multiple_of((1 - core) * ROWS, ROWS), ROWS), :]


def key_total_kernel(ids, own, r1, r2, keep_ref, send_ref, both_ref):
    core = ids[2]
    both_ref[:ROWS], both_ref[ROWS:] = add_terms(own, r1, r2)
    keep_ref[...] = both_ref[pl.ds(pl.multiple_of(core * ROWS, ROWS), ROWS), :]
    send_ref[...] = both_ref[pl.ds(pl.multiple_of((1 - core) * ROWS, ROWS), ROWS), :]


def total_call(ids, own, r1, r2, copies):
    return pl.pallas_call(
        value_total_kernel if copies else key_total_kernel,
        grid_spec=pltpu.PrefetchScalarGridSpec(
            num_scalar_prefetch=1,
            grid=(1,),
            in_specs=[WHOLE] * 3,
            out_specs=[WHOLE] * (3 if copies else 2),
            scratch_shapes=[] if copies else [pltpu.VMEM((2 * ROWS, HALF), BF16)],
        ),
        out_shape=[shape(ROWS, HALF)] * 2 + ([shape(4, 2 * ROWS, HALF)] if copies else []),
        compiler_params=PARAMS,
        cost_estimate=cost(0, 1),
        name="value_gradient_total" if copies else "key_gradient_total",
    )(ids, own, r1, r2)


def join_kernel(ids, *refs):
    core = ids[2]
    count = len(refs) // 3
    for keep, other, out in zip(refs[:count], refs[count : 2 * count], refs[2 * count :]):
        width = keep.shape[1]
        out[:, pl.ds(pl.multiple_of(core * width, HEAD), width)] = keep[...]
        out[:, pl.ds(pl.multiple_of((1 - core) * width, HEAD), width)] = other[...]


def join_call(ids, keep, other, name):
    return pl.pallas_call(
        join_kernel,
        grid_spec=pltpu.PrefetchScalarGridSpec(
            num_scalar_prefetch=1,
            grid=(1,),
            in_specs=[WHOLE] * (2 * len(keep)),
            out_specs=[WHOLE] * len(keep),
        ),
        out_shape=[shape(a.shape[0], 2 * a.shape[1], dtype=a.dtype) for a in keep],
        compiler_params=PARAMS,
        cost_estimate=cost(0, 0.5),
        name=name,
    )(ids, *keep, *other)


def weight_kernel(ids, grads, a0, a1, a2, a3, b0, b1, b2, b3, out_ref):
    x, core = ids[1], ids[2]
    left = [ref[...] for ref in (a0, a1, a2, a3, b0, b1, b2, b3)]
    right = []
    for side in (core, 1 - core):
        rows = pl.ds(pl.multiple_of(side * ROWS, ROWS), ROWS)
        right += [grads[(x + 4 - d) & 3, rows, :] for d in range(4)]
    left, right = jnp.concatenate(left, axis=0), jnp.concatenate(right, axis=0)
    out_ref[...] = tn(left, right).astype(BF16)


def weight_call(ids, grads, own, other):
    taken = pl.BlockSpec((ROWS, 256), lambda i, _: (0, i))
    return pl.pallas_call(
        weight_kernel,
        grid_spec=pltpu.PrefetchScalarGridSpec(
            num_scalar_prefetch=1,
            grid=(4,),
            in_specs=[pl.BlockSpec((4, 2 * ROWS, HALF), lambda i, _: (0, 0, 0))] + [taken] * 8,
            out_specs=pl.BlockSpec((256, HALF), lambda i, _: (i, 0)),
        ),
        out_shape=shape(1024, HALF),
        compiler_params=LARGE,
        cost_estimate=cost(2 * 1024 * 1024 * 256, 3),
        name="weight_gradient",
    )(ids, grads, *own, *other)


def final_kernel(ids, in_ref, keep_ref, send_ref, total_ref):
    core = ids[2]
    total = in_ref[0].astype(F32)
    for i in range(1, 32):
        total += in_ref[i].astype(F32)
    total_ref[...] = total
    keep_ref[...] = total_ref[pl.ds(pl.multiple_of(core * 16, 16), 16), :]
    send_ref[...] = total_ref[pl.ds(pl.multiple_of((1 - core) * 16, 16), 16), :]


def final_call(ids, parts):
    return pl.pallas_call(
        final_kernel,
        grid_spec=pltpu.PrefetchScalarGridSpec(
            num_scalar_prefetch=1,
            grid=(1,),
            in_specs=[WHOLE],
            out_specs=[WHOLE] * 2,
            scratch_shapes=[pltpu.VMEM((32, HALF), F32)],
        ),
        out_shape=[shape(16, HALF, dtype=F32)] * 2,
        compiler_params=PARAMS,
        cost_estimate=cost(0, 0.5),
        name="weight_rows",
    )(ids, parts)


def shift_chips(block, distance):
    route = [(i - distance, i) for i in range(N_CHIP) if 0 <= i - distance < N_CHIP]
    return lax.ppermute(block, CHIP, route)


def shift_x(block, distance):
    return lax.ppermute(block, "x", [(i, (i + distance) % 4) for i in range(4)])


def swap_core(block):
    return lax.ppermute(block, "c", [(0, 1), (1, 0)])


def shards(query, key, value, grad, inputs, stretch_order, session_starts):
    query, key, value, grad, inputs = query[0], key[0], value[0], grad[0], inputs[0]
    core = lax.axis_index("c")
    ids = jnp.stack([lax.axis_index(CTX), lax.axis_index("x"), core]).astype(jnp.int32)

    key_other, value = lax.optimization_barrier((swap_core(key), value))
    (key0,) = pick_call(ids, key, key_other)
    key0, query, grad, value = lax.optimization_barrier((key0, query, grad, value))
    key1 = shift_chips(key0, 1)
    value0, last = pick_call(ids, value, swap_core(value), key0)
    far2 = shift_chips(last, 2)
    keys = [far2, key1, key0]
    bias, queries, grads = prepare_call(
        ids,
        stretch_order.reshape(-1),
        session_starts.reshape(-1),
        query,
        swap_core(query),
        grad,
        swap_core(grad),
    )

    bias, inputs = lax.optimization_barrier((bias, inputs))
    packed = pack_call(ids, inputs)
    own = [packed[0]] + [shift_x(packed[d], d) for d in range(1, 4)]

    prob, value_own, value_t1, value_t2 = forward_call(bias, queries, grads, keys)
    value_r2 = shift_chips(value_t2, -2)
    value_r1 = shift_chips(value_t1, -1)
    value_own, value0 = lax.optimization_barrier((value_own, value0))
    values = [far2, shift_chips(value0, 1), value0]
    prob, *far = lax.optimization_barrier((prob, *own[1:]))
    own = [own[0]] + far
    other = [swap_core(block) for block in own]
    query_keep, query_send, key_own, key_t1, key_t2 = backward_call(
        ids, prob, queries, grads, keys, values
    )
    value_r1, query_send = lax.optimization_barrier((value_r1, query_send))
    value_keep, value_send, sent = total_call(ids, value_own, value_r1, value_r2, True)
    key_r2 = shift_chips(key_t2, -2)
    key_r1 = shift_chips(key_t1, -1)
    gathered = lax.all_to_all(sent, "x", 0, 0, tiled=True)
    partial = weight_call(ids, gathered, own, other)
    partial, key_r1, key_r2 = lax.optimization_barrier((partial, key_r1, key_r2))
    partial = lax.all_to_all(partial.reshape(32, 32, HALF), ("zl", "zh", "y"), 0, 0, tiled=True)

    key_keep, key_send = total_call(ids, key_own, key_r1, key_r2, False)
    grad_query, grad_key, grad_value = join_call(
        ids,
        [query_keep, key_keep, value_keep],
        [swap_core(query_send), swap_core(key_send), swap_core(value_send)],
        "join_outputs",
    )
    partial, grad_query = lax.optimization_barrier((partial, grad_query))
    row_keep, row_send = final_call(ids, partial)
    swapped = swap_core(row_send)
    first, second = jnp.where(core == 0, row_keep, swapped), jnp.where(core == 0, swapped, row_keep)
    weight_grad = jnp.concatenate([first, second], axis=1)
    return grad_query[None], grad_key[None], grad_value[None], weight_grad


def solution(mesh):
    fine = Mesh(mesh.devices.reshape(4, 2, 4, 4, 2), AXES)
    rows = P("zl", CTX, None)
    return jax.shard_map(
        shards,
        mesh=fine,
        in_specs=(rows, rows, rows, rows, rows, P("zl", None, None), P("zl", None)),
        out_specs=(rows, rows, rows, P(AXES, None)),
        check_vma=False,
    )
```

```python
import math

import jax
import jax.numpy as jnp
from jax import lax
from jax.experimental import pallas as pl
from jax.experimental.pallas import tpu as pltpu
from jax.sharding import Mesh, PartitionSpec as P

HEAD = 128
STRETCH = 64
SPAN = 4
PER_GROUP = 4
GROUPS = 2
ROWS = 128
KEYS = SPAN * ROWS
WIDE = PER_GROUP * HEAD
HALF = GROUPS * HEAD
MASKED = -1e30
SCALE = HEAD**-0.5
LOG2E = math.log2(math.e)
BF16 = jnp.bfloat16
F32 = jnp.float32
AXES = ("zl", "zh", "x", "y", "c")
CTX = ("zh", "x", "y", "c")
CHIP = ("zh", "x", "y")
N_CHIP = 32
NSTART = 64
MIB = 1024 * 1024
PARAMS = pltpu.CompilerParams(vmem_limit_bytes=8 * MIB)
LARGE = pltpu.CompilerParams(vmem_limit_bytes=24 * MIB)
WHOLE = pl.BlockSpec(memory_space=pltpu.VMEM)


def nt(a, b):
    return lax.dot_general(a, b, (((1,), (1,)), ((), ())), preferred_element_type=F32)


def tn(a, b):
    return lax.dot_general(a, b, (((0,), (0,)), ((), ())), preferred_element_type=F32)


def nn(a, b):
    return lax.dot_general(a, b, (((1,), (0,)), ((), ())), preferred_element_type=F32)


def shape(*dims, dtype=BF16):
    return jax.ShapeDtypeStruct(dims, dtype)


def cost(flops, mib):
    return pl.CostEstimate(flops=flops, bytes_accessed=int(mib * MIB), transcendentals=0)


def stack_heads(block):
    return jnp.concatenate([block[:, h * HEAD : (h + 1) * HEAD] for h in range(PER_GROUP)], axis=0)


def put_rows(out_ref, core, own, other):
    out_ref[pl.ds(pl.multiple_of(core * ROWS, ROWS), ROWS), :] = own[...]
    out_ref[pl.ds(pl.multiple_of((1 - core) * ROWS, ROWS), ROWS), :] = other[...]


def pick_kernel(ids, k_own, k_other, v_own, v_other, both_ref, last_ref):
    put_rows(both_ref.at[:, :HALF], ids[2], k_own, k_other)
    put_rows(both_ref.at[:, HALF:], ids[2], v_own, v_other)
    last_ref[...] = both_ref[ROWS:]


def pick_call(ids, *blocks):
    half = pl.BlockSpec((ROWS, HALF), lambda i, ids: (0, ids[2]))
    return pl.pallas_call(
        pick_kernel,
        grid_spec=pltpu.PrefetchScalarGridSpec(
            num_scalar_prefetch=1, grid=(1,), in_specs=[half] * 4, out_specs=[WHOLE] * 2
        ),
        out_shape=[shape(2 * ROWS, 2 * HALF), shape(ROWS, 2 * HALF)],
        compiler_params=PARAMS,
        cost_estimate=cost(0, 0.5),
        name="pick_keys_and_values",
    )(ids, *blocks)


def prepare_kernel(
    ids, order, starts, q_own, q_other, g_own, g_other, bias_ref, queries_ref, grads_ref
):
    put_rows(queries_ref, ids[2], q_own, q_other)
    put_rows(grads_ref, ids[2], g_own, g_other)
    base = ids[0] - ids[2]
    lane = lax.broadcasted_iota(jnp.int32, (1, ROWS), 1)
    row = lax.broadcasted_iota(jnp.int32, (STRETCH, ROWS), 0)
    for s in range(2):
        shard = base + s
        stretch = jnp.where(lane < STRETCH, order[2 * shard], order[2 * shard + 1])
        query_pos = shard * ROWS + stretch * STRETCH + (lane & (STRETCH - 1))
        begin = jnp.zeros((1, ROWS), jnp.int32)
        for i in range(NSTART):
            begin = jnp.where(starts[i] <= query_pos, starts[i], begin)
        for d in range(SPAN):
            source = shard - (SPAN - 1) + d
            known = jnp.maximum(source, 0)
            for j in range(2):
                key_pos = source * ROWS + order[2 * known + j] * STRETCH + row
                allowed = (key_pos <= query_pos) & (key_pos >= begin)
                bias_ref[s, (2 * d + j) * STRETCH : (2 * d + j + 1) * STRETCH, :] = jnp.where(
                    allowed, 0.0, MASKED
                )


def prepare_call(ids, order, starts, *blocks):
    half = pl.BlockSpec((ROWS, GROUPS * WIDE), lambda i, ids, *_: (0, ids[2]))
    return pl.pallas_call(
        prepare_kernel,
        grid_spec=pltpu.PrefetchScalarGridSpec(
            num_scalar_prefetch=3, grid=(1,), in_specs=[half] * 4, out_specs=[WHOLE] * 3
        ),
        out_shape=[shape(2, KEYS, ROWS, dtype=F32)] + [shape(2 * ROWS, GROUPS * WIDE)] * 2,
        compiler_params=PARAMS,
        cost_estimate=cost(0, 2.5),
        name="prepare",
    )(ids, order, starts, *blocks)


def spread(out, far1, far2, s0, s1):
    out[:ROWS] = s0[3 * ROWS :] + s1[2 * ROWS : 3 * ROWS]
    out[ROWS:] = s1[3 * ROWS :]
    far1[:ROWS] = (s0[ROWS : 2 * ROWS] + s1[:ROWS]).astype(BF16)
    far1[ROWS:] = (s0[2 * ROWS : 3 * ROWS] + s1[ROWS : 2 * ROWS]).astype(BF16)
    far2[...] = s0[:ROWS].astype(far2.dtype)


def forward_kernel(bias, q_ref, g_ref, k2, k1, k0, prob_ref, own_ref, far1, far2):
    keys = jnp.concatenate([k2[...], k1[...], k0[...]], axis=0)
    terms = []
    for s in range(2):
        rows = slice(s * ROWS, (s + 1) * ROWS)
        window = keys[s * ROWS : s * ROWS + KEYS]
        for h in range(PER_GROUP):
            cols = slice(h * HEAD, (h + 1) * HEAD)
            score = nt(window, q_ref[rows, cols]) * (SCALE * LOG2E) + bias[s]
            weight = jnp.exp2(score - jnp.max(score, axis=0, keepdims=True))
            total = jnp.sum(weight, axis=0, keepdims=True)
            prob_ref[0, s, :, cols] = (weight * (1.0 / total)).astype(BF16)
        terms.append(nn(prob_ref[0, s], stack_heads(g_ref[rows, :])))
    spread(own_ref, far1, far2, *terms)


def backward_kernel(
    ids,
    prob_ref,
    q_ref,
    g_ref,
    k2,
    k1,
    k0,
    v2,
    v1,
    v0,
    keep_ref,
    send_ref,
    own_ref,
    far1,
    far2,
    gq_ref,
):
    core = ids[2]
    keys = jnp.concatenate([k2[...], k1[...], k0[...]], axis=0)
    values = jnp.concatenate([v2[...], v1[...], v0[...]], axis=0)
    terms = []
    for s in range(2):
        rows = slice(s * ROWS, (s + 1) * ROWS)
        window = slice(s * ROWS, s * ROWS + KEYS)
        prob = prob_ref[0, s].astype(F32)
        weighted = prob * nt(values[window], stack_heads(g_ref[rows, :]))
        delta = jnp.sum(weighted, axis=0, keepdims=True)
        grad_score = (weighted - prob * delta).astype(BF16)
        terms.append(nn(grad_score, stack_heads(q_ref[rows, :])) * SCALE)
        query_grad = tn(grad_score, keys[window]) * SCALE
        for h in range(PER_GROUP):
            gq_ref[s, :, h * HEAD : (h + 1) * HEAD] = query_grad[h * ROWS : (h + 1) * ROWS].astype(
                BF16
            )
    spread(own_ref, far1, far2, *terms)
    keep_ref[...] = gq_ref[core]
    send_ref[...] = gq_ref[1 - core]


def narrow(rows, shift=0):
    return pl.BlockSpec((rows, HEAD), lambda j, *_: (0, j + shift))


def wide(rows):
    return pl.BlockSpec((rows, WIDE), lambda j, *_: (0, j))


WINDOW = [narrow(ROWS), narrow(2 * ROWS), narrow(2 * ROWS)]
VALUE_WINDOW = [narrow(ROWS, GROUPS), narrow(2 * ROWS, GROUPS), narrow(2 * ROWS, GROUPS)]
TERMS = [narrow(2 * ROWS), narrow(2 * ROWS), narrow(ROWS)]
PROB_SPEC = pl.BlockSpec((1, 2, KEYS, WIDE), lambda j, *_: (j, 0, 0, 0))


def term_shapes(last):
    return [shape(2 * ROWS, HALF, dtype=F32), shape(2 * ROWS, HALF), shape(ROWS, HALF, dtype=last)]


def forward_call(bias, queries, grads, blocks):
    return pl.pallas_call(
        forward_kernel,
        grid=(GROUPS,),
        in_specs=[pl.BlockSpec((2, KEYS, ROWS), lambda j: (0, 0, 0))]
        + [wide(2 * ROWS)] * 2
        + WINDOW,
        out_specs=[PROB_SPEC] + TERMS,
        out_shape=[shape(GROUPS, 2, KEYS, WIDE)] + term_shapes(BF16),
        compiler_params=LARGE,
        cost_estimate=cost(4 * 16 * ROWS * KEYS * HEAD, 6),
        name="forward_and_value_gradient",
    )(bias, queries, grads, *blocks)


def backward_call(ids, prob, queries, grads, blocks):
    return pl.pallas_call(
        backward_kernel,
        grid_spec=pltpu.PrefetchScalarGridSpec(
            num_scalar_prefetch=1,
            grid=(GROUPS,),
            in_specs=[PROB_SPEC] + [wide(2 * ROWS)] * 2 + WINDOW + VALUE_WINDOW,
            out_specs=[wide(ROWS)] * 2 + TERMS,
            scratch_shapes=[pltpu.VMEM((2, ROWS, WIDE), BF16)],
        ),
        out_shape=[shape(ROWS, GROUPS * WIDE)] * 2 + term_shapes(BF16),
        compiler_params=LARGE,
        cost_estimate=cost(6 * 16 * ROWS * KEYS * HEAD, 6),
        name="query_and_key_gradient",
    )(ids, prob, queries, grads, *blocks, *blocks)


def pack_kernel(ids, in_ref, o0, o1, o2, o3):
    for d, out_ref in enumerate((o0, o1, o2, o3)):
        x = (ids[1] + d) & 3
        for z in range(8):
            column = pl.multiple_of((4 * z + x) * HEAD, HEAD)
            out_ref[:, z * HEAD : (z + 1) * HEAD] = in_ref[:, pl.ds(column, HEAD)]


def pack_call(ids, inputs):
    return pl.pallas_call(
        pack_kernel,
        grid_spec=pltpu.PrefetchScalarGridSpec(
            num_scalar_prefetch=1, grid=(1,), in_specs=[WHOLE], out_specs=[WHOLE] * 4
        ),
        out_shape=[shape(ROWS, 8 * HEAD)] * 4,
        compiler_params=PARAMS,
        cost_estimate=cost(0, 2),
        name="pack_inputs",
    )(ids, inputs)


def add_terms(own, r1, r2):
    first = own[:ROWS] + r1[:ROWS].astype(F32)
    second = own[ROWS:] + r1[ROWS:].astype(F32) + r2[...].astype(F32)
    return first.astype(BF16), second.astype(BF16)


def value_total_kernel(ids, own, r1, r2, keep_ref, send_ref, copies_ref):
    core = ids[2]
    first, second = add_terms(own, r1, r2)
    for x in range(4):
        copies_ref[x, :ROWS], copies_ref[x, ROWS:] = first, second
    keep_ref[...] = copies_ref[0, pl.ds(pl.multiple_of(core * ROWS, ROWS), ROWS), :]
    send_ref[...] = copies_ref[0, pl.ds(pl.multiple_of((1 - core) * ROWS, ROWS), ROWS), :]


def key_total_kernel(ids, own, r1, r2, keep_ref, send_ref, both_ref):
    core = ids[2]
    both_ref[:ROWS], both_ref[ROWS:] = add_terms(own, r1, r2)
    keep_ref[...] = both_ref[pl.ds(pl.multiple_of(core * ROWS, ROWS), ROWS), :]
    send_ref[...] = both_ref[pl.ds(pl.multiple_of((1 - core) * ROWS, ROWS), ROWS), :]


def total_call(ids, own, r1, r2, copies):
    return pl.pallas_call(
        value_total_kernel if copies else key_total_kernel,
        grid_spec=pltpu.PrefetchScalarGridSpec(
            num_scalar_prefetch=1,
            grid=(1,),
            in_specs=[WHOLE] * 3,
            out_specs=[WHOLE] * (3 if copies else 2),
            scratch_shapes=[] if copies else [pltpu.VMEM((2 * ROWS, HALF), BF16)],
        ),
        out_shape=[shape(ROWS, HALF)] * 2 + ([shape(4, 2 * ROWS, HALF)] if copies else []),
        compiler_params=PARAMS,
        cost_estimate=cost(0, 1),
        name="value_gradient_total" if copies else "key_gradient_total",
    )(ids, own, r1, r2)


def join_kernel(ids, *refs):
    core = ids[2]
    count = len(refs) // 3
    for keep, other, out in zip(refs[:count], refs[count : 2 * count], refs[2 * count :]):
        width = keep.shape[1]
        out[:, pl.ds(pl.multiple_of(core * width, HEAD), width)] = keep[...]
        out[:, pl.ds(pl.multiple_of((1 - core) * width, HEAD), width)] = other[...]


def join_call(ids, keep, other, name):
    return pl.pallas_call(
        join_kernel,
        grid_spec=pltpu.PrefetchScalarGridSpec(
            num_scalar_prefetch=1,
            grid=(1,),
            in_specs=[WHOLE] * (2 * len(keep)),
            out_specs=[WHOLE] * len(keep),
        ),
        out_shape=[shape(a.shape[0], 2 * a.shape[1], dtype=a.dtype) for a in keep],
        compiler_params=PARAMS,
        cost_estimate=cost(0, 0.5),
        name=name,
    )(ids, *keep, *other)


def weight_kernel(ids, grads, a0, a1, a2, a3, b0, b1, b2, b3, out_ref):
    x, core = ids[1], ids[2]
    left = [ref[...] for ref in (a0, a1, a2, a3, b0, b1, b2, b3)]
    right = []
    for side in (core, 1 - core):
        rows = pl.ds(pl.multiple_of(side * ROWS, ROWS), ROWS)
        right += [grads[(x + 4 - d) & 3, rows, :] for d in range(4)]
    left, right = jnp.concatenate(left, axis=0), jnp.concatenate(right, axis=0)
    out_ref[...] = tn(left, right).astype(BF16)


def weight_call(ids, grads, own, other):
    taken = pl.BlockSpec((ROWS, 256), lambda i, _: (0, i))
    return pl.pallas_call(
        weight_kernel,
        grid_spec=pltpu.PrefetchScalarGridSpec(
            num_scalar_prefetch=1,
            grid=(4,),
            in_specs=[pl.BlockSpec((4, 2 * ROWS, HALF), lambda i, _: (0, 0, 0))] + [taken] * 8,
            out_specs=pl.BlockSpec((256, HALF), lambda i, _: (i, 0)),
        ),
        out_shape=shape(1024, HALF),
        compiler_params=LARGE,
        cost_estimate=cost(2 * 1024 * 1024 * 256, 3),
        name="weight_gradient",
    )(ids, grads, *own, *other)


def final_kernel(ids, in_ref, keep_ref, send_ref, total_ref):
    core = ids[2]
    total = in_ref[0].astype(F32)
    for i in range(1, 32):
        total += in_ref[i].astype(F32)
    total_ref[...] = total
    keep_ref[...] = total_ref[pl.ds(pl.multiple_of(core * 16, 16), 16), :]
    send_ref[...] = total_ref[pl.ds(pl.multiple_of((1 - core) * 16, 16), 16), :]


def final_call(ids, parts):
    return pl.pallas_call(
        final_kernel,
        grid_spec=pltpu.PrefetchScalarGridSpec(
            num_scalar_prefetch=1,
            grid=(1,),
            in_specs=[WHOLE],
            out_specs=[WHOLE] * 2,
            scratch_shapes=[pltpu.VMEM((32, HALF), F32)],
        ),
        out_shape=[shape(16, HALF, dtype=F32)] * 2,
        compiler_params=PARAMS,
        cost_estimate=cost(0, 0.5),
        name="weight_rows",
    )(ids, parts)


def shift_chips(block, distance):
    route = [(i - distance, i) for i in range(N_CHIP) if 0 <= i - distance < N_CHIP]
    return lax.ppermute(block, CHIP, route)


def shift_x(block, distance):
    return lax.ppermute(block, "x", [(i, (i + distance) % 4) for i in range(4)])


def swap_core(block):
    return lax.ppermute(block, "c", [(0, 1), (1, 0)])


def shards(query, key, value, grad, inputs, stretch_order, session_starts):
    query, key, value, grad, inputs = query[0], key[0], value[0], grad[0], inputs[0]
    core = lax.axis_index("c")
    ids = jnp.stack([lax.axis_index(CTX), lax.axis_index("x"), core]).astype(jnp.int32)

    key_other, value_other = swap_core(key), swap_core(value)
    both, last = pick_call(ids, key, key_other, value, value_other)
    blocks = [shift_chips(last, 2), shift_chips(both, 1), both]
    bias, queries, grads = prepare_call(
        ids,
        stretch_order.reshape(-1),
        session_starts.reshape(-1),
        query,
        swap_core(query),
        grad,
        swap_core(grad),
    )

    bias, inputs = lax.optimization_barrier((bias, inputs))
    packed = pack_call(ids, inputs)
    own = [packed[0]] + [shift_x(packed[d], d) for d in range(1, 4)]

    prob, value_own, value_t1, value_t2 = forward_call(bias, queries, grads, blocks)
    value_r2 = shift_chips(value_t2, -2)
    value_r1 = shift_chips(value_t1, -1)
    query_keep, query_send, key_own, key_t1, key_t2 = backward_call(
        ids, prob, queries, grads, blocks
    )
    value_r1, query_send, *far = lax.optimization_barrier((value_r1, query_send, *own[1:]))
    own = [own[0]] + far
    other = [swap_core(block) for block in own]
    value_keep, value_send, sent = total_call(ids, value_own, value_r1, value_r2, True)
    key_r2 = shift_chips(key_t2, -2)
    key_r1 = shift_chips(key_t1, -1)
    gathered = lax.all_to_all(sent, "x", 0, 0, tiled=True)
    partial = weight_call(ids, gathered, own, other)
    partial, key_r1, key_r2 = lax.optimization_barrier((partial, key_r1, key_r2))
    partial = lax.all_to_all(partial.reshape(32, 32, HALF), ("zl", "zh", "y"), 0, 0, tiled=True)

    key_keep, key_send = total_call(ids, key_own, key_r1, key_r2, False)
    grad_query, grad_key, grad_value = join_call(
        ids,
        [query_keep, key_keep, value_keep],
        [swap_core(query_send), swap_core(key_send), swap_core(value_send)],
        "join_outputs",
    )
    partial, grad_query = lax.optimization_barrier((partial, grad_query))
    row_keep, row_send = final_call(ids, partial)
    swapped = swap_core(row_send)
    first, second = jnp.where(core == 0, row_keep, swapped), jnp.where(core == 0, swapped, row_keep)
    weight_grad = jnp.concatenate([first, second], axis=1)
    return grad_query[None], grad_key[None], grad_value[None], weight_grad


def solution(mesh):
    fine = Mesh(mesh.devices.reshape(4, 2, 4, 4, 2), AXES)
    rows = P("zl", CTX, None)
    return jax.shard_map(
        shards,
        mesh=fine,
        in_specs=(rows, rows, rows, rows, rows, P("zl", None, None), P("zl", None)),
        out_specs=(rows, rows, rows, P(AXES, None)),
        check_vma=False,
    )
```

```python
import math

import jax
import jax.numpy as jnp
from jax import lax
from jax.experimental import pallas as pl
from jax.experimental.pallas import tpu as pltpu
from jax.sharding import Mesh, PartitionSpec as P

HEAD = 128
STRETCH = 64
SPAN = 4
PER_GROUP = 4
GROUPS = 2
ROWS = 128
KEYS = SPAN * ROWS
WIDE = PER_GROUP * HEAD
HALF = GROUPS * HEAD
MASKED = -1e30
SCALE = HEAD**-0.5
LOG2E = math.log2(math.e)
BF16 = jnp.bfloat16
F32 = jnp.float32
AXES = ("zl", "zh", "x", "y", "c")
CTX = ("zh", "x", "y", "c")
CHIP = ("zh", "x", "y")
N_CHIP = 32
NSTART = 64
MIB = 1024 * 1024
PARAMS = pltpu.CompilerParams(vmem_limit_bytes=8 * MIB)
LARGE = pltpu.CompilerParams(vmem_limit_bytes=24 * MIB)
WHOLE = pl.BlockSpec(memory_space=pltpu.VMEM)


def nt(a, b):
    return lax.dot_general(a, b, (((1,), (1,)), ((), ())), preferred_element_type=F32)


def tn(a, b):
    return lax.dot_general(a, b, (((0,), (0,)), ((), ())), preferred_element_type=F32)


def nn(a, b):
    return lax.dot_general(a, b, (((1,), (0,)), ((), ())), preferred_element_type=F32)


def shape(*dims, dtype=BF16):
    return jax.ShapeDtypeStruct(dims, dtype)


def cost(flops, mib):
    return pl.CostEstimate(flops=flops, bytes_accessed=int(mib * MIB), transcendentals=0)


def stack_heads(block):
    return jnp.concatenate([block[:, h * HEAD : (h + 1) * HEAD] for h in range(PER_GROUP)], axis=0)


def put_rows(out_ref, core, own, other):
    out_ref[pl.ds(pl.multiple_of(core * ROWS, ROWS), ROWS), :] = own[...]
    out_ref[pl.ds(pl.multiple_of((1 - core) * ROWS, ROWS), ROWS), :] = other[...]


def pick_keys_kernel(ids, own, other, both_ref):
    put_rows(both_ref, ids[2], own, other)


def pick_values_kernel(ids, own, other, keys, both_ref, last_ref):
    put_rows(both_ref, ids[2], own, other)
    last_ref[:, :HALF] = keys[ROWS:]
    last_ref[:, HALF:] = both_ref[ROWS:]


def pick_call(ids, own, other, keys=None):
    half = pl.BlockSpec((ROWS, HALF), lambda i, ids: (0, ids[2]))
    extra = [] if keys is None else [keys]
    return pl.pallas_call(
        pick_values_kernel if extra else pick_keys_kernel,
        grid_spec=pltpu.PrefetchScalarGridSpec(
            num_scalar_prefetch=1,
            grid=(1,),
            in_specs=[half] * 2 + [WHOLE] * len(extra),
            out_specs=[WHOLE] * (1 + len(extra)),
        ),
        out_shape=[shape(2 * ROWS, HALF)] + [shape(ROWS, 2 * HALF)] * len(extra),
        compiler_params=PARAMS,
        cost_estimate=cost(0, 0.5),
        name="pick_values" if extra else "pick_keys",
    )(ids, own, other, *extra)


def prepare_kernel(
    ids, order, starts, q_own, q_other, g_own, g_other, bias_ref, queries_ref, grads_ref
):
    put_rows(queries_ref, ids[2], q_own, q_other)
    put_rows(grads_ref, ids[2], g_own, g_other)
    base = ids[0] - ids[2]
    lane = lax.broadcasted_iota(jnp.int32, (1, ROWS), 1)
    row = lax.broadcasted_iota(jnp.int32, (STRETCH, ROWS), 0)
    for s in range(2):
        shard = base + s
        stretch = jnp.where(lane < STRETCH, order[2 * shard], order[2 * shard + 1])
        query_pos = shard * ROWS + stretch * STRETCH + (lane & (STRETCH - 1))
        begin = jnp.zeros((1, ROWS), jnp.int32)
        for i in range(NSTART):
            begin = jnp.where(starts[i] <= query_pos, starts[i], begin)
        for d in range(SPAN):
            source = shard - (SPAN - 1) + d
            known = jnp.maximum(source, 0)
            for j in range(2):
                key_pos = source * ROWS + order[2 * known + j] * STRETCH + row
                allowed = (key_pos <= query_pos) & (key_pos >= begin)
                bias_ref[s, (2 * d + j) * STRETCH : (2 * d + j + 1) * STRETCH, :] = jnp.where(
                    allowed, 0.0, MASKED
                )


def prepare_call(ids, order, starts, *blocks):
    half = pl.BlockSpec((ROWS, GROUPS * WIDE), lambda i, ids, *_: (0, ids[2]))
    return pl.pallas_call(
        prepare_kernel,
        grid_spec=pltpu.PrefetchScalarGridSpec(
            num_scalar_prefetch=3, grid=(1,), in_specs=[half] * 4, out_specs=[WHOLE] * 3
        ),
        out_shape=[shape(2, KEYS, ROWS, dtype=F32)] + [shape(2 * ROWS, GROUPS * WIDE)] * 2,
        compiler_params=PARAMS,
        cost_estimate=cost(0, 2.5),
        name="prepare",
    )(ids, order, starts, *blocks)


def spread(out, far1, far2, s0, s1):
    out[:ROWS] = s0[3 * ROWS :] + s1[2 * ROWS : 3 * ROWS]
    out[ROWS:] = s1[3 * ROWS :]
    far1[:ROWS] = (s0[ROWS : 2 * ROWS] + s1[:ROWS]).astype(BF16)
    far1[ROWS:] = (s0[2 * ROWS : 3 * ROWS] + s1[ROWS : 2 * ROWS]).astype(BF16)
    far2[...] = s0[:ROWS].astype(far2.dtype)


def forward_kernel(bias, q_ref, g_ref, k2, k1, k0, prob_ref, own_ref, far1, far2):
    keys = jnp.concatenate([k2[...], k1[...], k0[...]], axis=0)
    terms = []
    for s in range(2):
        rows = slice(s * ROWS, (s + 1) * ROWS)
        window = keys[s * ROWS : s * ROWS + KEYS]
        for h in range(PER_GROUP):
            cols = slice(h * HEAD, (h + 1) * HEAD)
            score = nt(window, q_ref[rows, cols]) * (SCALE * LOG2E) + bias[s]
            weight = jnp.exp2(score - jnp.max(score, axis=0, keepdims=True))
            total = jnp.sum(weight, axis=0, keepdims=True)
            prob_ref[0, s, :, cols] = (weight * (1.0 / total)).astype(BF16)
        terms.append(nn(prob_ref[0, s], stack_heads(g_ref[rows, :])))
    spread(own_ref, far1, far2, *terms)


def backward_kernel(
    ids,
    prob_ref,
    q_ref,
    g_ref,
    k2,
    k1,
    k0,
    v2,
    v1,
    v0,
    keep_ref,
    send_ref,
    own_ref,
    far1,
    far2,
    gq_ref,
):
    core = ids[2]
    keys = jnp.concatenate([k2[...], k1[...], k0[...]], axis=0)
    values = jnp.concatenate([v2[...], v1[...], v0[...]], axis=0)
    terms = []
    for s in range(2):
        rows = slice(s * ROWS, (s + 1) * ROWS)
        window = slice(s * ROWS, s * ROWS + KEYS)
        prob = prob_ref[0, s].astype(F32)
        weighted = prob * nt(values[window], stack_heads(g_ref[rows, :]))
        delta = jnp.sum(weighted, axis=0, keepdims=True)
        grad_score = (weighted - prob * delta).astype(BF16)
        terms.append(nn(grad_score, stack_heads(q_ref[rows, :])) * SCALE)
        query_grad = tn(grad_score, keys[window]) * SCALE
        for h in range(PER_GROUP):
            gq_ref[s, :, h * HEAD : (h + 1) * HEAD] = query_grad[h * ROWS : (h + 1) * ROWS].astype(
                BF16
            )
    spread(own_ref, far1, far2, *terms)
    keep_ref[...] = gq_ref[core]
    send_ref[...] = gq_ref[1 - core]


def narrow(rows, shift=0):
    return pl.BlockSpec((rows, HEAD), lambda j, *_: (0, j + shift))


def wide(rows):
    return pl.BlockSpec((rows, WIDE), lambda j, *_: (0, j))


WINDOW = [narrow(ROWS), narrow(2 * ROWS), narrow(2 * ROWS)]
VALUE_WINDOW = [narrow(ROWS, GROUPS)] + WINDOW[1:]
TERMS = [narrow(2 * ROWS), narrow(2 * ROWS), narrow(ROWS)]
PROB_SPEC = pl.BlockSpec((1, 2, KEYS, WIDE), lambda j, *_: (j, 0, 0, 0))


def term_shapes(last):
    return [shape(2 * ROWS, HALF, dtype=F32), shape(2 * ROWS, HALF), shape(ROWS, HALF, dtype=last)]


def forward_call(bias, queries, grads, keys):
    return pl.pallas_call(
        forward_kernel,
        grid=(GROUPS,),
        in_specs=[pl.BlockSpec((2, KEYS, ROWS), lambda j: (0, 0, 0))]
        + [wide(2 * ROWS)] * 2
        + WINDOW,
        out_specs=[PROB_SPEC] + TERMS,
        out_shape=[shape(GROUPS, 2, KEYS, WIDE)] + term_shapes(BF16),
        compiler_params=LARGE,
        cost_estimate=cost(4 * 16 * ROWS * KEYS * HEAD, 6),
        name="forward_and_value_gradient",
    )(bias, queries, grads, *keys)


def backward_call(ids, prob, queries, grads, keys, values):
    return pl.pallas_call(
        backward_kernel,
        grid_spec=pltpu.PrefetchScalarGridSpec(
            num_scalar_prefetch=1,
            grid=(GROUPS,),
            in_specs=[PROB_SPEC] + [wide(2 * ROWS)] * 2 + WINDOW + VALUE_WINDOW,
            out_specs=[wide(ROWS)] * 2 + TERMS,
            scratch_shapes=[pltpu.VMEM((2, ROWS, WIDE), BF16)],
        ),
        out_shape=[shape(ROWS, GROUPS * WIDE)] * 2 + term_shapes(BF16),
        compiler_params=LARGE,
        cost_estimate=cost(6 * 16 * ROWS * KEYS * HEAD, 6),
        name="query_and_key_gradient",
    )(ids, prob, queries, grads, *keys, *values)


def pack_kernel(ids, in_ref, o0, o1, o2, o3):
    for d, out_ref in enumerate((o0, o1, o2, o3)):
        x = (ids[1] + d) & 3
        for z in range(8):
            column = pl.multiple_of((4 * z + x) * HEAD, HEAD)
            out_ref[:, z * HEAD : (z + 1) * HEAD] = in_ref[:, pl.ds(column, HEAD)]


def pack_call(ids, inputs):
    return pl.pallas_call(
        pack_kernel,
        grid_spec=pltpu.PrefetchScalarGridSpec(
            num_scalar_prefetch=1, grid=(1,), in_specs=[WHOLE], out_specs=[WHOLE] * 4
        ),
        out_shape=[shape(ROWS, 8 * HEAD)] * 4,
        compiler_params=PARAMS,
        cost_estimate=cost(0, 2),
        name="pack_inputs",
    )(ids, inputs)


def add_terms(own, r1, r2):
    first = own[:ROWS] + r1[:ROWS].astype(F32)
    second = own[ROWS:] + r1[ROWS:].astype(F32) + r2[...].astype(F32)
    return first.astype(BF16), second.astype(BF16)


def value_total_kernel(ids, own, r1, r2, keep_ref, send_ref, copies_ref):
    core = ids[2]
    first, second = add_terms(own, r1, r2)
    for x in range(4):
        copies_ref[x, :ROWS], copies_ref[x, ROWS:] = first, second
    keep_ref[...] = copies_ref[0, pl.ds(pl.multiple_of(core * ROWS, ROWS), ROWS), :]
    send_ref[...] = copies_ref[0, pl.ds(pl.multiple_of((1 - core) * ROWS, ROWS), ROWS), :]


def key_total_kernel(ids, own, r1, r2, keep_ref, send_ref, both_ref):
    core = ids[2]
    both_ref[:ROWS], both_ref[ROWS:] = add_terms(own, r1, r2)
    keep_ref[...] = both_ref[pl.ds(pl.multiple_of(core * ROWS, ROWS), ROWS), :]
    send_ref[...] = both_ref[pl.ds(pl.multiple_of((1 - core) * ROWS, ROWS), ROWS), :]


def total_call(ids, own, r1, r2, copies):
    return pl.pallas_call(
        value_total_kernel if copies else key_total_kernel,
        grid_spec=pltpu.PrefetchScalarGridSpec(
            num_scalar_prefetch=1,
            grid=(1,),
            in_specs=[WHOLE] * 3,
            out_specs=[WHOLE] * (3 if copies else 2),
            scratch_shapes=[] if copies else [pltpu.VMEM((2 * ROWS, HALF), BF16)],
        ),
        out_shape=[shape(ROWS, HALF)] * 2 + ([shape(4, 2 * ROWS, HALF)] if copies else []),
        compiler_params=PARAMS,
        cost_estimate=cost(0, 1),
        name="value_gradient_total" if copies else "key_gradient_total",
    )(ids, own, r1, r2)


def join_kernel(ids, *refs):
    core = ids[2]
    count = len(refs) // 3
    for keep, other, out in zip(refs[:count], refs[count : 2 * count], refs[2 * count :]):
        width = keep.shape[1]
        out[:, pl.ds(pl.multiple_of(core * width, HEAD), width)] = keep[...]
        out[:, pl.ds(pl.multiple_of((1 - core) * width, HEAD), width)] = other[...]


def join_call(ids, keep, other, name):
    return pl.pallas_call(
        join_kernel,
        grid_spec=pltpu.PrefetchScalarGridSpec(
            num_scalar_prefetch=1,
            grid=(1,),
            in_specs=[WHOLE] * (2 * len(keep)),
            out_specs=[WHOLE] * len(keep),
        ),
        out_shape=[shape(a.shape[0], 2 * a.shape[1], dtype=a.dtype) for a in keep],
        compiler_params=PARAMS,
        cost_estimate=cost(0, 0.5),
        name=name,
    )(ids, *keep, *other)


def weight_kernel(ids, grads, a0, a1, a2, a3, b0, b1, b2, b3, out_ref):
    x, core = ids[1], ids[2]
    left = [ref[...] for ref in (a0, a1, a2, a3, b0, b1, b2, b3)]
    right = []
    for side in (core, 1 - core):
        rows = pl.ds(pl.multiple_of(side * ROWS, ROWS), ROWS)
        right += [grads[(x + 4 - d) & 3, rows, :] for d in range(4)]
    left, right = jnp.concatenate(left, axis=0), jnp.concatenate(right, axis=0)
    out_ref[...] = tn(left, right).astype(BF16)


def weight_call(ids, grads, own, other):
    taken = pl.BlockSpec((ROWS, 256), lambda i, _: (0, i))
    return pl.pallas_call(
        weight_kernel,
        grid_spec=pltpu.PrefetchScalarGridSpec(
            num_scalar_prefetch=1,
            grid=(4,),
            in_specs=[pl.BlockSpec((4, 2 * ROWS, HALF), lambda i, _: (0, 0, 0))] + [taken] * 8,
            out_specs=pl.BlockSpec((256, HALF), lambda i, _: (i, 0)),
        ),
        out_shape=shape(1024, HALF),
        compiler_params=LARGE,
        cost_estimate=cost(2 * 1024 * 1024 * 256, 3),
        name="weight_gradient",
    )(ids, grads, *own, *other)


def final_kernel(ids, in_ref, keep_ref, send_ref, total_ref):
    core = ids[2]
    total = in_ref[0].astype(F32)
    for i in range(1, 32):
        total += in_ref[i].astype(F32)
    total_ref[...] = total
    keep_ref[...] = total_ref[pl.ds(pl.multiple_of(core * 16, 16), 16), :]
    send_ref[...] = total_ref[pl.ds(pl.multiple_of((1 - core) * 16, 16), 16), :]


def final_call(ids, parts):
    return pl.pallas_call(
        final_kernel,
        grid_spec=pltpu.PrefetchScalarGridSpec(
            num_scalar_prefetch=1,
            grid=(1,),
            in_specs=[WHOLE],
            out_specs=[WHOLE] * 2,
            scratch_shapes=[pltpu.VMEM((32, HALF), F32)],
        ),
        out_shape=[shape(16, HALF, dtype=F32)] * 2,
        compiler_params=PARAMS,
        cost_estimate=cost(0, 0.5),
        name="weight_rows",
    )(ids, parts)


def shift_chips(block, distance):
    route = [(i - distance, i) for i in range(N_CHIP) if 0 <= i - distance < N_CHIP]
    return lax.ppermute(block, CHIP, route)


def shift_x(block, distance):
    return lax.ppermute(block, "x", [(i, (i + distance) % 4) for i in range(4)])


def swap_core(block):
    return lax.ppermute(block, "c", [(0, 1), (1, 0)])


def shards(query, key, value, grad, inputs, stretch_order, session_starts):
    query, key, value, grad, inputs = query[0], key[0], value[0], grad[0], inputs[0]
    core = lax.axis_index("c")
    ids = jnp.stack([lax.axis_index(CTX), lax.axis_index("x"), core]).astype(jnp.int32)

    key_other, value = lax.optimization_barrier((swap_core(key), value))
    (key0,) = pick_call(ids, key, key_other)
    key0, query, grad, value = lax.optimization_barrier((key0, query, grad, value))
    key1 = shift_chips(key0, 1)
    value0, last = pick_call(ids, value, swap_core(value), key0)
    far2 = shift_chips(last, 2)
    keys = [far2, key1, key0]
    bias, queries, grads = prepare_call(
        ids,
        stretch_order.reshape(-1),
        session_starts.reshape(-1),
        query,
        swap_core(query),
        grad,
        swap_core(grad),
    )
    bias, value0 = lax.optimization_barrier((bias, value0))
    values = [far2, shift_chips(value0, 1), value0]

    bias, inputs = lax.optimization_barrier((bias, inputs))
    packed = pack_call(ids, inputs)
    own = [packed[0]] + [shift_x(packed[d], d) for d in range(1, 4)]

    prob, value_own, value_t1, value_t2 = forward_call(bias, queries, grads, keys)
    value_r2 = shift_chips(value_t2, -2)
    value_r1 = shift_chips(value_t1, -1)
    query_keep, query_send, key_own, key_t1, key_t2 = backward_call(
        ids, prob, queries, grads, keys, values
    )
    value_r1, query_send, *far = lax.optimization_barrier((value_r1, query_send, *own[1:]))
    own = [own[0]] + far
    other = [swap_core(block) for block in own]
    value_keep, value_send, sent = total_call(ids, value_own, value_r1, value_r2, True)
    key_r2 = shift_chips(key_t2, -2)
    key_r1 = shift_chips(key_t1, -1)
    gathered = lax.all_to_all(sent, "x", 0, 0, tiled=True)
    partial = weight_call(ids, gathered, own, other)
    partial, key_r1, key_r2 = lax.optimization_barrier((partial, key_r1, key_r2))
    partial = lax.all_to_all(partial.reshape(32, 32, HALF), ("zl", "zh", "y"), 0, 0, tiled=True)

    key_keep, key_send = total_call(ids, key_own, key_r1, key_r2, False)
    grad_query, grad_key, grad_value = join_call(
        ids,
        [query_keep, key_keep, value_keep],
        [swap_core(query_send), swap_core(key_send), swap_core(value_send)],
        "join_outputs",
    )
    partial, grad_query = lax.optimization_barrier((partial, grad_query))
    row_keep, row_send = final_call(ids, partial)
    swapped = swap_core(row_send)
    first, second = jnp.where(core == 0, row_keep, swapped), jnp.where(core == 0, swapped, row_keep)
    weight_grad = jnp.concatenate([first, second], axis=1)
    return grad_query[None], grad_key[None], grad_value[None], weight_grad


def solution(mesh):
    fine = Mesh(mesh.devices.reshape(4, 2, 4, 4, 2), AXES)
    rows = P("zl", CTX, None)
    return jax.shard_map(
        shards,
        mesh=fine,
        in_specs=(rows, rows, rows, rows, rows, P("zl", None, None), P("zl", None)),
        out_specs=(rows, rows, rows, P(AXES, None)),
        check_vma=False,
    )
```

```python
import math

import jax
import jax.numpy as jnp
from jax import lax
from jax.experimental import pallas as pl
from jax.experimental.pallas import tpu as pltpu
from jax.sharding import Mesh, PartitionSpec as P

HEAD = 128
STRETCH = 64
SPAN = 4
PER_GROUP = 4
GROUPS = 2
ROWS = 128
KEYS = SPAN * ROWS
WIDE = PER_GROUP * HEAD
HALF = GROUPS * HEAD
MASKED = -1e30
SCALE = HEAD**-0.5
LOG2E = math.log2(math.e)
BF16 = jnp.bfloat16
F32 = jnp.float32
AXES = ("zl", "zh", "x", "y", "c")
CTX = ("zh", "x", "y", "c")
CHIP = ("zh", "x", "y")
N_CHIP = 32
N_SHARD = 64
NSTART = 64
MIB = 1024 * 1024
PARAMS = pltpu.CompilerParams(vmem_limit_bytes=8 * MIB)
LARGE = pltpu.CompilerParams(vmem_limit_bytes=24 * MIB)
WHOLE = pl.BlockSpec(memory_space=pltpu.VMEM)


def nt(a, b):
    return lax.dot_general(a, b, (((1,), (1,)), ((), ())), preferred_element_type=F32)


def tn(a, b):
    return lax.dot_general(a, b, (((0,), (0,)), ((), ())), preferred_element_type=F32)


def nn(a, b):
    return lax.dot_general(a, b, (((1,), (0,)), ((), ())), preferred_element_type=F32)


def shape(*dims, dtype=BF16):
    return jax.ShapeDtypeStruct(dims, dtype)


def cost(flops, mib):
    return pl.CostEstimate(flops=flops, bytes_accessed=int(mib * MIB), transcendentals=0)


def stack_heads(block):
    return jnp.concatenate([block[:, h * HEAD : (h + 1) * HEAD] for h in range(PER_GROUP)], axis=0)


def put_rows(out_ref, core, own, other):
    out_ref[pl.ds(pl.multiple_of(core * ROWS, ROWS), ROWS), :] = own[...]
    out_ref[pl.ds(pl.multiple_of((1 - core) * ROWS, ROWS), ROWS), :] = other[...]


def pick_keys_kernel(ids, own, other, both_ref):
    put_rows(both_ref, ids[2], own, other)


def pick_values_kernel(ids, own, other, keys, both_ref, last_ref):
    put_rows(both_ref, ids[2], own, other)
    last_ref[:, :HALF] = keys[ROWS:]
    last_ref[:, HALF:] = both_ref[ROWS:]


def pick_call(ids, own, other, keys=None):
    half = pl.BlockSpec((ROWS, HALF), lambda i, ids: (0, ids[2]))
    whole = pl.BlockSpec((ROWS, HALF), lambda i, ids: (0, 0))
    extra = [] if keys is None else [keys]
    return pl.pallas_call(
        pick_values_kernel if extra else pick_keys_kernel,
        grid_spec=pltpu.PrefetchScalarGridSpec(
            num_scalar_prefetch=1,
            grid=(1,),
            in_specs=[whole, half] + [WHOLE] * len(extra),
            out_specs=[WHOLE] * (1 + len(extra)),
        ),
        out_shape=[shape(2 * ROWS, HALF)] + [shape(ROWS, 2 * HALF)] * len(extra),
        compiler_params=PARAMS,
        cost_estimate=cost(0, 0.5),
        name="pick_values" if extra else "pick_keys",
    )(ids, own, other, *extra)


def prepare_kernel(
    ids, table, q_own, q_other, g_own, g_other, bias_ref, queries_ref, grads_ref
):
    put_rows(queries_ref, ids[2], q_own, q_other)
    put_rows(grads_ref, ids[2], g_own, g_other)
    base = ids[0] - ids[2]
    lane = lax.broadcasted_iota(jnp.int32, (1, ROWS), 1)
    row = lax.broadcasted_iota(jnp.int32, (STRETCH, ROWS), 0)
    for s in range(2):
        shard = base + s
        stretch = jnp.where(lane < STRETCH, table[2 * shard], table[2 * shard + 1])
        query_pos = shard * ROWS + stretch * STRETCH + (lane & (STRETCH - 1))
        begin = jnp.zeros((1, ROWS), jnp.int32)
        for i in range(NSTART):
            start = table[2 * N_SHARD + i]
            begin = jnp.where(start <= query_pos, start, begin)
        for d in range(SPAN):
            source = shard - (SPAN - 1) + d
            known = jnp.maximum(source, 0)
            for j in range(2):
                key_pos = source * ROWS + table[2 * known + j] * STRETCH + row
                allowed = (key_pos <= query_pos) & (key_pos >= begin)
                bias_ref[s, (2 * d + j) * STRETCH : (2 * d + j + 1) * STRETCH, :] = jnp.where(
                    allowed, 0.0, MASKED
                )


def prepare_call(ids, table, *blocks):
    width = GROUPS * WIDE
    own = pl.BlockSpec((ROWS, width), lambda i, *_: (0, 0))
    other = pl.BlockSpec((ROWS, width), lambda i, ids, *_: (0, ids[2]))
    return pl.pallas_call(
        prepare_kernel,
        grid_spec=pltpu.PrefetchScalarGridSpec(
            num_scalar_prefetch=2,
            grid=(1,),
            in_specs=[own, other] * 2,
            out_specs=[WHOLE] * 3,
        ),
        out_shape=[shape(2, KEYS, ROWS, dtype=F32)] + [shape(2 * ROWS, width)] * 2,
        compiler_params=PARAMS,
        cost_estimate=cost(0, 2.5),
        name="prepare",
    )(ids, table, *blocks)


def spread(out, far1, far2, s0, s1):
    out[:ROWS] = s0[3 * ROWS :] + s1[2 * ROWS : 3 * ROWS]
    out[ROWS:] = s1[3 * ROWS :]
    far1[:ROWS] = (s0[ROWS : 2 * ROWS] + s1[:ROWS]).astype(BF16)
    far1[ROWS:] = (s0[2 * ROWS : 3 * ROWS] + s1[ROWS : 2 * ROWS]).astype(BF16)
    far2[...] = s0[:ROWS].astype(far2.dtype)


def forward_kernel(bias, q_ref, g_ref, k2, k1, k0, prob_ref, own_ref, far1, far2):
    keys = jnp.concatenate([k2[...], k1[...], k0[...]], axis=0)
    terms = []
    for s in range(2):
        rows = slice(s * ROWS, (s + 1) * ROWS)
        window = keys[s * ROWS : s * ROWS + KEYS]
        for h in range(PER_GROUP):
            cols = slice(h * HEAD, (h + 1) * HEAD)
            score = nt(window, q_ref[rows, cols]) * (SCALE * LOG2E) + bias[s]
            weight = jnp.exp2(score - jnp.max(score, axis=0, keepdims=True))
            total = jnp.sum(weight, axis=0, keepdims=True)
            prob_ref[0, s, :, cols] = (weight * (1.0 / total)).astype(BF16)
        terms.append(nn(prob_ref[0, s], stack_heads(g_ref[rows, :])))
    spread(own_ref, far1, far2, *terms)


def backward_kernel(
    ids,
    prob_ref,
    q_ref,
    g_ref,
    k2,
    k1,
    k0,
    v2,
    v1,
    v0,
    keep_ref,
    send_ref,
    own_ref,
    far1,
    far2,
    gq_ref,
):
    core = ids[2]
    keys = jnp.concatenate([k2[...], k1[...], k0[...]], axis=0)
    values = jnp.concatenate([v2[...], v1[...], v0[...]], axis=0)
    terms = []
    for s in range(2):
        rows = slice(s * ROWS, (s + 1) * ROWS)
        window = slice(s * ROWS, s * ROWS + KEYS)
        prob = prob_ref[0, s].astype(F32)
        weighted = prob * nt(values[window], stack_heads(g_ref[rows, :]))
        delta = jnp.sum(weighted, axis=0, keepdims=True)
        grad_score = (weighted - prob * delta).astype(BF16)
        terms.append(nn(grad_score, stack_heads(q_ref[rows, :])) * SCALE)
        query_grad = tn(grad_score, keys[window]) * SCALE
        for h in range(PER_GROUP):
            gq_ref[s, :, h * HEAD : (h + 1) * HEAD] = query_grad[h * ROWS : (h + 1) * ROWS].astype(
                BF16
            )
    spread(own_ref, far1, far2, *terms)
    keep_ref[...] = gq_ref[core]
    send_ref[...] = gq_ref[1 - core]


def narrow(rows, shift=0):
    return pl.BlockSpec((rows, HEAD), lambda j, *_: (0, j + shift))


def wide(rows):
    return pl.BlockSpec((rows, WIDE), lambda j, *_: (0, j))


WINDOW = [narrow(ROWS), narrow(2 * ROWS), narrow(2 * ROWS)]
VALUE_WINDOW = [narrow(ROWS, GROUPS)] + WINDOW[1:]
TERMS = [narrow(2 * ROWS), narrow(2 * ROWS), narrow(ROWS)]
PROB_SPEC = pl.BlockSpec((1, 2, KEYS, WIDE), lambda j, *_: (j, 0, 0, 0))


def term_shapes(last):
    return [shape(2 * ROWS, HALF, dtype=F32), shape(2 * ROWS, HALF), shape(ROWS, HALF, dtype=last)]


def forward_call(bias, queries, grads, keys):
    return pl.pallas_call(
        forward_kernel,
        grid=(GROUPS,),
        in_specs=[pl.BlockSpec((2, KEYS, ROWS), lambda j: (0, 0, 0))]
        + [wide(2 * ROWS)] * 2
        + WINDOW,
        out_specs=[PROB_SPEC] + TERMS,
        out_shape=[shape(GROUPS, 2, KEYS, WIDE)] + term_shapes(F32),
        compiler_params=LARGE,
        cost_estimate=cost(4 * 16 * ROWS * KEYS * HEAD, 6),
        name="forward_and_value_gradient",
    )(bias, queries, grads, *keys)


def backward_call(ids, prob, queries, grads, keys, values):
    return pl.pallas_call(
        backward_kernel,
        grid_spec=pltpu.PrefetchScalarGridSpec(
            num_scalar_prefetch=1,
            grid=(GROUPS,),
            in_specs=[PROB_SPEC] + [wide(2 * ROWS)] * 2 + WINDOW + VALUE_WINDOW,
            out_specs=[wide(ROWS)] * 2 + TERMS,
            scratch_shapes=[pltpu.VMEM((2, ROWS, WIDE), BF16)],
        ),
        out_shape=[shape(ROWS, GROUPS * WIDE)] * 2 + term_shapes(BF16),
        compiler_params=LARGE,
        cost_estimate=cost(6 * 16 * ROWS * KEYS * HEAD, 6),
        name="query_and_key_gradient",
    )(ids, prob, queries, grads, *keys, *values)


def pack_kernel(ids, in_ref, o0, o1, o2, o3):
    for d, out_ref in enumerate((o0, o1, o2, o3)):
        x = (ids[1] + d) & 3
        for z in range(8):
            column = pl.multiple_of((4 * z + x) * HEAD, HEAD)
            out_ref[:, z * HEAD : (z + 1) * HEAD] = in_ref[:, pl.ds(column, HEAD)]


def pack_call(ids, inputs):
    return pl.pallas_call(
        pack_kernel,
        grid_spec=pltpu.PrefetchScalarGridSpec(
            num_scalar_prefetch=1, grid=(1,), in_specs=[WHOLE], out_specs=[WHOLE] * 4
        ),
        out_shape=[shape(ROWS, 8 * HEAD)] * 4,
        compiler_params=PARAMS,
        cost_estimate=cost(0, 2),
        name="pack_inputs",
    )(ids, inputs)


def add_terms(own, r1, r2):
    first = own[:ROWS] + r1[:ROWS].astype(F32)
    second = own[ROWS:] + r1[ROWS:].astype(F32) + r2[...].astype(F32)
    return first.astype(BF16), second.astype(BF16)


def value_total_kernel(ids, own, r1, r2, keep_ref, send_ref, copies_ref):
    core = ids[2]
    first, second = add_terms(own, r1, r2)
    for x in range(4):
        copies_ref[x, :ROWS], copies_ref[x, ROWS:] = first, second
    keep_ref[...] = copies_ref[0, pl.ds(pl.multiple_of(core * ROWS, ROWS), ROWS), :]
    send_ref[...] = copies_ref[0, pl.ds(pl.multiple_of((1 - core) * ROWS, ROWS), ROWS), :]


def key_total_kernel(ids, own, r1, r2, keep_ref, send_ref, both_ref):
    core = ids[2]
    both_ref[:ROWS], both_ref[ROWS:] = add_terms(own, r1, r2)
    keep_ref[...] = both_ref[pl.ds(pl.multiple_of(core * ROWS, ROWS), ROWS), :]
    send_ref[...] = both_ref[pl.ds(pl.multiple_of((1 - core) * ROWS, ROWS), ROWS), :]


def total_call(ids, own, r1, r2, copies):
    return pl.pallas_call(
        value_total_kernel if copies else key_total_kernel,
        grid_spec=pltpu.PrefetchScalarGridSpec(
            num_scalar_prefetch=1,
            grid=(1,),
            in_specs=[WHOLE] * 3,
            out_specs=[WHOLE] * (3 if copies else 2),
            scratch_shapes=[] if copies else [pltpu.VMEM((2 * ROWS, HALF), BF16)],
        ),
        out_shape=[shape(ROWS, HALF)] * 2 + ([shape(4, 2 * ROWS, HALF)] if copies else []),
        compiler_params=PARAMS,
        cost_estimate=cost(0, 1),
        name="value_gradient_total" if copies else "key_gradient_total",
    )(ids, own, r1, r2)


def join_kernel(ids, *refs):
    core = ids[2]
    count = len(refs) // 3
    for keep, other, out in zip(refs[:count], refs[count : 2 * count], refs[2 * count :]):
        width = keep.shape[1]
        out[:, pl.ds(pl.multiple_of(core * width, HEAD), width)] = keep[...]
        out[:, pl.ds(pl.multiple_of((1 - core) * width, HEAD), width)] = other[...]


def join_call(ids, keep, other, name):
    return pl.pallas_call(
        join_kernel,
        grid_spec=pltpu.PrefetchScalarGridSpec(
            num_scalar_prefetch=1,
            grid=(1,),
            in_specs=[WHOLE] * (2 * len(keep)),
            out_specs=[WHOLE] * len(keep),
        ),
        out_shape=[shape(a.shape[0], 2 * a.shape[1], dtype=a.dtype) for a in keep],
        compiler_params=PARAMS,
        cost_estimate=cost(0, 0.5),
        name=name,
    )(ids, *keep, *other)


def weight_kernel(ids, grads, a0, a1, a2, a3, b0, b1, b2, b3, out_ref):
    x, core = ids[1], ids[2]
    left = [ref[...] for ref in (a0, a1, a2, a3, b0, b1, b2, b3)]
    right = []
    for side in (core, 1 - core):
        rows = pl.ds(pl.multiple_of(side * ROWS, ROWS), ROWS)
        right += [grads[(x + 4 - d) & 3, rows, :] for d in range(4)]
    left, right = jnp.concatenate(left, axis=0), jnp.concatenate(right, axis=0)
    out_ref[...] = tn(left, right).astype(BF16)


def weight_call(ids, grads, own, other):
    taken = pl.BlockSpec((ROWS, 256), lambda i, _: (0, i))
    return pl.pallas_call(
        weight_kernel,
        grid_spec=pltpu.PrefetchScalarGridSpec(
            num_scalar_prefetch=1,
            grid=(4,),
            in_specs=[pl.BlockSpec((4, 2 * ROWS, HALF), lambda i, _: (0, 0, 0))] + [taken] * 8,
            out_specs=pl.BlockSpec((256, HALF), lambda i, _: (i, 0)),
        ),
        out_shape=shape(1024, HALF),
        compiler_params=LARGE,
        cost_estimate=cost(2 * 1024 * 1024 * 256, 3),
        name="weight_gradient",
    )(ids, grads, *own, *other)


def final_kernel(ids, in_ref, keep_ref, send_ref, total_ref):
    core = ids[2]
    total = in_ref[0].astype(F32)
    for i in range(1, 32):
        total += in_ref[i].astype(F32)
    total_ref[...] = total
    keep_ref[...] = total_ref[pl.ds(pl.multiple_of(core * 16, 16), 16), :]
    send_ref[...] = total_ref[pl.ds(pl.multiple_of((1 - core) * 16, 16), 16), :]


def final_call(ids, parts):
    return pl.pallas_call(
        final_kernel,
        grid_spec=pltpu.PrefetchScalarGridSpec(
            num_scalar_prefetch=1,
            grid=(1,),
            in_specs=[WHOLE],
            out_specs=[WHOLE] * 2,
            scratch_shapes=[pltpu.VMEM((32, HALF), F32)],
        ),
        out_shape=[shape(16, HALF, dtype=F32)] * 2,
        compiler_params=PARAMS,
        cost_estimate=cost(0, 0.5),
        name="weight_rows",
    )(ids, parts)


def shift_chips(block, distance):
    route = [(i - distance, i) for i in range(N_CHIP) if 0 <= i - distance < N_CHIP]
    return lax.ppermute(block, CHIP, route)


def shift_x(block, distance):
    return lax.ppermute(block, "x", [(i, (i + distance) % 4) for i in range(4)])


def swap_core(block):
    return lax.ppermute(block, "c", [(0, 1), (1, 0)])


def own_half(block, core):
    width = block.shape[1] // 2
    return lax.dynamic_slice(block, (0, core * width), (ROWS, width))


def shards(query, key, value, grad, inputs, stretch_order, session_starts):
    query, key, value, grad, inputs = query[0], key[0], value[0], grad[0], inputs[0]
    core = lax.axis_index("c")
    ids = jnp.stack([lax.axis_index(CTX), lax.axis_index("x"), core]).astype(jnp.int32)

    table = jnp.concatenate([stretch_order.reshape(-1), session_starts.reshape(-1)])
    key_other, value, table, value_half, key_half = lax.optimization_barrier(
        (swap_core(key), value, table, own_half(value, core), own_half(key, core))
    )
    (key0,) = pick_call(ids, key_half, key_other)
    key0, query, grad, value = lax.optimization_barrier((key0, query, grad, value))
    key1 = shift_chips(key0, 1)
    value0, last = pick_call(ids, value_half, swap_core(value), key0)
    far2 = shift_chips(last, 2)
    keys = [far2, key1, key0]
    bias, queries, grads = prepare_call(
        ids,
        table,
        own_half(query, core),
        swap_core(query),
        own_half(grad, core),
        swap_core(grad),
    )
    bias, value0 = lax.optimization_barrier((bias, value0))
    values = [far2, shift_chips(value0, 1), value0]

    prob, value_own, value_t1, value_t2 = forward_call(bias, queries, grads, keys)
    value_r2 = shift_chips(value_t2, -2)
    value_r1 = shift_chips(value_t1, -1)
    query_keep, query_send, key_own, key_t1, key_t2 = backward_call(
        ids, prob, queries, grads, keys, values
    )
    inputs, query_send = lax.optimization_barrier((inputs, query_send))
    packed = pack_call(ids, inputs)
    own = [packed[0]] + [shift_x(packed[d], d) for d in range(1, 4)]
    other = [swap_core(block) for block in own]
    value_r1, query_send = lax.optimization_barrier((value_r1, query_send))
    value_keep, value_send, sent = total_call(ids, value_own, value_r1, value_r2, True)
    key_r2 = shift_chips(key_t2, -2)
    key_r1 = shift_chips(key_t1, -1)
    gathered = lax.all_to_all(sent, "x", 0, 0, tiled=True)
    partial = weight_call(ids, gathered, own, other)
    partial, key_r1, key_r2 = lax.optimization_barrier((partial, key_r1, key_r2))
    partial = lax.all_to_all(partial.reshape(32, 32, HALF), ("zl", "zh", "y"), 0, 0, tiled=True)

    key_keep, key_send = total_call(ids, key_own, key_r1, key_r2, False)
    grad_query, grad_key, grad_value = join_call(
        ids,
        [query_keep, key_keep, value_keep],
        [swap_core(query_send), swap_core(key_send), swap_core(value_send)],
        "join_outputs",
    )
    partial, grad_query = lax.optimization_barrier((partial, grad_query))
    row_keep, row_send = final_call(ids, partial)
    swapped = swap_core(row_send)
    first, second = jnp.where(core == 0, row_keep, swapped), jnp.where(core == 0, swapped, row_keep)
    weight_grad = jnp.concatenate([first, second], axis=1)
    return grad_query[None], grad_key[None], grad_value[None], weight_grad


def solution(mesh):
    fine = Mesh(mesh.devices.reshape(4, 2, 4, 4, 2), AXES)
    rows = P("zl", CTX, None)
    return jax.shard_map(
        shards,
        mesh=fine,
        in_specs=(rows, rows, rows, rows, rows, P("zl", None, None), P("zl", None)),
        out_specs=(rows, rows, rows, P(AXES, None)),
        check_vma=False,
    )
```

```python
import math

import jax
import jax.numpy as jnp
from jax import lax
from jax.experimental import pallas as pl
from jax.experimental.pallas import tpu as pltpu
from jax.sharding import Mesh, PartitionSpec as P

HEAD = 128
STRETCH = 64
SPAN = 4
PER_GROUP = 4
GROUPS = 2
ROWS = 128
KEYS = SPAN * ROWS
WIDE = PER_GROUP * HEAD
HALF = GROUPS * HEAD
MASKED = -1e30
SCALE = HEAD**-0.5
LOG2E = math.log2(math.e)
BF16 = jnp.bfloat16
F32 = jnp.float32
AXES = ("zl", "zh", "x", "y", "c")
CTX = ("zh", "x", "y", "c")
CHIP = ("zh", "x", "y")
N_CHIP = 32
N_SHARD = 64
NSTART = 64
MIB = 1024 * 1024
PARAMS = pltpu.CompilerParams(vmem_limit_bytes=8 * MIB)
LARGE = pltpu.CompilerParams(vmem_limit_bytes=24 * MIB)
WHOLE = pl.BlockSpec(memory_space=pltpu.VMEM)


def nt(a, b):
    return lax.dot_general(a, b, (((1,), (1,)), ((), ())), preferred_element_type=F32)


def tn(a, b):
    return lax.dot_general(a, b, (((0,), (0,)), ((), ())), preferred_element_type=F32)


def nn(a, b):
    return lax.dot_general(a, b, (((1,), (0,)), ((), ())), preferred_element_type=F32)


def shape(*dims, dtype=BF16):
    return jax.ShapeDtypeStruct(dims, dtype)


def cost(flops, mib):
    return pl.CostEstimate(flops=flops, bytes_accessed=int(mib * MIB), transcendentals=0)


def stack_heads(block):
    return jnp.concatenate([block[:, h * HEAD : (h + 1) * HEAD] for h in range(PER_GROUP)], axis=0)


def put_rows(out_ref, core, own, other):
    out_ref[pl.ds(pl.multiple_of(core * ROWS, ROWS), ROWS), :] = own[...]
    out_ref[pl.ds(pl.multiple_of((1 - core) * ROWS, ROWS), ROWS), :] = other[...]


def pick_keys_kernel(ids, own, other, both_ref):
    put_rows(both_ref, ids[2], own, other)


def pick_values_kernel(ids, own, other, keys, both_ref, last_ref):
    put_rows(both_ref, ids[2], own, other)
    last_ref[:, :HALF] = keys[ROWS:]
    last_ref[:, HALF:] = both_ref[ROWS:]


def pick_call(ids, own, other, keys=None):
    half = pl.BlockSpec((ROWS, HALF), lambda i, ids: (0, ids[2]))
    whole = pl.BlockSpec((ROWS, HALF), lambda i, ids: (0, 0))
    extra = [] if keys is None else [keys]
    return pl.pallas_call(
        pick_values_kernel if extra else pick_keys_kernel,
        grid_spec=pltpu.PrefetchScalarGridSpec(
            num_scalar_prefetch=1,
            grid=(1,),
            in_specs=[whole, half] + [WHOLE] * len(extra),
            out_specs=[WHOLE] * (1 + len(extra)),
        ),
        out_shape=[shape(2 * ROWS, HALF)] + [shape(ROWS, 2 * HALF)] * len(extra),
        compiler_params=PARAMS,
        cost_estimate=cost(0, 0.5),
        name="pick_values" if extra else "pick_keys",
    )(ids, own, other, *extra)


def prepare_kernel(
    ids, table, q_own, q_other, g_own, g_other, bias_ref, queries_ref, grads_ref
):
    put_rows(queries_ref, ids[2], q_own, q_other)
    put_rows(grads_ref, ids[2], g_own, g_other)
    base = ids[0] - ids[2]
    lane = lax.broadcasted_iota(jnp.int32, (1, ROWS), 1)
    row = lax.broadcasted_iota(jnp.int32, (STRETCH, ROWS), 0)
    for s in range(2):
        shard = base + s
        stretch = jnp.where(lane < STRETCH, table[2 * shard], table[2 * shard + 1])
        query_pos = shard * ROWS + stretch * STRETCH + (lane & (STRETCH - 1))
        begin = jnp.zeros((1, ROWS), jnp.int32)
        for i in range(NSTART):
            start = table[2 * N_SHARD + i]
            begin = jnp.where(start <= query_pos, start, begin)
        for d in range(SPAN):
            source = shard - (SPAN - 1) + d
            known = jnp.maximum(source, 0)
            for j in range(2):
                key_pos = source * ROWS + table[2 * known + j] * STRETCH + row
                allowed = (key_pos <= query_pos) & (key_pos >= begin)
                bias_ref[s, (2 * d + j) * STRETCH : (2 * d + j + 1) * STRETCH, :] = jnp.where(
                    allowed, 0.0, MASKED
                )


def prepare_call(ids, table, *blocks):
    width = GROUPS * WIDE
    own = pl.BlockSpec((ROWS, width), lambda i, *_: (0, 0))
    other = pl.BlockSpec((ROWS, width), lambda i, ids, *_: (0, ids[2]))
    return pl.pallas_call(
        prepare_kernel,
        grid_spec=pltpu.PrefetchScalarGridSpec(
            num_scalar_prefetch=2,
            grid=(1,),
            in_specs=[own, other] * 2,
            out_specs=[WHOLE] * 3,
        ),
        out_shape=[shape(2, KEYS, ROWS, dtype=F32)] + [shape(2 * ROWS, width)] * 2,
        compiler_params=PARAMS,
        cost_estimate=cost(0, 2.5),
        name="prepare",
    )(ids, table, *blocks)


def spread(out, far1, far2, s0, s1):
    out[:ROWS] = s0[3 * ROWS :] + s1[2 * ROWS : 3 * ROWS]
    out[ROWS:] = s1[3 * ROWS :]
    far1[:ROWS] = (s0[ROWS : 2 * ROWS] + s1[:ROWS]).astype(BF16)
    far1[ROWS:] = (s0[2 * ROWS : 3 * ROWS] + s1[ROWS : 2 * ROWS]).astype(BF16)
    far2[...] = s0[:ROWS].astype(far2.dtype)


def forward_kernel(bias, q_ref, g_ref, k2, k1, k0, prob_ref, own_ref, far1, far2):
    keys = jnp.concatenate([k2[...], k1[...], k0[...]], axis=0)
    terms = []
    for s in range(2):
        rows = slice(s * ROWS, (s + 1) * ROWS)
        window = keys[s * ROWS : s * ROWS + KEYS]
        for h in range(PER_GROUP):
            cols = slice(h * HEAD, (h + 1) * HEAD)
            score = nt(window, q_ref[rows, cols]) * (SCALE * LOG2E) + bias[s]
            weight = jnp.exp2(score - jnp.max(score, axis=0, keepdims=True))
            total = jnp.sum(weight, axis=0, keepdims=True)
            prob_ref[0, s, :, cols] = (weight * (1.0 / total)).astype(BF16)
        terms.append(nn(prob_ref[0, s], stack_heads(g_ref[rows, :])))
    spread(own_ref, far1, far2, *terms)


def backward_kernel(
    ids,
    prob_ref,
    q_ref,
    g_ref,
    k2,
    k1,
    k0,
    v2,
    v1,
    v0,
    keep_ref,
    send_ref,
    own_ref,
    far1,
    far2,
    gq_ref,
):
    core = ids[2]
    keys = jnp.concatenate([k2[...], k1[...], k0[...]], axis=0)
    values = jnp.concatenate([v2[...], v1[...], v0[...]], axis=0)
    terms = []
    for s in range(2):
        rows = slice(s * ROWS, (s + 1) * ROWS)
        window = slice(s * ROWS, s * ROWS + KEYS)
        prob = prob_ref[0, s].astype(F32)
        weighted = prob * nt(values[window], stack_heads(g_ref[rows, :]))
        delta = jnp.sum(weighted, axis=0, keepdims=True)
        grad_score = (weighted - prob * delta).astype(BF16)
        terms.append(nn(grad_score, stack_heads(q_ref[rows, :])) * SCALE)
        query_grad = tn(grad_score, keys[window]) * SCALE
        for h in range(PER_GROUP):
            gq_ref[s, :, h * HEAD : (h + 1) * HEAD] = query_grad[h * ROWS : (h + 1) * ROWS].astype(
                BF16
            )
    spread(own_ref, far1, far2, *terms)
    keep_ref[...] = gq_ref[core]
    send_ref[...] = gq_ref[1 - core]


def narrow(rows, shift=0):
    return pl.BlockSpec((rows, HEAD), lambda j, *_: (0, j + shift))


def wide(rows):
    return pl.BlockSpec((rows, WIDE), lambda j, *_: (0, j))


WINDOW = [narrow(ROWS), narrow(2 * ROWS), narrow(2 * ROWS)]
VALUE_WINDOW = [narrow(ROWS, GROUPS)] + WINDOW[1:]
TERMS = [narrow(2 * ROWS), narrow(2 * ROWS), narrow(ROWS)]
PROB_SPEC = pl.BlockSpec((1, 2, KEYS, WIDE), lambda j, *_: (j, 0, 0, 0))


def term_shapes(last):
    return [shape(2 * ROWS, HALF, dtype=F32), shape(2 * ROWS, HALF), shape(ROWS, HALF, dtype=last)]


def forward_call(bias, queries, grads, keys):
    return pl.pallas_call(
        forward_kernel,
        grid=(GROUPS,),
        in_specs=[pl.BlockSpec((2, KEYS, ROWS), lambda j: (0, 0, 0))]
        + [wide(2 * ROWS)] * 2
        + WINDOW,
        out_specs=[PROB_SPEC] + TERMS,
        out_shape=[shape(GROUPS, 2, KEYS, WIDE)] + term_shapes(BF16),
        compiler_params=LARGE,
        cost_estimate=cost(4 * 16 * ROWS * KEYS * HEAD, 6),
        name="forward_and_value_gradient",
    )(bias, queries, grads, *keys)


def backward_call(ids, prob, queries, grads, keys, values):
    return pl.pallas_call(
        backward_kernel,
        grid_spec=pltpu.PrefetchScalarGridSpec(
            num_scalar_prefetch=1,
            grid=(GROUPS,),
            in_specs=[PROB_SPEC] + [wide(2 * ROWS)] * 2 + WINDOW + VALUE_WINDOW,
            out_specs=[wide(ROWS)] * 2 + TERMS,
            scratch_shapes=[pltpu.VMEM((2, ROWS, WIDE), BF16)],
        ),
        out_shape=[shape(ROWS, GROUPS * WIDE)] * 2 + term_shapes(BF16),
        compiler_params=LARGE,
        cost_estimate=cost(6 * 16 * ROWS * KEYS * HEAD, 6),
        name="query_and_key_gradient",
    )(ids, prob, queries, grads, *keys, *values)


def pack_kernel(ids, in_ref, o0, o1, o2, o3):
    for d, out_ref in enumerate((o0, o1, o2, o3)):
        x = (ids[1] + d) & 3
        for z in range(8):
            column = pl.multiple_of((4 * z + x) * HEAD, HEAD)
            out_ref[:, z * HEAD : (z + 1) * HEAD] = in_ref[:, pl.ds(column, HEAD)]


def pack_call(ids, inputs):
    return pl.pallas_call(
        pack_kernel,
        grid_spec=pltpu.PrefetchScalarGridSpec(
            num_scalar_prefetch=1, grid=(1,), in_specs=[WHOLE], out_specs=[WHOLE] * 4
        ),
        out_shape=[shape(ROWS, 8 * HEAD)] * 4,
        compiler_params=PARAMS,
        cost_estimate=cost(0, 2),
        name="pack_inputs",
    )(ids, inputs)


def add_terms(own, r1, r2):
    first = own[:ROWS] + r1[:ROWS].astype(F32)
    second = own[ROWS:] + r1[ROWS:].astype(F32) + r2[...].astype(F32)
    return first.astype(BF16), second.astype(BF16)


def value_total_kernel(ids, own, r1, r2, keep_ref, send_ref, copies_ref):
    core = ids[2]
    first, second = add_terms(own, r1, r2)
    for x in range(4):
        copies_ref[x, :ROWS], copies_ref[x, ROWS:] = first, second
    keep_ref[...] = copies_ref[0, pl.ds(pl.multiple_of(core * ROWS, ROWS), ROWS), :]
    send_ref[...] = copies_ref[0, pl.ds(pl.multiple_of((1 - core) * ROWS, ROWS), ROWS), :]


def key_total_kernel(ids, own, r1, r2, keep_ref, send_ref, both_ref):
    core = ids[2]
    both_ref[:ROWS], both_ref[ROWS:] = add_terms(own, r1, r2)
    keep_ref[...] = both_ref[pl.ds(pl.multiple_of(core * ROWS, ROWS), ROWS), :]
    send_ref[...] = both_ref[pl.ds(pl.multiple_of((1 - core) * ROWS, ROWS), ROWS), :]


def total_call(ids, own, r1, r2, copies):
    return pl.pallas_call(
        value_total_kernel if copies else key_total_kernel,
        grid_spec=pltpu.PrefetchScalarGridSpec(
            num_scalar_prefetch=1,
            grid=(1,),
            in_specs=[WHOLE] * 3,
            out_specs=[WHOLE] * (3 if copies else 2),
            scratch_shapes=[] if copies else [pltpu.VMEM((2 * ROWS, HALF), BF16)],
        ),
        out_shape=[shape(ROWS, HALF)] * 2 + ([shape(4, 2 * ROWS, HALF)] if copies else []),
        compiler_params=PARAMS,
        cost_estimate=cost(0, 1),
        name="value_gradient_total" if copies else "key_gradient_total",
    )(ids, own, r1, r2)


def join_kernel(ids, *refs):
    core = ids[2]
    count = len(refs) // 3
    for keep, other, out in zip(refs[:count], refs[count : 2 * count], refs[2 * count :]):
        width = keep.shape[1]
        out[:, pl.ds(pl.multiple_of(core * width, HEAD), width)] = keep[...]
        out[:, pl.ds(pl.multiple_of((1 - core) * width, HEAD), width)] = other[...]


def join_call(ids, keep, other, name):
    return pl.pallas_call(
        join_kernel,
        grid_spec=pltpu.PrefetchScalarGridSpec(
            num_scalar_prefetch=1,
            grid=(1,),
            in_specs=[WHOLE] * (2 * len(keep)),
            out_specs=[WHOLE] * len(keep),
        ),
        out_shape=[shape(a.shape[0], 2 * a.shape[1], dtype=a.dtype) for a in keep],
        compiler_params=PARAMS,
        cost_estimate=cost(0, 0.5),
        name=name,
    )(ids, *keep, *other)


def weight_kernel(ids, grads, a0, a1, a2, a3, b0, b1, b2, b3, out_ref):
    x, core = ids[1], ids[2]
    left = [ref[...] for ref in (a0, a1, a2, a3, b0, b1, b2, b3)]
    right = []
    for side in (core, 1 - core):
        rows = pl.ds(pl.multiple_of(side * ROWS, ROWS), ROWS)
        right += [grads[(x + 4 - d) & 3, rows, :] for d in range(4)]
    left, right = jnp.concatenate(left, axis=0), jnp.concatenate(right, axis=0)
    out_ref[...] = tn(left, right).astype(BF16)


def weight_call(ids, grads, own, other):
    taken = pl.BlockSpec((ROWS, 256), lambda i, _: (0, i))
    return pl.pallas_call(
        weight_kernel,
        grid_spec=pltpu.PrefetchScalarGridSpec(
            num_scalar_prefetch=1,
            grid=(4,),
            in_specs=[pl.BlockSpec((4, 2 * ROWS, HALF), lambda i, _: (0, 0, 0))] + [taken] * 8,
            out_specs=pl.BlockSpec((256, HALF), lambda i, _: (i, 0)),
        ),
        out_shape=shape(1024, HALF),
        compiler_params=LARGE,
        cost_estimate=cost(2 * 1024 * 1024 * 256, 3),
        name="weight_gradient",
    )(ids, grads, *own, *other)


def final_kernel(ids, in_ref, keep_ref, send_ref, total_ref):
    core = ids[2]
    total = in_ref[0].astype(F32)
    for i in range(1, 32):
        total += in_ref[i].astype(F32)
    total_ref[...] = total
    keep_ref[...] = total_ref[pl.ds(pl.multiple_of(core * 16, 16), 16), :]
    send_ref[...] = total_ref[pl.ds(pl.multiple_of((1 - core) * 16, 16), 16), :]


def final_call(ids, parts):
    return pl.pallas_call(
        final_kernel,
        grid_spec=pltpu.PrefetchScalarGridSpec(
            num_scalar_prefetch=1,
            grid=(1,),
            in_specs=[WHOLE],
            out_specs=[WHOLE] * 2,
            scratch_shapes=[pltpu.VMEM((32, HALF), F32)],
        ),
        out_shape=[shape(16, HALF, dtype=F32)] * 2,
        compiler_params=PARAMS,
        cost_estimate=cost(0, 0.5),
        name="weight_rows",
    )(ids, parts)


def shift_chips(block, distance):
    route = [(i - distance, i) for i in range(N_CHIP) if 0 <= i - distance < N_CHIP]
    return lax.ppermute(block, CHIP, route)


def shift_x(block, distance):
    return lax.ppermute(block, "x", [(i, (i + distance) % 4) for i in range(4)])


def swap_core(block):
    return lax.ppermute(block, "c", [(0, 1), (1, 0)])


def own_half(block, core):
    width = block.shape[1] // 2
    return lax.dynamic_slice(block, (0, core * width), (ROWS, width))


def shards(query, key, value, grad, inputs, stretch_order, session_starts):
    query, key, value, grad, inputs = query[0], key[0], value[0], grad[0], inputs[0]
    core = lax.axis_index("c")
    ids = jnp.stack([lax.axis_index(CTX), lax.axis_index("x"), core]).astype(jnp.int32)

    table = jnp.concatenate([stretch_order.reshape(-1), session_starts.reshape(-1)])
    key_other, value, table, value_half, key_half = lax.optimization_barrier(
        (swap_core(key), value, table, own_half(value, core), own_half(key, core))
    )
    (key0,) = pick_call(ids, key_half, key_other)
    key0, query, grad, value = lax.optimization_barrier((key0, query, grad, value))
    key1 = shift_chips(key0, 1)
    value0, last = pick_call(ids, value_half, swap_core(value), key0)
    far2 = shift_chips(last, 2)
    keys = [far2, key1, key0]
    bias, queries, grads = prepare_call(
        ids,
        table,
        own_half(query, core),
        swap_core(query),
        own_half(grad, core),
        swap_core(grad),
    )
    bias, value0 = lax.optimization_barrier((bias, value0))
    values = [far2, shift_chips(value0, 1), value0]

    prob, value_own, value_t1, value_t2 = forward_call(bias, queries, grads, keys)
    value_own, inputs = lax.optimization_barrier((value_own, inputs))
    packed = pack_call(ids, inputs)
    own = [packed[0]] + [shift_x(packed[d], d) for d in range(1, 4)]
    other = [swap_core(block) for block in own]
    value_r2 = shift_chips(value_t2, -2)
    value_r1 = shift_chips(value_t1, -1)
    query_keep, query_send, key_own, key_t1, key_t2 = backward_call(
        ids, prob, queries, grads, keys, values
    )
    value_r1, query_send = lax.optimization_barrier((value_r1, query_send))
    value_keep, value_send, sent = total_call(ids, value_own, value_r1, value_r2, True)
    key_r2 = shift_chips(key_t2, -2)
    key_r1 = shift_chips(key_t1, -1)
    gathered = lax.all_to_all(sent, "x", 0, 0, tiled=True)
    partial = weight_call(ids, gathered, own, other)
    partial, key_r1, key_r2 = lax.optimization_barrier((partial, key_r1, key_r2))
    partial = lax.all_to_all(partial.reshape(32, 32, HALF), ("zl", "zh", "y"), 0, 0, tiled=True)

    key_keep, key_send = total_call(ids, key_own, key_r1, key_r2, False)
    grad_query, grad_key, grad_value = join_call(
        ids,
        [query_keep, key_keep, value_keep],
        [swap_core(query_send), swap_core(key_send), swap_core(value_send)],
        "join_outputs",
    )
    partial, grad_query = lax.optimization_barrier((partial, grad_query))
    row_keep, row_send = final_call(ids, partial)
    swapped = swap_core(row_send)
    first, second = jnp.where(core == 0, row_keep, swapped), jnp.where(core == 0, swapped, row_keep)
    weight_grad = jnp.concatenate([first, second], axis=1)
    return grad_query[None], grad_key[None], grad_value[None], weight_grad


def solution(mesh):
    fine = Mesh(mesh.devices.reshape(4, 2, 4, 4, 2), AXES)
    rows = P("zl", CTX, None)
    return jax.shard_map(
        shards,
        mesh=fine,
        in_specs=(rows, rows, rows, rows, rows, P("zl", None, None), P("zl", None)),
        out_specs=(rows, rows, rows, P(AXES, None)),
        check_vma=False,
    )
```

```python
import math

import jax
import jax.numpy as jnp
from jax import lax
from jax.experimental import pallas as pl
from jax.experimental.pallas import tpu as pltpu
from jax.sharding import Mesh, PartitionSpec as P

HEAD = 128
STRETCH = 64
SPAN = 4
PER_GROUP = 4
GROUPS = 2
ROWS = 128
KEYS = SPAN * ROWS
WIDE = PER_GROUP * HEAD
HALF = GROUPS * HEAD
MASKED = -1e30
SCALE = HEAD**-0.5
LOG2E = math.log2(math.e)
BF16 = jnp.bfloat16
F32 = jnp.float32
AXES = ("zl", "zh", "x", "y", "c")
CTX = ("zh", "x", "y", "c")
CHIP = ("zh", "x", "y")
N_CHIP = 32
N_SHARD = 64
NSTART = 64
MIB = 1024 * 1024
EXTRA = 96
PARAMS = pltpu.CompilerParams(vmem_limit_bytes=8 * MIB)
LARGE = pltpu.CompilerParams(vmem_limit_bytes=24 * MIB)
WHOLE = pl.BlockSpec(memory_space=pltpu.VMEM)


def nt(a, b):
    return lax.dot_general(a, b, (((1,), (1,)), ((), ())), preferred_element_type=F32)


def tn(a, b):
    return lax.dot_general(a, b, (((0,), (0,)), ((), ())), preferred_element_type=F32)


def nn(a, b):
    return lax.dot_general(a, b, (((1,), (0,)), ((), ())), preferred_element_type=F32)


def shape(*dims, dtype=BF16):
    return jax.ShapeDtypeStruct(dims, dtype)


def cost(flops, mib):
    return pl.CostEstimate(flops=flops, bytes_accessed=int(mib * MIB), transcendentals=0)


def stack_heads(block):
    return jnp.concatenate([block[:, h * HEAD : (h + 1) * HEAD] for h in range(PER_GROUP)], axis=0)


def put_rows(out_ref, core, own, other):
    out_ref[pl.ds(pl.multiple_of(core * ROWS, ROWS), ROWS), :] = own[...]
    out_ref[pl.ds(pl.multiple_of((1 - core) * ROWS, ROWS), ROWS), :] = other[...]


def pick_keys_kernel(ids, own, other, both_ref):
    put_rows(both_ref, ids[2], own, other)


def pick_values_kernel(ids, own, other, keys, both_ref, last_ref):
    put_rows(both_ref, ids[2], own, other)
    last_ref[:, :HALF] = keys[ROWS:]
    last_ref[:, HALF:] = both_ref[ROWS:]


def pick_call(ids, own, other, keys=None):
    half = pl.BlockSpec((ROWS, HALF), lambda i, ids: (0, ids[2]))
    whole = pl.BlockSpec((ROWS, HALF), lambda i, ids: (0, 0))
    extra = [] if keys is None else [keys]
    return pl.pallas_call(
        pick_values_kernel if extra else pick_keys_kernel,
        grid_spec=pltpu.PrefetchScalarGridSpec(
            num_scalar_prefetch=1,
            grid=(1,),
            in_specs=[whole, half] + [WHOLE] * len(extra),
            out_specs=[WHOLE] * (1 + len(extra)),
        ),
        out_shape=[shape(2 * ROWS, HALF)] + [shape(ROWS, 2 * HALF)] * len(extra),
        compiler_params=PARAMS,
        cost_estimate=cost(0, 0.5),
        name="pick_values" if extra else "pick_keys",
    )(ids, own, other, *extra)


def prepare_kernel(
    ids, table, q_own, q_other, g_own, g_other, bias_ref, queries_ref, grads_ref
):
    put_rows(queries_ref, ids[2], q_own, q_other)
    put_rows(grads_ref, ids[2], g_own, g_other)
    base = ids[0] - ids[2]
    lane = lax.broadcasted_iota(jnp.int32, (1, ROWS), 1)
    row = lax.broadcasted_iota(jnp.int32, (STRETCH, ROWS), 0)
    for s in range(2):
        shard = base + s
        stretch = jnp.where(lane < STRETCH, table[2 * shard], table[2 * shard + 1])
        query_pos = shard * ROWS + stretch * STRETCH + (lane & (STRETCH - 1))
        begin = jnp.zeros((1, ROWS), jnp.int32)
        for i in range(NSTART):
            start = table[2 * N_SHARD + i]
            begin = jnp.where(start <= query_pos, start, begin)
        for d in range(SPAN):
            source = shard - (SPAN - 1) + d
            known = jnp.maximum(source, 0)
            for j in range(2):
                key_pos = source * ROWS + table[2 * known + j] * STRETCH + row
                allowed = (key_pos <= query_pos) & (key_pos >= begin)
                bias_ref[s, (2 * d + j) * STRETCH : (2 * d + j + 1) * STRETCH, :] = jnp.where(
                    allowed, 0.0, MASKED
                )


def prepare_call(ids, table, *blocks):
    width = GROUPS * WIDE
    own = pl.BlockSpec((ROWS, width), lambda i, *_: (0, 0))
    other = pl.BlockSpec((ROWS, width), lambda i, ids, *_: (0, ids[2]))
    return pl.pallas_call(
        prepare_kernel,
        grid_spec=pltpu.PrefetchScalarGridSpec(
            num_scalar_prefetch=2,
            grid=(1,),
            in_specs=[own, other] * 2,
            out_specs=[WHOLE] * 3,
        ),
        out_shape=[shape(2, KEYS, ROWS, dtype=F32)] + [shape(2 * ROWS, width)] * 2,
        compiler_params=PARAMS,
        cost_estimate=cost(0, 2.5),
        name="prepare",
    )(ids, table, *blocks)


def spread(out, far1, far2, s0, s1):
    out[:ROWS] = s0[3 * ROWS :] + s1[2 * ROWS : 3 * ROWS]
    out[ROWS:] = s1[3 * ROWS :]
    far1[:ROWS] = (s0[ROWS : 2 * ROWS] + s1[:ROWS]).astype(BF16)
    far1[ROWS:] = (s0[2 * ROWS : 3 * ROWS] + s1[ROWS : 2 * ROWS]).astype(BF16)
    far2[...] = s0[:ROWS].astype(far2.dtype)


def forward_kernel(bias, q_ref, g_ref, k2, k1, k0, prob_ref, own_ref, far1, far2):
    keys = jnp.concatenate([k2[...], k1[...], k0[...]], axis=0)
    terms = []
    for s in range(2):
        rows = slice(s * ROWS, (s + 1) * ROWS)
        window = keys[s * ROWS : s * ROWS + KEYS]
        for h in range(PER_GROUP):
            cols = slice(h * HEAD, (h + 1) * HEAD)
            score = nt(window, q_ref[rows, cols]) * (SCALE * LOG2E) + bias[s]
            weight = jnp.exp2(score - jnp.max(score, axis=0, keepdims=True))
            total = jnp.sum(weight, axis=0, keepdims=True)
            prob_ref[0, s, :, cols] = (weight * (1.0 / total)).astype(BF16)
        terms.append(nn(prob_ref[0, s], stack_heads(g_ref[rows, :])))
    spread(own_ref, far1, far2, *terms)


def backward_kernel(
    ids,
    prob_ref,
    q_ref,
    g_ref,
    k2,
    k1,
    k0,
    v2,
    v1,
    v0,
    keep_ref,
    send_ref,
    own_ref,
    far1,
    far2,
    gq_ref,
):
    core = ids[2]
    keys = jnp.concatenate([k2[...], k1[...], k0[...]], axis=0)
    values = jnp.concatenate([v2[...], v1[...], v0[...]], axis=0)
    terms = []
    for s in range(2):
        rows = slice(s * ROWS, (s + 1) * ROWS)
        window = slice(s * ROWS, s * ROWS + KEYS)
        prob = prob_ref[0, s].astype(F32)
        weighted = prob * nt(values[window], stack_heads(g_ref[rows, :]))
        delta = jnp.sum(weighted, axis=0, keepdims=True)
        grad_score = (weighted - prob * delta).astype(BF16)
        terms.append(nn(grad_score, stack_heads(q_ref[rows, :])) * SCALE)
        query_grad = tn(grad_score, keys[window]) * SCALE
        for h in range(PER_GROUP):
            gq_ref[s, :, h * HEAD : (h + 1) * HEAD] = query_grad[h * ROWS : (h + 1) * ROWS]
    spread(own_ref, far1, far2, *terms)
    keep_ref[...] = gq_ref[core].astype(BF16)
    send_ref[:ROWS] = gq_ref[1 - core]
    send_ref[ROWS:] = gq_ref[core, :EXTRA]


def narrow(rows, shift=0):
    return pl.BlockSpec((rows, HEAD), lambda j, *_: (0, j + shift))


def wide(rows):
    return pl.BlockSpec((rows, WIDE), lambda j, *_: (0, j))


WINDOW = [narrow(ROWS), narrow(2 * ROWS), narrow(2 * ROWS)]
VALUE_WINDOW = [narrow(ROWS, GROUPS)] + WINDOW[1:]
TERMS = [narrow(2 * ROWS), narrow(2 * ROWS), narrow(ROWS)]
PROB_SPEC = pl.BlockSpec((1, 2, KEYS, WIDE), lambda j, *_: (j, 0, 0, 0))


def term_shapes(last):
    return [shape(2 * ROWS, HALF, dtype=F32), shape(2 * ROWS, HALF), shape(ROWS, HALF, dtype=last)]


def forward_call(bias, queries, grads, keys):
    return pl.pallas_call(
        forward_kernel,
        grid=(GROUPS,),
        in_specs=[pl.BlockSpec((2, KEYS, ROWS), lambda j: (0, 0, 0))]
        + [wide(2 * ROWS)] * 2
        + WINDOW,
        out_specs=[PROB_SPEC] + TERMS,
        out_shape=[shape(GROUPS, 2, KEYS, WIDE)] + term_shapes(BF16),
        compiler_params=LARGE,
        cost_estimate=cost(4 * 16 * ROWS * KEYS * HEAD, 6),
        name="forward_and_value_gradient",
    )(bias, queries, grads, *keys)


def backward_call(ids, prob, queries, grads, keys, values):
    return pl.pallas_call(
        backward_kernel,
        grid_spec=pltpu.PrefetchScalarGridSpec(
            num_scalar_prefetch=1,
            grid=(GROUPS,),
            in_specs=[PROB_SPEC] + [wide(2 * ROWS)] * 2 + WINDOW + VALUE_WINDOW,
            out_specs=[wide(ROWS), wide(ROWS + EXTRA)] + TERMS,
            scratch_shapes=[pltpu.VMEM((2, ROWS, WIDE), F32)],
        ),
        out_shape=[
            shape(ROWS, GROUPS * WIDE),
            shape(ROWS + EXTRA, GROUPS * WIDE, dtype=F32),
        ]
        + term_shapes(F32),
        compiler_params=LARGE,
        cost_estimate=cost(6 * 16 * ROWS * KEYS * HEAD, 6),
        name="query_and_key_gradient",
    )(ids, prob, queries, grads, *keys, *values)


def pack_kernel(ids, in_ref, o0, o1, o2, o3):
    for d, out_ref in enumerate((o0, o1, o2, o3)):
        x = (ids[1] + d) & 3
        for z in range(8):
            column = pl.multiple_of((4 * z + x) * HEAD, HEAD)
            out_ref[:, z * HEAD : (z + 1) * HEAD] = in_ref[:, pl.ds(column, HEAD)]


def pack_call(ids, inputs):
    return pl.pallas_call(
        pack_kernel,
        grid_spec=pltpu.PrefetchScalarGridSpec(
            num_scalar_prefetch=1, grid=(1,), in_specs=[WHOLE], out_specs=[WHOLE] * 4
        ),
        out_shape=[shape(ROWS, 8 * HEAD)] * 4,
        compiler_params=PARAMS,
        cost_estimate=cost(0, 2),
        name="pack_inputs",
    )(ids, inputs)


def add_terms(own, r1, r2):
    first = own[:ROWS] + r1[:ROWS].astype(F32)
    second = own[ROWS:] + r1[ROWS:].astype(F32) + r2[...].astype(F32)
    return first.astype(BF16), second.astype(BF16)


def value_total_kernel(ids, own, r1, r2, keep_ref, send_ref, copies_ref):
    core = ids[2]
    first, second = add_terms(own, r1, r2)
    for x in range(4):
        copies_ref[x, :ROWS], copies_ref[x, ROWS:] = first, second
    keep_ref[...] = copies_ref[0, pl.ds(pl.multiple_of(core * ROWS, ROWS), ROWS), :]
    send_ref[...] = copies_ref[0, pl.ds(pl.multiple_of((1 - core) * ROWS, ROWS), ROWS), :]


def key_total_kernel(ids, own, r1, r2, keep_ref, send_ref, both_ref):
    core = ids[2]
    both_ref[:ROWS], both_ref[ROWS:] = add_terms(own, r1, r2)
    keep_ref[...] = both_ref[pl.ds(pl.multiple_of(core * ROWS, ROWS), ROWS), :]
    send_ref[...] = both_ref[pl.ds(pl.multiple_of((1 - core) * ROWS, ROWS), ROWS), :]


def total_call(ids, own, r1, r2, copies):
    return pl.pallas_call(
        value_total_kernel if copies else key_total_kernel,
        grid_spec=pltpu.PrefetchScalarGridSpec(
            num_scalar_prefetch=1,
            grid=(1,),
            in_specs=[WHOLE] * 3,
            out_specs=[WHOLE] * (3 if copies else 2),
            scratch_shapes=[] if copies else [pltpu.VMEM((2 * ROWS, HALF), BF16)],
        ),
        out_shape=[shape(ROWS, HALF)] * 2 + ([shape(4, 2 * ROWS, HALF)] if copies else []),
        compiler_params=PARAMS,
        cost_estimate=cost(0, 1),
        name="value_gradient_total" if copies else "key_gradient_total",
    )(ids, own, r1, r2)


def join_kernel(ids, query, query_other, key, key_other, value, value_other, gq, gk, gv):
    core = ids[2]
    parts = (
        (gq, query[...], query_other[:ROWS]),
        (gk, key[...], key_other[...]),
        (gv, value[...], value_other[...]),
    )
    for out, own, other in parts:
        width = own.shape[1]
        out[:, pl.ds(pl.multiple_of(core * width, HEAD), width)] = own.astype(BF16)
        out[:, pl.ds(pl.multiple_of((1 - core) * width, HEAD), width)] = other.astype(BF16)


def join_call(ids, *blocks):
    return pl.pallas_call(
        join_kernel,
        grid_spec=pltpu.PrefetchScalarGridSpec(
            num_scalar_prefetch=1, grid=(1,), in_specs=[WHOLE] * 6, out_specs=[WHOLE] * 3
        ),
        out_shape=[shape(ROWS, 2 * a.shape[1]) for a in blocks[::2]],
        compiler_params=PARAMS,
        cost_estimate=cost(0, 2),
        name="join_outputs",
    )(ids, *blocks)


def weight_kernel(ids, grads, a0, a1, a2, a3, b0, b1, b2, b3, out_ref):
    x, core = ids[1], ids[2]
    left = [ref[...] for ref in (a0, a1, a2, a3, b0, b1, b2, b3)]
    right = []
    for side in (core, 1 - core):
        rows = pl.ds(pl.multiple_of(side * ROWS, ROWS), ROWS)
        right += [grads[(x + 4 - d) & 3, rows, :] for d in range(4)]
    left, right = jnp.concatenate(left, axis=0), jnp.concatenate(right, axis=0)
    out_ref[...] = tn(left, right).astype(BF16)


def weight_call(ids, grads, own, other):
    taken = pl.BlockSpec((ROWS, 256), lambda i, _: (0, i))
    return pl.pallas_call(
        weight_kernel,
        grid_spec=pltpu.PrefetchScalarGridSpec(
            num_scalar_prefetch=1,
            grid=(4,),
            in_specs=[pl.BlockSpec((4, 2 * ROWS, HALF), lambda i, _: (0, 0, 0))] + [taken] * 8,
            out_specs=pl.BlockSpec((256, HALF), lambda i, _: (i, 0)),
        ),
        out_shape=shape(1024, HALF),
        compiler_params=LARGE,
        cost_estimate=cost(2 * 1024 * 1024 * 256, 3),
        name="weight_gradient",
    )(ids, grads, *own, *other)


def final_kernel(ids, in_ref, keep_ref, send_ref, total_ref):
    core = ids[2]
    total = in_ref[0].astype(F32)
    for i in range(1, 32):
        total += in_ref[i].astype(F32)
    total_ref[...] = total
    keep_ref[...] = total_ref[pl.ds(pl.multiple_of(core * 16, 16), 16), :]
    send_ref[...] = total_ref[pl.ds(pl.multiple_of((1 - core) * 16, 16), 16), :]


def final_call(ids, parts):
    return pl.pallas_call(
        final_kernel,
        grid_spec=pltpu.PrefetchScalarGridSpec(
            num_scalar_prefetch=1,
            grid=(1,),
            in_specs=[WHOLE],
            out_specs=[WHOLE] * 2,
            scratch_shapes=[pltpu.VMEM((32, HALF), F32)],
        ),
        out_shape=[shape(16, HALF, dtype=F32)] * 2,
        compiler_params=PARAMS,
        cost_estimate=cost(0, 0.5),
        name="weight_rows",
    )(ids, parts)


def shift_chips(block, distance):
    route = [(i - distance, i) for i in range(N_CHIP) if 0 <= i - distance < N_CHIP]
    return lax.ppermute(block, CHIP, route)


def shift_x(block, distance):
    return lax.ppermute(block, "x", [(i, (i + distance) % 4) for i in range(4)])


def swap_core(block):
    return lax.ppermute(block, "c", [(0, 1), (1, 0)])


def own_half(block, core):
    width = block.shape[1] // 2
    return lax.dynamic_slice(block, (0, core * width), (ROWS, width))


def shards(query, key, value, grad, inputs, stretch_order, session_starts):
    query, key, value, grad, inputs = query[0], key[0], value[0], grad[0], inputs[0]
    core = lax.axis_index("c")
    ids = jnp.stack([lax.axis_index(CTX), lax.axis_index("x"), core]).astype(jnp.int32)

    table = jnp.concatenate([stretch_order.reshape(-1), session_starts.reshape(-1)])
    key_other, value, table, value_half, key_half = lax.optimization_barrier(
        (swap_core(key), value, table, own_half(value, core), own_half(key, core))
    )
    (key0,) = pick_call(ids, key_half, key_other)
    key0, query, grad, value = lax.optimization_barrier((key0, query, grad, value))
    key1 = shift_chips(key0, 1)
    value0, last = pick_call(ids, value_half, swap_core(value), key0)
    far2 = shift_chips(last, 2)
    keys = [far2, key1, key0]
    bias, queries, grads = prepare_call(
        ids,
        table,
        own_half(query, core),
        swap_core(query),
        own_half(grad, core),
        swap_core(grad),
    )
    bias, value0 = lax.optimization_barrier((bias, value0))
    values = [far2, shift_chips(value0, 1), value0]

    prob, value_own, value_t1, value_t2 = forward_call(bias, queries, grads, keys)
    value_own, inputs = lax.optimization_barrier((value_own, inputs))
    packed = pack_call(ids, inputs)
    own = [packed[0]] + [shift_x(packed[d], d) for d in range(1, 4)]
    other = [swap_core(block) for block in own]
    value_r2 = shift_chips(value_t2, -2)
    value_r1 = shift_chips(value_t1, -1)
    query_keep, query_send, key_own, key_t1, key_t2 = backward_call(
        ids, prob, queries, grads, keys, values
    )
    value_r1, query_send = lax.optimization_barrier((value_r1, query_send))
    value_keep, value_send, sent = total_call(ids, value_own, value_r1, value_r2, True)
    key_r2 = shift_chips(key_t2, -2)
    key_r1 = shift_chips(key_t1, -1)
    gathered = lax.all_to_all(sent, "x", 0, 0, tiled=True)
    partial = weight_call(ids, gathered, own, other)
    partial = lax.all_to_all(partial.reshape(32, 32, HALF), ("zl", "zh", "y"), 0, 0, tiled=True)

    key_keep, key_send = total_call(ids, key_own, key_r1, key_r2, False)
    key_keep, query_send = lax.optimization_barrier((key_keep, query_send))
    grad_query, grad_key, grad_value = join_call(
        ids,
        query_keep,
        swap_core(query_send),
        key_keep,
        swap_core(key_send),
        value_keep,
        swap_core(value_send),
    )
    partial, grad_query = lax.optimization_barrier((partial, grad_query))
    row_keep, row_send = final_call(ids, partial)
    swapped = swap_core(row_send)
    first, second = jnp.where(core == 0, row_keep, swapped), jnp.where(core == 0, swapped, row_keep)
    weight_grad = jnp.concatenate([first, second], axis=1)
    return grad_query[None], grad_key[None], grad_value[None], weight_grad


def solution(mesh):
    fine = Mesh(mesh.devices.reshape(4, 2, 4, 4, 2), AXES)
    rows = P("zl", CTX, None)
    return jax.shard_map(
        shards,
        mesh=fine,
        in_specs=(rows, rows, rows, rows, rows, P("zl", None, None), P("zl", None)),
        out_specs=(rows, rows, rows, P(AXES, None)),
        check_vma=False,
    )
```

```python
import math

import jax
import jax.numpy as jnp
from jax import lax
from jax.experimental import pallas as pl
from jax.experimental.pallas import tpu as pltpu
from jax.sharding import Mesh, PartitionSpec as P

HEAD = 128
STRETCH = 64
SPAN = 4
PER_GROUP = 4
GROUPS = 2
ROWS = 128
KEYS = SPAN * ROWS
WIDE = PER_GROUP * HEAD
HALF = GROUPS * HEAD
MASKED = -1e30
SCALE = HEAD**-0.5
LOG2E = math.log2(math.e)
BF16 = jnp.bfloat16
F32 = jnp.float32
AXES = ("zl", "zh", "x", "y", "c")
CTX = ("zh", "x", "y", "c")
CHIP = ("zh", "x", "y")
N_CHIP = 32
N_SHARD = 64
NSTART = 64
MIB = 1024 * 1024
EXTRA = 96
PARAMS = pltpu.CompilerParams(vmem_limit_bytes=8 * MIB)
LARGE = pltpu.CompilerParams(vmem_limit_bytes=24 * MIB)
WHOLE = pl.BlockSpec(memory_space=pltpu.VMEM)


def nt(a, b):
    return lax.dot_general(a, b, (((1,), (1,)), ((), ())), preferred_element_type=F32)


def tn(a, b):
    return lax.dot_general(a, b, (((0,), (0,)), ((), ())), preferred_element_type=F32)


def nn(a, b):
    return lax.dot_general(a, b, (((1,), (0,)), ((), ())), preferred_element_type=F32)


def shape(*dims, dtype=BF16):
    return jax.ShapeDtypeStruct(dims, dtype)


def cost(flops, mib):
    return pl.CostEstimate(flops=flops, bytes_accessed=int(mib * MIB), transcendentals=0)


def stack_heads(block):
    return jnp.concatenate([block[:, h * HEAD : (h + 1) * HEAD] for h in range(PER_GROUP)], axis=0)


def put_rows(out_ref, core, own, other):
    out_ref[pl.ds(pl.multiple_of(core * ROWS, ROWS), ROWS), :] = own[...]
    out_ref[pl.ds(pl.multiple_of((1 - core) * ROWS, ROWS), ROWS), :] = other[...]


def pick_keys_kernel(ids, own, other, both_ref):
    put_rows(both_ref, ids[2], own, other)


def pick_values_kernel(ids, own, other, keys, both_ref, last_ref):
    put_rows(both_ref, ids[2], own, other)
    last_ref[:, :HALF] = keys[ROWS:]
    last_ref[:, HALF:] = both_ref[ROWS:]


def pick_call(ids, own, other, keys=None):
    half = pl.BlockSpec((ROWS, HALF), lambda i, ids: (0, ids[2]))
    whole = pl.BlockSpec((ROWS, HALF), lambda i, ids: (0, 0))
    extra = [] if keys is None else [keys]
    return pl.pallas_call(
        pick_values_kernel if extra else pick_keys_kernel,
        grid_spec=pltpu.PrefetchScalarGridSpec(
            num_scalar_prefetch=1,
            grid=(1,),
            in_specs=[whole, half] + [WHOLE] * len(extra),
            out_specs=[WHOLE] * (1 + len(extra)),
        ),
        out_shape=[shape(2 * ROWS, HALF)] + [shape(ROWS, 2 * HALF)] * len(extra),
        compiler_params=PARAMS,
        cost_estimate=cost(0, 0.5),
        name="pick_values" if extra else "pick_keys",
    )(ids, own, other, *extra)


def prepare_kernel(
    ids, table, q_own, q_other, g_own, g_other, bias_ref, queries_ref, grads_ref
):
    put_rows(queries_ref, ids[2], q_own, q_other)
    put_rows(grads_ref, ids[2], g_own, g_other)
    base = ids[0] - ids[2]
    lane = lax.broadcasted_iota(jnp.int32, (1, ROWS), 1)
    row = lax.broadcasted_iota(jnp.int32, (STRETCH, ROWS), 0)
    for s in range(2):
        shard = base + s
        stretch = jnp.where(lane < STRETCH, table[2 * shard], table[2 * shard + 1])
        query_pos = shard * ROWS + stretch * STRETCH + (lane & (STRETCH - 1))
        begin = jnp.zeros((1, ROWS), jnp.int32)
        for i in range(NSTART):
            start = table[2 * N_SHARD + i]
            begin = jnp.where(start <= query_pos, start, begin)
        for d in range(SPAN):
            source = shard - (SPAN - 1) + d
            known = jnp.maximum(source, 0)
            for j in range(2):
                key_pos = source * ROWS + table[2 * known + j] * STRETCH + row
                allowed = (key_pos <= query_pos) & (key_pos >= begin)
                bias_ref[s, (2 * d + j) * STRETCH : (2 * d + j + 1) * STRETCH, :] = jnp.where(
                    allowed, 0.0, MASKED
                )


def prepare_call(ids, table, *blocks):
    width = GROUPS * WIDE
    own = pl.BlockSpec((ROWS, width), lambda i, *_: (0, 0))
    other = pl.BlockSpec((ROWS, width), lambda i, ids, *_: (0, ids[2]))
    return pl.pallas_call(
        prepare_kernel,
        grid_spec=pltpu.PrefetchScalarGridSpec(
            num_scalar_prefetch=2,
            grid=(1,),
            in_specs=[own, other] * 2,
            out_specs=[WHOLE] * 3,
        ),
        out_shape=[shape(2, KEYS, ROWS, dtype=F32)] + [shape(2 * ROWS, width)] * 2,
        compiler_params=PARAMS,
        cost_estimate=cost(0, 2.5),
        name="prepare",
    )(ids, table, *blocks)


def spread(out, far1, far2, s0, s1):
    out[:ROWS] = s0[3 * ROWS :] + s1[2 * ROWS : 3 * ROWS]
    out[ROWS:] = s1[3 * ROWS :]
    far1[:ROWS] = (s0[ROWS : 2 * ROWS] + s1[:ROWS]).astype(BF16)
    far1[ROWS:] = (s0[2 * ROWS : 3 * ROWS] + s1[ROWS : 2 * ROWS]).astype(BF16)
    far2[...] = s0[:ROWS].astype(far2.dtype)


def forward_kernel(bias, q_ref, g_ref, k2, k1, k0, prob_ref, own_ref, far1, far2):
    keys = jnp.concatenate([k2[...], k1[...], k0[...]], axis=0)
    terms = []
    for s in range(2):
        rows = slice(s * ROWS, (s + 1) * ROWS)
        window = keys[s * ROWS : s * ROWS + KEYS]
        for h in range(PER_GROUP):
            cols = slice(h * HEAD, (h + 1) * HEAD)
            score = nt(window, q_ref[rows, cols]) * (SCALE * LOG2E) + bias[s]
            weight = jnp.exp2(score - jnp.max(score, axis=0, keepdims=True))
            total = jnp.sum(weight, axis=0, keepdims=True)
            prob_ref[0, s, :, cols] = (weight * (1.0 / total)).astype(BF16)
        terms.append(nn(prob_ref[0, s], stack_heads(g_ref[rows, :])))
    spread(own_ref, far1, far2, *terms)


def backward_kernel(
    ids,
    prob_ref,
    q_ref,
    g_ref,
    k2,
    k1,
    k0,
    v2,
    v1,
    v0,
    keep_ref,
    send_ref,
    own_ref,
    far1,
    far2,
    gq_ref,
):
    core = ids[2]
    keys = jnp.concatenate([k2[...], k1[...], k0[...]], axis=0)
    values = jnp.concatenate([v2[...], v1[...], v0[...]], axis=0)
    terms = []
    for s in range(2):
        rows = slice(s * ROWS, (s + 1) * ROWS)
        window = slice(s * ROWS, s * ROWS + KEYS)
        prob = prob_ref[0, s].astype(F32)
        weighted = prob * nt(values[window], stack_heads(g_ref[rows, :]))
        delta = jnp.sum(weighted, axis=0, keepdims=True)
        grad_score = (weighted - prob * delta).astype(BF16)
        terms.append(nn(grad_score, stack_heads(q_ref[rows, :])) * SCALE)
        query_grad = tn(grad_score, keys[window]) * SCALE
        for h in range(PER_GROUP):
            gq_ref[s, :, h * HEAD : (h + 1) * HEAD] = query_grad[h * ROWS : (h + 1) * ROWS]
    spread(own_ref, far1, far2, *terms)
    keep_ref[...] = gq_ref[core].astype(BF16)
    send_ref[:ROWS] = gq_ref[1 - core]
    send_ref[ROWS:] = gq_ref[core, :EXTRA]


def narrow(rows, shift=0):
    return pl.BlockSpec((rows, HEAD), lambda j, *_: (0, j + shift))


def wide(rows):
    return pl.BlockSpec((rows, WIDE), lambda j, *_: (0, j))


WINDOW = [narrow(ROWS), narrow(2 * ROWS), narrow(2 * ROWS)]
VALUE_WINDOW = [narrow(ROWS, GROUPS)] + WINDOW[1:]
TERMS = [narrow(2 * ROWS), narrow(2 * ROWS), narrow(ROWS)]
PROB_SPEC = pl.BlockSpec((1, 2, KEYS, WIDE), lambda j, *_: (j, 0, 0, 0))


def term_shapes(last):
    return [shape(2 * ROWS, HALF, dtype=F32), shape(2 * ROWS, HALF), shape(ROWS, HALF, dtype=last)]


def forward_call(bias, queries, grads, keys):
    return pl.pallas_call(
        forward_kernel,
        grid=(GROUPS,),
        in_specs=[pl.BlockSpec((2, KEYS, ROWS), lambda j: (0, 0, 0))]
        + [wide(2 * ROWS)] * 2
        + WINDOW,
        out_specs=[PROB_SPEC] + TERMS,
        out_shape=[shape(GROUPS, 2, KEYS, WIDE)] + term_shapes(F32),
        compiler_params=LARGE,
        cost_estimate=cost(4 * 16 * ROWS * KEYS * HEAD, 6),
        name="forward_and_value_gradient",
    )(bias, queries, grads, *keys)


def backward_call(ids, prob, queries, grads, keys, values):
    return pl.pallas_call(
        backward_kernel,
        grid_spec=pltpu.PrefetchScalarGridSpec(
            num_scalar_prefetch=1,
            grid=(GROUPS,),
            in_specs=[PROB_SPEC] + [wide(2 * ROWS)] * 2 + WINDOW + VALUE_WINDOW,
            out_specs=[wide(ROWS), wide(ROWS + EXTRA)] + TERMS,
            scratch_shapes=[pltpu.VMEM((2, ROWS, WIDE), F32)],
        ),
        out_shape=[
            shape(ROWS, GROUPS * WIDE),
            shape(ROWS + EXTRA, GROUPS * WIDE, dtype=F32),
        ]
        + term_shapes(F32),
        compiler_params=LARGE,
        cost_estimate=cost(6 * 16 * ROWS * KEYS * HEAD, 6),
        name="query_and_key_gradient",
    )(ids, prob, queries, grads, *keys, *values)


def pack_kernel(ids, in_ref, o0, o1, o2, o3):
    for d, out_ref in enumerate((o0, o1, o2, o3)):
        x = (ids[1] + d) & 3
        for z in range(8):
            column = pl.multiple_of((4 * z + x) * HEAD, HEAD)
            out_ref[:, z * HEAD : (z + 1) * HEAD] = in_ref[:, pl.ds(column, HEAD)]


def pack_call(ids, inputs):
    return pl.pallas_call(
        pack_kernel,
        grid_spec=pltpu.PrefetchScalarGridSpec(
            num_scalar_prefetch=1, grid=(1,), in_specs=[WHOLE], out_specs=[WHOLE] * 4
        ),
        out_shape=[shape(ROWS, 8 * HEAD)] * 4,
        compiler_params=PARAMS,
        cost_estimate=cost(0, 2),
        name="pack_inputs",
    )(ids, inputs)


def add_terms(own, r1, r2):
    first = own[:ROWS] + r1[:ROWS].astype(F32)
    second = own[ROWS:] + r1[ROWS:].astype(F32) + r2[...].astype(F32)
    return first.astype(BF16), second.astype(BF16)


def value_total_kernel(ids, own, r1, r2, keep_ref, send_ref, copies_ref):
    core = ids[2]
    first, second = add_terms(own, r1, r2)
    for x in range(4):
        copies_ref[x, :ROWS], copies_ref[x, ROWS:] = first, second
    keep_ref[...] = copies_ref[0, pl.ds(pl.multiple_of(core * ROWS, ROWS), ROWS), :]
    send_ref[...] = copies_ref[0, pl.ds(pl.multiple_of((1 - core) * ROWS, ROWS), ROWS), :]


def key_total_kernel(ids, own, r1, r2, keep_ref, send_ref, both_ref):
    core = ids[2]
    both_ref[:ROWS], both_ref[ROWS:] = add_terms(own, r1, r2)
    keep_ref[...] = both_ref[pl.ds(pl.multiple_of(core * ROWS, ROWS), ROWS), :]
    send_ref[...] = both_ref[pl.ds(pl.multiple_of((1 - core) * ROWS, ROWS), ROWS), :]


def total_call(ids, own, r1, r2, copies):
    return pl.pallas_call(
        value_total_kernel if copies else key_total_kernel,
        grid_spec=pltpu.PrefetchScalarGridSpec(
            num_scalar_prefetch=1,
            grid=(1,),
            in_specs=[WHOLE] * 3,
            out_specs=[WHOLE] * (3 if copies else 2),
            scratch_shapes=[] if copies else [pltpu.VMEM((2 * ROWS, HALF), BF16)],
        ),
        out_shape=[shape(ROWS, HALF)] * 2 + ([shape(4, 2 * ROWS, HALF)] if copies else []),
        compiler_params=PARAMS,
        cost_estimate=cost(0, 1),
        name="value_gradient_total" if copies else "key_gradient_total",
    )(ids, own, r1, r2)


def join_kernel(ids, query, query_other, key, key_other, value, value_other, gq, gk, gv):
    core = ids[2]
    parts = (
        (gq, query[...], query_other[:ROWS]),
        (gk, key[...], key_other[...]),
        (gv, value[...], value_other[...]),
    )
    for out, own, other in parts:
        width = own.shape[1]
        out[:, pl.ds(pl.multiple_of(core * width, HEAD), width)] = own.astype(BF16)
        out[:, pl.ds(pl.multiple_of((1 - core) * width, HEAD), width)] = other.astype(BF16)


def join_call(ids, *blocks):
    return pl.pallas_call(
        join_kernel,
        grid_spec=pltpu.PrefetchScalarGridSpec(
            num_scalar_prefetch=1, grid=(1,), in_specs=[WHOLE] * 6, out_specs=[WHOLE] * 3
        ),
        out_shape=[shape(ROWS, 2 * a.shape[1]) for a in blocks[::2]],
        compiler_params=PARAMS,
        cost_estimate=cost(0, 2),
        name="join_outputs",
    )(ids, *blocks)


def weight_kernel(ids, grads, a0, a1, a2, a3, b0, b1, b2, b3, out_ref):
    x, core = ids[1], ids[2]
    left = [ref[...] for ref in (a0, a1, a2, a3, b0, b1, b2, b3)]
    right = []
    for side in (core, 1 - core):
        rows = pl.ds(pl.multiple_of(side * ROWS, ROWS), ROWS)
        right += [grads[(x + 4 - d) & 3, rows, :] for d in range(4)]
    left, right = jnp.concatenate(left, axis=0), jnp.concatenate(right, axis=0)
    out_ref[...] = tn(left, right).astype(BF16)


def weight_call(ids, grads, own, other):
    taken = pl.BlockSpec((ROWS, 256), lambda i, _: (0, i))
    return pl.pallas_call(
        weight_kernel,
        grid_spec=pltpu.PrefetchScalarGridSpec(
            num_scalar_prefetch=1,
            grid=(4,),
            in_specs=[pl.BlockSpec((4, 2 * ROWS, HALF), lambda i, _: (0, 0, 0))] + [taken] * 8,
            out_specs=pl.BlockSpec((256, HALF), lambda i, _: (i, 0)),
        ),
        out_shape=shape(1024, HALF),
        compiler_params=LARGE,
        cost_estimate=cost(2 * 1024 * 1024 * 256, 3),
        name="weight_gradient",
    )(ids, grads, *own, *other)


def final_kernel(ids, in_ref, keep_ref, send_ref, total_ref):
    core = ids[2]
    total = in_ref[0].astype(F32)
    for i in range(1, 32):
        total += in_ref[i].astype(F32)
    total_ref[...] = total
    keep_ref[...] = total_ref[pl.ds(pl.multiple_of(core * 16, 16), 16), :]
    send_ref[...] = total_ref[pl.ds(pl.multiple_of((1 - core) * 16, 16), 16), :]


def final_call(ids, parts):
    return pl.pallas_call(
        final_kernel,
        grid_spec=pltpu.PrefetchScalarGridSpec(
            num_scalar_prefetch=1,
            grid=(1,),
            in_specs=[WHOLE],
            out_specs=[WHOLE] * 2,
            scratch_shapes=[pltpu.VMEM((32, HALF), F32)],
        ),
        out_shape=[shape(16, HALF, dtype=F32)] * 2,
        compiler_params=PARAMS,
        cost_estimate=cost(0, 0.5),
        name="weight_rows",
    )(ids, parts)


def shift_chips(block, distance):
    route = [(i - distance, i) for i in range(N_CHIP) if 0 <= i - distance < N_CHIP]
    return lax.ppermute(block, CHIP, route)


def shift_x(block, distance):
    return lax.ppermute(block, "x", [(i, (i + distance) % 4) for i in range(4)])


def swap_core(block):
    return lax.ppermute(block, "c", [(0, 1), (1, 0)])


def own_half(block, core):
    width = block.shape[1] // 2
    return lax.dynamic_slice(block, (0, core * width), (ROWS, width))


def shards(query, key, value, grad, inputs, stretch_order, session_starts):
    query, key, value, grad, inputs = query[0], key[0], value[0], grad[0], inputs[0]
    core = lax.axis_index("c")
    ids = jnp.stack([lax.axis_index(CTX), lax.axis_index("x"), core]).astype(jnp.int32)

    table = jnp.concatenate([stretch_order.reshape(-1), session_starts.reshape(-1)])
    key_other, value, table, value_half, key_half = lax.optimization_barrier(
        (swap_core(key), value, table, own_half(value, core), own_half(key, core))
    )
    (key0,) = pick_call(ids, key_half, key_other)
    key0, query, grad, value = lax.optimization_barrier((key0, query, grad, value))
    key1 = shift_chips(key0, 1)
    value0, last = pick_call(ids, value_half, swap_core(value), key0)
    far2 = shift_chips(last, 2)
    keys = [far2, key1, key0]
    bias, queries, grads = prepare_call(
        ids,
        table,
        own_half(query, core),
        swap_core(query),
        own_half(grad, core),
        swap_core(grad),
    )
    bias, value0 = lax.optimization_barrier((bias, value0))
    values = [far2, shift_chips(value0, 1), value0]

    prob, value_own, value_t1, value_t2 = forward_call(bias, queries, grads, keys)
    value_own, inputs = lax.optimization_barrier((value_own, inputs))
    packed = pack_call(ids, inputs)
    own = [packed[0]] + [shift_x(packed[d], d) for d in range(1, 4)]
    other = [swap_core(block) for block in own]
    value_r2 = shift_chips(value_t2, -2)
    value_r1 = shift_chips(value_t1, -1)
    query_keep, query_send, key_own, key_t1, key_t2 = backward_call(
        ids, prob, queries, grads, keys, values
    )
    value_r1, query_send = lax.optimization_barrier((value_r1, query_send))
    value_keep, value_send, sent = total_call(ids, value_own, value_r1, value_r2, True)
    key_r2 = shift_chips(key_t2, -2)
    key_r1 = shift_chips(key_t1, -1)
    gathered = lax.all_to_all(sent, "x", 0, 0, tiled=True)
    partial = weight_call(ids, gathered, own, other)
    partial = lax.all_to_all(partial.reshape(32, 32, HALF), ("zl", "zh", "y"), 0, 0, tiled=True)

    key_keep, key_send = total_call(ids, key_own, key_r1, key_r2, False)
    key_keep, query_send = lax.optimization_barrier((key_keep, query_send))
    grad_query, grad_key, grad_value = join_call(
        ids,
        query_keep,
        swap_core(query_send),
        key_keep,
        swap_core(key_send),
        value_keep,
        swap_core(value_send),
    )
    partial, grad_query = lax.optimization_barrier((partial, grad_query))
    row_keep, row_send = final_call(ids, partial)
    swapped = swap_core(row_send)
    first, second = jnp.where(core == 0, row_keep, swapped), jnp.where(core == 0, swapped, row_keep)
    weight_grad = jnp.concatenate([first, second], axis=1)
    return grad_query[None], grad_key[None], grad_value[None], weight_grad


def solution(mesh):
    fine = Mesh(mesh.devices.reshape(4, 2, 4, 4, 2), AXES)
    rows = P("zl", CTX, None)
    return jax.shard_map(
        shards,
        mesh=fine,
        in_specs=(rows, rows, rows, rows, rows, P("zl", None, None), P("zl", None)),
        out_specs=(rows, rows, rows, P(AXES, None)),
        check_vma=False,
    )
```

```python
import math

import jax
import jax.numpy as jnp
from jax import lax
from jax.experimental import pallas as pl
from jax.experimental.pallas import tpu as pltpu
from jax.sharding import Mesh, PartitionSpec as P

HEAD = 128
STRETCH = 64
SPAN = 4
PER_GROUP = 4
GROUPS = 2
ROWS = 128
KEYS = SPAN * ROWS
WIDE = PER_GROUP * HEAD
HALF = GROUPS * HEAD
MASKED = -1e30
SCALE = HEAD**-0.5
LOG2E = math.log2(math.e)
BF16 = jnp.bfloat16
F32 = jnp.float32
AXES = ("zl", "zh", "x", "y", "c")
CTX = ("zh", "x", "y", "c")
CHIP = ("zh", "x", "y")
N_CHIP = 32
N_SHARD = 64
NSTART = 64
MIB = 1024 * 1024
EXTRA = 96
PARAMS = pltpu.CompilerParams(vmem_limit_bytes=8 * MIB)
LARGE = pltpu.CompilerParams(vmem_limit_bytes=24 * MIB)
WHOLE = pl.BlockSpec(memory_space=pltpu.VMEM)


def nt(a, b):
    return lax.dot_general(a, b, (((1,), (1,)), ((), ())), preferred_element_type=F32)


def tn(a, b):
    return lax.dot_general(a, b, (((0,), (0,)), ((), ())), preferred_element_type=F32)


def nn(a, b):
    return lax.dot_general(a, b, (((1,), (0,)), ((), ())), preferred_element_type=F32)


def shape(*dims, dtype=BF16):
    return jax.ShapeDtypeStruct(dims, dtype)


def cost(flops, mib):
    return pl.CostEstimate(flops=flops, bytes_accessed=int(mib * MIB), transcendentals=0)


def stack_heads(block):
    return jnp.concatenate([block[:, h * HEAD : (h + 1) * HEAD] for h in range(PER_GROUP)], axis=0)


def put_rows(out_ref, core, own, other):
    out_ref[pl.ds(pl.multiple_of(core * ROWS, ROWS), ROWS), :] = own[...]
    out_ref[pl.ds(pl.multiple_of((1 - core) * ROWS, ROWS), ROWS), :] = other[...]


def pick_keys_kernel(ids, own, other, both_ref):
    put_rows(both_ref, ids[2], own, other)


def pick_values_kernel(ids, own, other, keys, both_ref, last_ref):
    put_rows(both_ref, ids[2], own, other)
    last_ref[:, :HALF] = keys[ROWS:]
    last_ref[:, HALF:] = both_ref[ROWS:]


def pick_call(ids, own, other, keys=None):
    half = pl.BlockSpec((ROWS, HALF), lambda i, ids: (0, ids[2]))
    whole = pl.BlockSpec((ROWS, HALF), lambda i, ids: (0, 0))
    extra = [] if keys is None else [keys]
    return pl.pallas_call(
        pick_values_kernel if extra else pick_keys_kernel,
        grid_spec=pltpu.PrefetchScalarGridSpec(
            num_scalar_prefetch=1,
            grid=(1,),
            in_specs=[whole, half] + [WHOLE] * len(extra),
            out_specs=[WHOLE] * (1 + len(extra)),
        ),
        out_shape=[shape(2 * ROWS, HALF)] + [shape(ROWS, 2 * HALF)] * len(extra),
        compiler_params=PARAMS,
        cost_estimate=cost(0, 0.5),
        name="pick_values" if extra else "pick_keys",
    )(ids, own, other, *extra)


def prepare_kernel(
    ids, table, q_own, q_other, g_own, g_other, bias_ref, queries_ref, grads_ref
):
    put_rows(queries_ref, ids[2], q_own, q_other)
    put_rows(grads_ref, ids[2], g_own, g_other)
    base = ids[0] - ids[2]
    lane = lax.broadcasted_iota(jnp.int32, (1, ROWS), 1)
    row = lax.broadcasted_iota(jnp.int32, (STRETCH, ROWS), 0)
    for s in range(2):
        shard = base + s
        stretch = jnp.where(lane < STRETCH, table[2 * shard], table[2 * shard + 1])
        query_pos = shard * ROWS + stretch * STRETCH + (lane & (STRETCH - 1))
        begin = jnp.zeros((1, ROWS), jnp.int32)
        for i in range(NSTART):
            start = table[2 * N_SHARD + i]
            begin = jnp.where(start <= query_pos, start, begin)
        for d in range(SPAN):
            source = shard - (SPAN - 1) + d
            known = jnp.maximum(source, 0)
            for j in range(2):
                key_pos = source * ROWS + table[2 * known + j] * STRETCH + row
                allowed = (key_pos <= query_pos) & (key_pos >= begin)
                bias_ref[s, (2 * d + j) * STRETCH : (2 * d + j + 1) * STRETCH, :] = jnp.where(
                    allowed, 0.0, MASKED
                )


def prepare_call(ids, table, *blocks):
    width = GROUPS * WIDE
    own = pl.BlockSpec((ROWS, width), lambda i, *_: (0, 0))
    other = pl.BlockSpec((ROWS, width), lambda i, ids, *_: (0, ids[2]))
    return pl.pallas_call(
        prepare_kernel,
        grid_spec=pltpu.PrefetchScalarGridSpec(
            num_scalar_prefetch=2,
            grid=(1,),
            in_specs=[own, other] * 2,
            out_specs=[WHOLE] * 3,
        ),
        out_shape=[shape(2, KEYS, ROWS, dtype=F32)] + [shape(2 * ROWS, width)] * 2,
        compiler_params=PARAMS,
        cost_estimate=cost(0, 2.5),
        name="prepare",
    )(ids, table, *blocks)


def spread(out, far1, far2, s0, s1):
    out[:ROWS] = s0[3 * ROWS :] + s1[2 * ROWS : 3 * ROWS]
    out[ROWS:] = s1[3 * ROWS :]
    far1[:ROWS] = (s0[ROWS : 2 * ROWS] + s1[:ROWS]).astype(BF16)
    far1[ROWS:] = (s0[2 * ROWS : 3 * ROWS] + s1[ROWS : 2 * ROWS]).astype(BF16)
    far2[...] = s0[:ROWS].astype(far2.dtype)


def forward_kernel(bias, q_ref, g_ref, k2, k1, k0, prob_ref, own_ref, far1, far2):
    keys = jnp.concatenate([k2[...], k1[...], k0[...]], axis=0)
    terms = []
    for s in range(2):
        rows = slice(s * ROWS, (s + 1) * ROWS)
        window = keys[s * ROWS : s * ROWS + KEYS]
        for h in range(PER_GROUP):
            cols = slice(h * HEAD, (h + 1) * HEAD)
            score = nt(window, q_ref[rows, cols]) * (SCALE * LOG2E) + bias[s]
            weight = jnp.exp2(score - jnp.max(score, axis=0, keepdims=True))
            total = jnp.sum(weight, axis=0, keepdims=True)
            prob_ref[0, s, :, cols] = (weight * (1.0 / total)).astype(BF16)
        terms.append(nn(prob_ref[0, s], stack_heads(g_ref[rows, :])))
    spread(own_ref, far1, far2, *terms)


def backward_kernel(
    ids,
    prob_ref,
    q_ref,
    g_ref,
    k2,
    k1,
    k0,
    v2,
    v1,
    v0,
    keep_ref,
    send_ref,
    own_ref,
    far1,
    far2,
    gq_ref,
):
    core = ids[2]
    keys = jnp.concatenate([k2[...], k1[...], k0[...]], axis=0)
    values = jnp.concatenate([v2[...], v1[...], v0[...]], axis=0)
    terms = []
    for s in range(2):
        rows = slice(s * ROWS, (s + 1) * ROWS)
        window = slice(s * ROWS, s * ROWS + KEYS)
        prob = prob_ref[0, s].astype(F32)
        weighted = prob * nt(values[window], stack_heads(g_ref[rows, :]))
        delta = jnp.sum(weighted, axis=0, keepdims=True)
        grad_score = (weighted - prob * delta).astype(BF16)
        terms.append(nn(grad_score, stack_heads(q_ref[rows, :])) * SCALE)
        query_grad = tn(grad_score, keys[window]) * SCALE
        for h in range(PER_GROUP):
            gq_ref[s, :, h * HEAD : (h + 1) * HEAD] = query_grad[h * ROWS : (h + 1) * ROWS]
    spread(own_ref, far1, far2, *terms)
    keep_ref[...] = gq_ref[core].astype(BF16)
    send_ref[:ROWS] = gq_ref[1 - core]
    send_ref[ROWS:] = gq_ref[core, :EXTRA]


def narrow(rows, shift=0):
    return pl.BlockSpec((rows, HEAD), lambda j, *_: (0, j + shift))


def wide(rows):
    return pl.BlockSpec((rows, WIDE), lambda j, *_: (0, j))


WINDOW = [narrow(ROWS), narrow(2 * ROWS), narrow(2 * ROWS)]
VALUE_WINDOW = [narrow(ROWS, GROUPS)] + WINDOW[1:]
TERMS = [narrow(2 * ROWS), narrow(2 * ROWS), narrow(ROWS)]
PROB_SPEC = pl.BlockSpec((1, 2, KEYS, WIDE), lambda j, *_: (j, 0, 0, 0))


def term_shapes(last):
    return [shape(2 * ROWS, HALF, dtype=F32), shape(2 * ROWS, HALF), shape(ROWS, HALF, dtype=last)]


def forward_call(bias, queries, grads, keys):
    return pl.pallas_call(
        forward_kernel,
        grid=(GROUPS,),
        in_specs=[pl.BlockSpec((2, KEYS, ROWS), lambda j: (0, 0, 0))]
        + [wide(2 * ROWS)] * 2
        + WINDOW,
        out_specs=[PROB_SPEC] + TERMS,
        out_shape=[shape(GROUPS, 2, KEYS, WIDE)] + term_shapes(BF16),
        compiler_params=LARGE,
        cost_estimate=cost(4 * 16 * ROWS * KEYS * HEAD, 6),
        name="forward_and_value_gradient",
    )(bias, queries, grads, *keys)


def backward_call(ids, prob, queries, grads, keys, values):
    return pl.pallas_call(
        backward_kernel,
        grid_spec=pltpu.PrefetchScalarGridSpec(
            num_scalar_prefetch=1,
            grid=(GROUPS,),
            in_specs=[PROB_SPEC] + [wide(2 * ROWS)] * 2 + WINDOW + VALUE_WINDOW,
            out_specs=[wide(ROWS), wide(ROWS + EXTRA)] + TERMS,
            scratch_shapes=[pltpu.VMEM((2, ROWS, WIDE), F32)],
        ),
        out_shape=[
            shape(ROWS, GROUPS * WIDE),
            shape(ROWS + EXTRA, GROUPS * WIDE, dtype=F32),
        ]
        + term_shapes(F32),
        compiler_params=LARGE,
        cost_estimate=cost(6 * 16 * ROWS * KEYS * HEAD, 6),
        name="query_and_key_gradient",
    )(ids, prob, queries, grads, *keys, *values)


def widen_kernel(in_ref, out_ref):
    out_ref[...] = in_ref[...].astype(F32)


def widen_call(block):
    return pl.pallas_call(
        widen_kernel,
        out_shape=shape(*block.shape, dtype=F32),
        compiler_params=PARAMS,
        cost_estimate=cost(0, 0.25),
        name="widen",
    )(block)


def pack_kernel(ids, in_ref, o0, o1, o2, o3):
    for d, out_ref in enumerate((o0, o1, o2, o3)):
        x = (ids[1] + d) & 3
        for z in range(8):
            column = pl.multiple_of((4 * z + x) * HEAD, HEAD)
            out_ref[:, z * HEAD : (z + 1) * HEAD] = in_ref[:, pl.ds(column, HEAD)]


def pack_call(ids, inputs):
    return pl.pallas_call(
        pack_kernel,
        grid_spec=pltpu.PrefetchScalarGridSpec(
            num_scalar_prefetch=1, grid=(1,), in_specs=[WHOLE], out_specs=[WHOLE] * 4
        ),
        out_shape=[shape(ROWS, 8 * HEAD)] * 4,
        compiler_params=PARAMS,
        cost_estimate=cost(0, 2),
        name="pack_inputs",
    )(ids, inputs)


def add_terms(own, r1, r2):
    first = own[:ROWS] + r1[:ROWS].astype(F32)
    second = own[ROWS:] + r1[ROWS:].astype(F32) + r2[...].astype(F32)
    return first.astype(BF16), second.astype(BF16)


def value_total_kernel(ids, own, r1, r2, keep_ref, send_ref, copies_ref):
    core = ids[2]
    first, second = add_terms(own, r1, r2)
    for x in range(4):
        copies_ref[x, :ROWS], copies_ref[x, ROWS:] = first, second
    keep_ref[...] = copies_ref[0, pl.ds(pl.multiple_of(core * ROWS, ROWS), ROWS), :]
    send_ref[...] = copies_ref[0, pl.ds(pl.multiple_of((1 - core) * ROWS, ROWS), ROWS), :]


def key_total_kernel(ids, own, r1, r2, keep_ref, send_ref, both_ref):
    core = ids[2]
    both_ref[:ROWS], both_ref[ROWS:] = add_terms(own, r1, r2)
    keep_ref[...] = both_ref[pl.ds(pl.multiple_of(core * ROWS, ROWS), ROWS), :]
    send_ref[...] = both_ref[pl.ds(pl.multiple_of((1 - core) * ROWS, ROWS), ROWS), :]


def total_call(ids, own, r1, r2, copies):
    return pl.pallas_call(
        value_total_kernel if copies else key_total_kernel,
        grid_spec=pltpu.PrefetchScalarGridSpec(
            num_scalar_prefetch=1,
            grid=(1,),
            in_specs=[WHOLE] * 3,
            out_specs=[WHOLE] * (3 if copies else 2),
            scratch_shapes=[] if copies else [pltpu.VMEM((2 * ROWS, HALF), BF16)],
        ),
        out_shape=[shape(ROWS, HALF)] * 2 + ([shape(4, 2 * ROWS, HALF)] if copies else []),
        compiler_params=PARAMS,
        cost_estimate=cost(0, 1),
        name="value_gradient_total" if copies else "key_gradient_total",
    )(ids, own, r1, r2)


def join_kernel(ids, query, query_other, key, key_other, value, value_other, gq, gk, gv):
    core = ids[2]
    parts = (
        (gq, query[...], query_other[:ROWS]),
        (gk, key[...], key_other[...]),
        (gv, value[...], value_other[...]),
    )
    for out, own, other in parts:
        width = own.shape[1]
        out[:, pl.ds(pl.multiple_of(core * width, HEAD), width)] = own.astype(BF16)
        out[:, pl.ds(pl.multiple_of((1 - core) * width, HEAD), width)] = other.astype(BF16)


def join_call(ids, *blocks):
    return pl.pallas_call(
        join_kernel,
        grid_spec=pltpu.PrefetchScalarGridSpec(
            num_scalar_prefetch=1, grid=(1,), in_specs=[WHOLE] * 6, out_specs=[WHOLE] * 3
        ),
        out_shape=[shape(ROWS, 2 * a.shape[1]) for a in blocks[::2]],
        compiler_params=PARAMS,
        cost_estimate=cost(0, 2),
        name="join_outputs",
    )(ids, *blocks)


def weight_kernel(ids, grads, a0, a1, a2, a3, b0, b1, b2, b3, out_ref):
    x, core = ids[1], ids[2]
    left = [ref[...] for ref in (a0, a1, a2, a3, b0, b1, b2, b3)]
    right = []
    for side in (core, 1 - core):
        rows = pl.ds(pl.multiple_of(side * ROWS, ROWS), ROWS)
        right += [grads[(x + 4 - d) & 3, rows, :] for d in range(4)]
    left, right = jnp.concatenate(left, axis=0), jnp.concatenate(right, axis=0)
    out_ref[...] = tn(left, right).astype(BF16)


def weight_call(ids, grads, own, other):
    taken = pl.BlockSpec((ROWS, 256), lambda i, _: (0, i))
    return pl.pallas_call(
        weight_kernel,
        grid_spec=pltpu.PrefetchScalarGridSpec(
            num_scalar_prefetch=1,
            grid=(4,),
            in_specs=[pl.BlockSpec((4, 2 * ROWS, HALF), lambda i, _: (0, 0, 0))] + [taken] * 8,
            out_specs=pl.BlockSpec((256, HALF), lambda i, _: (i, 0)),
        ),
        out_shape=shape(1024, HALF),
        compiler_params=LARGE,
        cost_estimate=cost(2 * 1024 * 1024 * 256, 3),
        name="weight_gradient",
    )(ids, grads, *own, *other)


def final_kernel(ids, in_ref, keep_ref, send_ref, total_ref):
    core = ids[2]
    total = in_ref[0].astype(F32)
    for i in range(1, 32):
        total += in_ref[i].astype(F32)
    total_ref[...] = total
    keep_ref[...] = total_ref[pl.ds(pl.multiple_of(core * 16, 16), 16), :]
    send_ref[...] = total_ref[pl.ds(pl.multiple_of((1 - core) * 16, 16), 16), :]


def final_call(ids, parts):
    return pl.pallas_call(
        final_kernel,
        grid_spec=pltpu.PrefetchScalarGridSpec(
            num_scalar_prefetch=1,
            grid=(1,),
            in_specs=[WHOLE],
            out_specs=[WHOLE] * 2,
            scratch_shapes=[pltpu.VMEM((32, HALF), F32)],
        ),
        out_shape=[shape(16, HALF, dtype=F32)] * 2,
        compiler_params=PARAMS,
        cost_estimate=cost(0, 0.5),
        name="weight_rows",
    )(ids, parts)


def shift_chips(block, distance):
    route = [(i - distance, i) for i in range(N_CHIP) if 0 <= i - distance < N_CHIP]
    return lax.ppermute(block, CHIP, route)


def shift_x(block, distance):
    return lax.ppermute(block, "x", [(i, (i + distance) % 4) for i in range(4)])


def swap_core(block):
    return lax.ppermute(block, "c", [(0, 1), (1, 0)])


def own_half(block, core):
    width = block.shape[1] // 2
    return lax.dynamic_slice(block, (0, core * width), (ROWS, width))


def shards(query, key, value, grad, inputs, stretch_order, session_starts):
    query, key, value, grad, inputs = query[0], key[0], value[0], grad[0], inputs[0]
    core = lax.axis_index("c")
    ids = jnp.stack([lax.axis_index(CTX), lax.axis_index("x"), core]).astype(jnp.int32)

    table = jnp.concatenate([stretch_order.reshape(-1), session_starts.reshape(-1)])
    key_other, value, table, value_half, key_half = lax.optimization_barrier(
        (swap_core(key), value, table, own_half(value, core), own_half(key, core))
    )
    (key0,) = pick_call(ids, key_half, key_other)
    key0, query, grad, value = lax.optimization_barrier((key0, query, grad, value))
    key1 = shift_chips(key0, 1)
    value0, last = pick_call(ids, value_half, swap_core(value), key0)
    far2 = shift_chips(last, 2)
    keys = [far2, key1, key0]
    bias, queries, grads = prepare_call(
        ids,
        table,
        own_half(query, core),
        swap_core(query),
        own_half(grad, core),
        swap_core(grad),
    )
    bias, value0 = lax.optimization_barrier((bias, value0))
    values = [far2, shift_chips(value0, 1), value0]

    prob, value_own, value_t1, value_t2 = forward_call(bias, queries, grads, keys)
    value_own, inputs = lax.optimization_barrier((value_own, inputs))
    packed = pack_call(ids, inputs)
    own = [packed[0]] + [shift_x(packed[d], d) for d in range(1, 4)]
    other = [swap_core(block) for block in own]
    value_r2 = widen_call(shift_chips(value_t2, -2))
    value_r1 = shift_chips(value_t1, -1)
    query_keep, query_send, key_own, key_t1, key_t2 = backward_call(
        ids, prob, queries, grads, keys, values
    )
    value_r1, query_send = lax.optimization_barrier((value_r1, query_send))
    value_keep, value_send, sent = total_call(ids, value_own, value_r1, value_r2, True)
    key_r2 = shift_chips(key_t2, -2)
    key_r1 = shift_chips(key_t1, -1)
    gathered = lax.all_to_all(sent, "x", 0, 0, tiled=True)
    partial = weight_call(ids, gathered, own, other)
    partial = lax.all_to_all(partial.reshape(32, 32, HALF), ("zl", "zh", "y"), 0, 0, tiled=True)

    key_keep, key_send = total_call(ids, key_own, key_r1, key_r2, False)
    key_keep, query_send = lax.optimization_barrier((key_keep, query_send))
    grad_query, grad_key, grad_value = join_call(
        ids,
        query_keep,
        swap_core(query_send),
        key_keep,
        swap_core(key_send),
        value_keep,
        swap_core(value_send),
    )
    partial, grad_query = lax.optimization_barrier((partial, grad_query))
    row_keep, row_send = final_call(ids, partial)
    swapped = swap_core(row_send)
    first, second = jnp.where(core == 0, row_keep, swapped), jnp.where(core == 0, swapped, row_keep)
    weight_grad = jnp.concatenate([first, second], axis=1)
    return grad_query[None], grad_key[None], grad_value[None], weight_grad


def solution(mesh):
    fine = Mesh(mesh.devices.reshape(4, 2, 4, 4, 2), AXES)
    rows = P("zl", CTX, None)
    return jax.shard_map(
        shards,
        mesh=fine,
        in_specs=(rows, rows, rows, rows, rows, P("zl", None, None), P("zl", None)),
        out_specs=(rows, rows, rows, P(AXES, None)),
        check_vma=False,
    )
```

```python
import math

import jax
import jax.numpy as jnp
from jax import lax
from jax.experimental import pallas as pl
from jax.experimental.pallas import tpu as pltpu
from jax.sharding import Mesh, PartitionSpec as P

HEAD = 128
STRETCH = 64
SPAN = 4
PER_GROUP = 4
GROUPS = 2
ROWS = 128
KEYS = SPAN * ROWS
WIDE = PER_GROUP * HEAD
HALF = GROUPS * HEAD
MASKED = -1e30
SCALE = HEAD**-0.5
LOG2E = math.log2(math.e)
BF16 = jnp.bfloat16
F32 = jnp.float32
AXES = ("zl", "zh", "x", "y", "c")
CTX = ("zh", "x", "y", "c")
CHIP = ("zh", "x", "y")
N_CHIP = 32
N_SHARD = 64
NSTART = 64
MIB = 1024 * 1024
EXTRA = 96
PARAMS = pltpu.CompilerParams(vmem_limit_bytes=8 * MIB)
LARGE = pltpu.CompilerParams(vmem_limit_bytes=24 * MIB)
WHOLE = pl.BlockSpec(memory_space=pltpu.VMEM)


def nt(a, b):
    return lax.dot_general(a, b, (((1,), (1,)), ((), ())), preferred_element_type=F32)


def tn(a, b):
    return lax.dot_general(a, b, (((0,), (0,)), ((), ())), preferred_element_type=F32)


def nn(a, b):
    return lax.dot_general(a, b, (((1,), (0,)), ((), ())), preferred_element_type=F32)


def shape(*dims, dtype=BF16):
    return jax.ShapeDtypeStruct(dims, dtype)


def cost(flops, mib):
    return pl.CostEstimate(flops=flops, bytes_accessed=int(mib * MIB), transcendentals=0)


def stack_heads(block):
    return jnp.concatenate([block[:, h * HEAD : (h + 1) * HEAD] for h in range(PER_GROUP)], axis=0)


def put_rows(out_ref, core, own, other):
    out_ref[pl.ds(pl.multiple_of(core * ROWS, ROWS), ROWS), :] = own[...]
    out_ref[pl.ds(pl.multiple_of((1 - core) * ROWS, ROWS), ROWS), :] = other[...]


def pick_keys_kernel(ids, own, other, both_ref):
    put_rows(both_ref, ids[2], own, other)


def pick_values_kernel(ids, own, other, keys, both_ref, last_ref):
    put_rows(both_ref, ids[2], own, other)
    last_ref[:, :HALF] = keys[ROWS:]
    last_ref[:, HALF:] = both_ref[ROWS:]


def pick_call(ids, own, other, keys=None):
    half = pl.BlockSpec((ROWS, HALF), lambda i, ids: (0, ids[2]))
    whole = pl.BlockSpec((ROWS, HALF), lambda i, ids: (0, 0))
    extra = [] if keys is None else [keys]
    return pl.pallas_call(
        pick_values_kernel if extra else pick_keys_kernel,
        grid_spec=pltpu.PrefetchScalarGridSpec(
            num_scalar_prefetch=1,
            grid=(1,),
            in_specs=[whole, half] + [WHOLE] * len(extra),
            out_specs=[WHOLE] * (1 + len(extra)),
        ),
        out_shape=[shape(2 * ROWS, HALF)] + [shape(ROWS, 2 * HALF)] * len(extra),
        compiler_params=PARAMS,
        cost_estimate=cost(0, 0.5),
        name="pick_values" if extra else "pick_keys",
    )(ids, own, other, *extra)


def prepare_kernel(
    ids, table, q_own, q_other, g_own, g_other, bias_ref, queries_ref, grads_ref
):
    put_rows(queries_ref, ids[2], q_own, q_other)
    put_rows(grads_ref, ids[2], g_own, g_other)
    base = ids[0] - ids[2]
    lane = lax.broadcasted_iota(jnp.int32, (1, ROWS), 1)
    row = lax.broadcasted_iota(jnp.int32, (STRETCH, ROWS), 0)
    for s in range(2):
        shard = base + s
        stretch = jnp.where(lane < STRETCH, table[2 * shard], table[2 * shard + 1])
        query_pos = shard * ROWS + stretch * STRETCH + (lane & (STRETCH - 1))
        begin = jnp.zeros((1, ROWS), jnp.int32)
        for i in range(NSTART):
            start = table[2 * N_SHARD + i]
            begin = jnp.where(start <= query_pos, start, begin)
        for d in range(SPAN):
            source = shard - (SPAN - 1) + d
            known = jnp.maximum(source, 0)
            for j in range(2):
                key_pos = source * ROWS + table[2 * known + j] * STRETCH + row
                allowed = (key_pos <= query_pos) & (key_pos >= begin)
                bias_ref[s, (2 * d + j) * STRETCH : (2 * d + j + 1) * STRETCH, :] = jnp.where(
                    allowed, 0.0, MASKED
                )


def prepare_call(ids, table, *blocks):
    width = GROUPS * WIDE
    own = pl.BlockSpec((ROWS, width), lambda i, *_: (0, 0))
    other = pl.BlockSpec((ROWS, width), lambda i, ids, *_: (0, ids[2]))
    return pl.pallas_call(
        prepare_kernel,
        grid_spec=pltpu.PrefetchScalarGridSpec(
            num_scalar_prefetch=2,
            grid=(1,),
            in_specs=[own, other] * 2,
            out_specs=[WHOLE] * 3,
        ),
        out_shape=[shape(2, KEYS, ROWS, dtype=F32)] + [shape(2 * ROWS, width)] * 2,
        compiler_params=PARAMS,
        cost_estimate=cost(0, 2.5),
        name="prepare",
    )(ids, table, *blocks)


def spread(out, far1, far2, s0, s1):
    out[:ROWS] = s0[3 * ROWS :] + s1[2 * ROWS : 3 * ROWS]
    out[ROWS:] = s1[3 * ROWS :]
    far1[:ROWS] = (s0[ROWS : 2 * ROWS] + s1[:ROWS]).astype(BF16)
    far1[ROWS:] = (s0[2 * ROWS : 3 * ROWS] + s1[ROWS : 2 * ROWS]).astype(BF16)
    far2[...] = s0[:ROWS].astype(far2.dtype)


def forward_kernel(bias, q_ref, g_ref, k2, k1, k0, prob_ref, own_ref, far1, far2):
    keys = jnp.concatenate([k2[...], k1[...], k0[...]], axis=0)
    terms = []
    for s in range(2):
        rows = slice(s * ROWS, (s + 1) * ROWS)
        window = keys[s * ROWS : s * ROWS + KEYS]
        for h in range(PER_GROUP):
            cols = slice(h * HEAD, (h + 1) * HEAD)
            score = nt(window, q_ref[rows, cols]) * (SCALE * LOG2E) + bias[s]
            weight = jnp.exp2(score - jnp.max(score, axis=0, keepdims=True))
            total = jnp.sum(weight, axis=0, keepdims=True)
            prob_ref[0, s, :, cols] = (weight * (1.0 / total)).astype(BF16)
        terms.append(nn(prob_ref[0, s], stack_heads(g_ref[rows, :])))
    spread(own_ref, far1, far2, *terms)


def backward_kernel(
    ids,
    prob_ref,
    q_ref,
    g_ref,
    k2,
    k1,
    k0,
    v2,
    v1,
    v0,
    keep_ref,
    send_ref,
    own_ref,
    far1,
    far2,
    gq_ref,
):
    core = ids[2]
    keys = jnp.concatenate([k2[...], k1[...], k0[...]], axis=0)
    values = jnp.concatenate([v2[...], v1[...], v0[...]], axis=0)
    terms = []
    for s in range(2):
        rows = slice(s * ROWS, (s + 1) * ROWS)
        window = slice(s * ROWS, s * ROWS + KEYS)
        prob = prob_ref[0, s].astype(F32)
        weighted = prob * nt(values[window], stack_heads(g_ref[rows, :]))
        delta = jnp.sum(weighted, axis=0, keepdims=True)
        grad_score = (weighted - prob * delta).astype(BF16)
        terms.append(nn(grad_score, stack_heads(q_ref[rows, :])) * SCALE)
        query_grad = tn(grad_score, keys[window]) * SCALE
        for h in range(PER_GROUP):
            gq_ref[s, :, h * HEAD : (h + 1) * HEAD] = query_grad[h * ROWS : (h + 1) * ROWS]
    spread(own_ref, far1, far2, *terms)
    keep_ref[...] = gq_ref[core].astype(BF16)
    send_ref[:ROWS] = gq_ref[1 - core]
    send_ref[ROWS:] = gq_ref[core, :EXTRA]


def narrow(rows, shift=0):
    return pl.BlockSpec((rows, HEAD), lambda j, *_: (0, j + shift))


def wide(rows):
    return pl.BlockSpec((rows, WIDE), lambda j, *_: (0, j))


WINDOW = [narrow(ROWS), narrow(2 * ROWS), narrow(2 * ROWS)]
VALUE_WINDOW = [narrow(ROWS, GROUPS)] + WINDOW[1:]
TERMS = [narrow(2 * ROWS), narrow(2 * ROWS), narrow(ROWS)]
PROB_SPEC = pl.BlockSpec((1, 2, KEYS, WIDE), lambda j, *_: (j, 0, 0, 0))


def term_shapes(last):
    return [shape(2 * ROWS, HALF, dtype=F32), shape(2 * ROWS, HALF), shape(ROWS, HALF, dtype=last)]


def forward_call(bias, queries, grads, keys):
    return pl.pallas_call(
        forward_kernel,
        grid=(GROUPS,),
        in_specs=[pl.BlockSpec((2, KEYS, ROWS), lambda j: (0, 0, 0))]
        + [wide(2 * ROWS)] * 2
        + WINDOW,
        out_specs=[PROB_SPEC] + TERMS,
        out_shape=[shape(GROUPS, 2, KEYS, WIDE)] + term_shapes(BF16),
        compiler_params=LARGE,
        cost_estimate=cost(4 * 16 * ROWS * KEYS * HEAD, 6),
        name="forward_and_value_gradient",
    )(bias, queries, grads, *keys)


def backward_call(ids, prob, queries, grads, keys, values):
    return pl.pallas_call(
        backward_kernel,
        grid_spec=pltpu.PrefetchScalarGridSpec(
            num_scalar_prefetch=1,
            grid=(GROUPS,),
            in_specs=[PROB_SPEC] + [wide(2 * ROWS)] * 2 + WINDOW + VALUE_WINDOW,
            out_specs=[wide(ROWS), wide(ROWS + EXTRA)] + TERMS,
            scratch_shapes=[pltpu.VMEM((2, ROWS, WIDE), F32)],
        ),
        out_shape=[
            shape(ROWS, GROUPS * WIDE),
            shape(ROWS + EXTRA, GROUPS * WIDE, dtype=F32),
        ]
        + term_shapes(BF16),
        compiler_params=LARGE,
        cost_estimate=cost(6 * 16 * ROWS * KEYS * HEAD, 6),
        name="query_and_key_gradient",
    )(ids, prob, queries, grads, *keys, *values)


def widen_kernel(in_ref, out_ref):
    out_ref[...] = in_ref[...].astype(F32)


def widen_call(block):
    return pl.pallas_call(
        widen_kernel,
        out_shape=shape(*block.shape, dtype=F32),
        compiler_params=PARAMS,
        cost_estimate=cost(0, 0.25),
        name="widen",
    )(block)


def pack_kernel(ids, in_ref, o0, o1, o2, o3):
    for d, out_ref in enumerate((o0, o1, o2, o3)):
        x = (ids[1] + d) & 3
        for z in range(8):
            column = pl.multiple_of((4 * z + x) * HEAD, HEAD)
            out_ref[:, z * HEAD : (z + 1) * HEAD] = in_ref[:, pl.ds(column, HEAD)]


def pack_call(ids, inputs):
    return pl.pallas_call(
        pack_kernel,
        grid_spec=pltpu.PrefetchScalarGridSpec(
            num_scalar_prefetch=1, grid=(1,), in_specs=[WHOLE], out_specs=[WHOLE] * 4
        ),
        out_shape=[shape(ROWS, 8 * HEAD)] * 4,
        compiler_params=PARAMS,
        cost_estimate=cost(0, 2),
        name="pack_inputs",
    )(ids, inputs)


def add_terms(own, r1, r2):
    first = own[:ROWS] + r1[:ROWS].astype(F32)
    second = own[ROWS:] + r1[ROWS:].astype(F32) + r2[...].astype(F32)
    return first.astype(BF16), second.astype(BF16)


def value_total_kernel(ids, own, r1, r2, keep_ref, send_ref, copies_ref):
    core = ids[2]
    first, second = add_terms(own, r1, r2)
    for x in range(4):
        copies_ref[x, :ROWS], copies_ref[x, ROWS:] = first, second
    keep_ref[...] = copies_ref[0, pl.ds(pl.multiple_of(core * ROWS, ROWS), ROWS), :]
    send_ref[...] = copies_ref[0, pl.ds(pl.multiple_of((1 - core) * ROWS, ROWS), ROWS), :]


def key_total_kernel(ids, own, r1, r2, keep_ref, send_ref, both_ref):
    core = ids[2]
    both_ref[:ROWS], both_ref[ROWS:] = add_terms(own, r1, r2)
    keep_ref[...] = both_ref[pl.ds(pl.multiple_of(core * ROWS, ROWS), ROWS), :]
    send_ref[...] = both_ref[pl.ds(pl.multiple_of((1 - core) * ROWS, ROWS), ROWS), :]


def total_call(ids, own, r1, r2, copies):
    return pl.pallas_call(
        value_total_kernel if copies else key_total_kernel,
        grid_spec=pltpu.PrefetchScalarGridSpec(
            num_scalar_prefetch=1,
            grid=(1,),
            in_specs=[WHOLE] * 3,
            out_specs=[WHOLE] * (3 if copies else 2),
            scratch_shapes=[] if copies else [pltpu.VMEM((2 * ROWS, HALF), BF16)],
        ),
        out_shape=[shape(ROWS, HALF)] * 2 + ([shape(4, 2 * ROWS, HALF)] if copies else []),
        compiler_params=PARAMS,
        cost_estimate=cost(0, 1),
        name="value_gradient_total" if copies else "key_gradient_total",
    )(ids, own, r1, r2)


def join_kernel(ids, query, query_other, key, key_other, value, value_other, gq, gk, gv):
    core = ids[2]
    parts = (
        (gq, query[...], query_other[:ROWS]),
        (gk, key[...], key_other[...]),
        (gv, value[...], value_other[...]),
    )
    for out, own, other in parts:
        width = own.shape[1]
        out[:, pl.ds(pl.multiple_of(core * width, HEAD), width)] = own.astype(BF16)
        out[:, pl.ds(pl.multiple_of((1 - core) * width, HEAD), width)] = other.astype(BF16)


def join_call(ids, *blocks):
    return pl.pallas_call(
        join_kernel,
        grid_spec=pltpu.PrefetchScalarGridSpec(
            num_scalar_prefetch=1, grid=(1,), in_specs=[WHOLE] * 6, out_specs=[WHOLE] * 3
        ),
        out_shape=[shape(ROWS, 2 * a.shape[1]) for a in blocks[::2]],
        compiler_params=PARAMS,
        cost_estimate=cost(0, 2),
        name="join_outputs",
    )(ids, *blocks)


def weight_kernel(ids, grads, a0, a1, a2, a3, b0, b1, b2, b3, out_ref):
    x, core = ids[1], ids[2]
    left = [ref[...] for ref in (a0, a1, a2, a3, b0, b1, b2, b3)]
    right = []
    for side in (core, 1 - core):
        rows = pl.ds(pl.multiple_of(side * ROWS, ROWS), ROWS)
        right += [grads[(x + 4 - d) & 3, rows, :] for d in range(4)]
    left, right = jnp.concatenate(left, axis=0), jnp.concatenate(right, axis=0)
    out_ref[...] = tn(left, right).astype(BF16)


def weight_call(ids, grads, own, other):
    taken = pl.BlockSpec((ROWS, 256), lambda i, _: (0, i))
    return pl.pallas_call(
        weight_kernel,
        grid_spec=pltpu.PrefetchScalarGridSpec(
            num_scalar_prefetch=1,
            grid=(4,),
            in_specs=[pl.BlockSpec((4, 2 * ROWS, HALF), lambda i, _: (0, 0, 0))] + [taken] * 8,
            out_specs=pl.BlockSpec((256, HALF), lambda i, _: (i, 0)),
        ),
        out_shape=shape(1024, HALF),
        compiler_params=LARGE,
        cost_estimate=cost(2 * 1024 * 1024 * 256, 3),
        name="weight_gradient",
    )(ids, grads, *own, *other)


def final_kernel(ids, in_ref, keep_ref, send_ref, total_ref):
    core = ids[2]
    total = in_ref[0].astype(F32)
    for i in range(1, 32):
        total += in_ref[i].astype(F32)
    total_ref[...] = total
    keep_ref[...] = total_ref[pl.ds(pl.multiple_of(core * 16, 16), 16), :]
    send_ref[...] = total_ref[pl.ds(pl.multiple_of((1 - core) * 16, 16), 16), :]


def final_call(ids, parts):
    return pl.pallas_call(
        final_kernel,
        grid_spec=pltpu.PrefetchScalarGridSpec(
            num_scalar_prefetch=1,
            grid=(1,),
            in_specs=[WHOLE],
            out_specs=[WHOLE] * 2,
            scratch_shapes=[pltpu.VMEM((32, HALF), F32)],
        ),
        out_shape=[shape(16, HALF, dtype=F32)] * 2,
        compiler_params=PARAMS,
        cost_estimate=cost(0, 0.5),
        name="weight_rows",
    )(ids, parts)


def shift_chips(block, distance):
    route = [(i - distance, i) for i in range(N_CHIP) if 0 <= i - distance < N_CHIP]
    return lax.ppermute(block, CHIP, route)


def shift_x(block, distance):
    return lax.ppermute(block, "x", [(i, (i + distance) % 4) for i in range(4)])


def swap_core(block):
    return lax.ppermute(block, "c", [(0, 1), (1, 0)])


def own_half(block, core):
    width = block.shape[1] // 2
    return lax.dynamic_slice(block, (0, core * width), (ROWS, width))


def shards(query, key, value, grad, inputs, stretch_order, session_starts):
    query, key, value, grad, inputs = query[0], key[0], value[0], grad[0], inputs[0]
    core = lax.axis_index("c")
    ids = jnp.stack([lax.axis_index(CTX), lax.axis_index("x"), core]).astype(jnp.int32)

    table = jnp.concatenate([stretch_order.reshape(-1), session_starts.reshape(-1)])
    key_other, value, table, value_half, key_half = lax.optimization_barrier(
        (swap_core(key), value, table, own_half(value, core), own_half(key, core))
    )
    (key0,) = pick_call(ids, key_half, key_other)
    key0, query, grad, value = lax.optimization_barrier((key0, query, grad, value))
    key1 = shift_chips(key0, 1)
    value0, last = pick_call(ids, value_half, swap_core(value), key0)
    far2 = shift_chips(last, 2)
    keys = [far2, key1, key0]
    bias, queries, grads = prepare_call(
        ids,
        table,
        own_half(query, core),
        swap_core(query),
        own_half(grad, core),
        swap_core(grad),
    )
    bias, value0 = lax.optimization_barrier((bias, value0))
    values = [far2, shift_chips(value0, 1), value0]

    prob, value_own, value_t1, value_t2 = forward_call(bias, queries, grads, keys)
    value_own, inputs = lax.optimization_barrier((value_own, inputs))
    packed = pack_call(ids, inputs)
    own = [packed[0]] + [shift_x(packed[d], d) for d in range(1, 4)]
    other = [swap_core(block) for block in own]
    value_r2 = shift_chips(value_t2, -2)
    value_r1 = shift_chips(value_t1, -1)
    query_keep, query_send, key_own, key_t1, key_t2 = backward_call(
        ids, prob, queries, grads, keys, values
    )
    value_r1, query_send = lax.optimization_barrier((value_r1, query_send))
    value_keep, value_send, sent = total_call(ids, value_own, value_r1, value_r2, True)
    key_r2 = widen_call(shift_chips(key_t2, -2))
    key_r1 = shift_chips(key_t1, -1)
    gathered = lax.all_to_all(sent, "x", 0, 0, tiled=True)
    partial = weight_call(ids, gathered, own, other)
    partial = lax.all_to_all(partial.reshape(32, 32, HALF), ("zl", "zh", "y"), 0, 0, tiled=True)

    key_keep, key_send = total_call(ids, key_own, key_r1, key_r2, False)
    key_keep, query_send = lax.optimization_barrier((key_keep, query_send))
    grad_query, grad_key, grad_value = join_call(
        ids,
        query_keep,
        swap_core(query_send),
        key_keep,
        swap_core(key_send),
        value_keep,
        swap_core(value_send),
    )
    partial, grad_query = lax.optimization_barrier((partial, grad_query))
    row_keep, row_send = final_call(ids, partial)
    swapped = swap_core(row_send)
    first, second = jnp.where(core == 0, row_keep, swapped), jnp.where(core == 0, swapped, row_keep)
    weight_grad = jnp.concatenate([first, second], axis=1)
    return grad_query[None], grad_key[None], grad_value[None], weight_grad


def solution(mesh):
    fine = Mesh(mesh.devices.reshape(4, 2, 4, 4, 2), AXES)
    rows = P("zl", CTX, None)
    return jax.shard_map(
        shards,
        mesh=fine,
        in_specs=(rows, rows, rows, rows, rows, P("zl", None, None), P("zl", None)),
        out_specs=(rows, rows, rows, P(AXES, None)),
        check_vma=False,
    )
```
